256 devices in a mesh: grp: 16 (over x, y), exp: 16 (over z, core).
Axes of the slice: x: 4, y: 4, z: 8, core: 2. Of those that a mesh axis runs over, the one named last changes fastest.
Arguments:
- tokens: bfloat16 [32768, 2048], P(('grp', 'exp')), may hold values from -6 to 6
- cotangent: bfloat16 [32768, 2048], P(('grp', 'exp')), may hold values from -3 to 3
- timestep: int32 [32768], P(('grp', 'exp')), may hold values from 0 to 15
- shift_table: float32 [16, 2048], replicated, may hold values from -3 to 3
- scale_table: float32 [16, 2048], replicated, may hold values from -2.5 to 2.5
- gate_table: float32 [16, 2048], replicated, may hold values from -4 to 4
- chosen: int32 [16, 8, 256], P('grp'), may hold values from 0 to 2047, as said below
- combine: float32 [16, 8, 256], P('grp'), may hold values from 0.1 to 1
- w_gate: bfloat16 [16, 704, 2048], P('exp'), may hold values from -0.125 to 0.125
- w_up: bfloat16 [16, 704, 2048], P('exp'), may hold values from -0.125 to 0.125
- w_down: bfloat16 [16, 704, 2048], P('exp'), may hold values from -0.15625 to 0.15625
Outputs:
- d_tokens: bfloat16 [32768, 2048], P(('grp', 'exp'))
- d_combine: float32 [16, 16, 128], P('grp', 'exp')
- d_w_gate: bfloat16 [16, 704, 2048], P('exp', None, 'grp')
- d_w_up: bfloat16 [16, 704, 2048], P('exp', None, 'grp')
- d_w_down: bfloat16 [16, 704, 2048], P('exp', None, 'grp')
The draws below stay inside these ranges and needn't reach their ends.
Inputs may be any that keep to these rules, and one draw needn't show every extreme that they name: Each list chosen[g, e, :] names 256 different tokens of group g; at most 32 of them lie among the 128 tokens of one device, and in every list some device's tokens supply exactly 32.
All inputs are finite; a program needn't handle non-finite values.
Results may differ from the reference program's by a relative error of at most 0.014.
Values may be sent and summed in bfloat16 or wider, within the bound.
A program may use at most 128 MiB of HBM per device.

```python
import math
import jax
import jax.numpy as jnp
from jax import lax

D = 2048
FF = 1408
TSTEPS = 16
TOK_DEV = 128
GROUPS = 16
PEERS = 16
EXPERTS = 8
FF_HALF = 704
CAP = 256
SLOT = 32
TOKENS = 32768


def pick_order(sub_key):
    return jax.random.permutation(sub_key, TOK_DEV)


def one_list(list_key):
    owner_key, shift_key, pick_key, mix_key = jax.random.split(list_key, 4)
    half_slot = SLOT // 2
    owner_order = jax.random.permutation(owner_key, PEERS)
    moved_rows = jax.random.randint(shift_key, (PEERS // 2,), 0, half_slot + 1)
    moved_rows = moved_rows.at[0].set(half_slot)
    paired = jnp.stack([half_slot + moved_rows, half_slot - moved_rows], axis=1).reshape(PEERS)
    counts = jnp.zeros((PEERS,), jnp.int32).at[owner_order].set(paired.astype(jnp.int32))
    pick_keys = jax.random.split(pick_key, PEERS)
    picked = jax.vmap(pick_order)(pick_keys)[:, :SLOT].astype(jnp.int32)
    token_ids = picked + jnp.arange(PEERS, dtype=jnp.int32)[:, None] * TOK_DEV
    is_valid = jnp.arange(SLOT, dtype=jnp.int32)[None, :] < counts[:, None]
    scores = jnp.where(is_valid, 0, 1).reshape(-1) * (PEERS * SLOT) + jnp.arange(PEERS * SLOT, dtype=jnp.int32)
    ordering = jnp.argsort(scores, stable=True)[:CAP]
    chosen_ids = token_ids.reshape(-1)[ordering]
    return chosen_ids[jax.random.permutation(mix_key, CAP)]


def draw_chosen(key, part):
    base_key = jax.random.fold_in(key, 17)
    list_keys = jax.random.split(base_key, GROUPS * EXPERTS)
    all_lists = jax.vmap(one_list)(list_keys)
    return all_lists.reshape(GROUPS, EXPERTS, CAP).astype(jnp.int32)


def plant(entries, own_key, smallest, high):
    longest = entries.shape.index(max(entries.shape))
    spots = []
    for shift in (0, 1):
        where = [jax.random.randint(jax.random.fold_in(own_key, axis), (), 0, length) for axis, length in enumerate(entries.shape)]
        where[longest] = (where[longest] + shift) % entries.shape[longest]
        spots.append(tuple(where))
    return entries.at[spots[0]].set(smallest).at[spots[1]].set(high)


def block_levels(rng, shape, pieces, least, largest):
    factor_of, own = 1.0, jax.random.fold_in(rng, 6)
    for axis_at, shards_of in pieces:
        heights = jnp.exp(jax.random.uniform(jax.random.fold_in(own, axis_at), (shards_of,), jnp.float32, least / len(pieces), largest / len(pieces)))
        factor_of = factor_of * jnp.repeat(heights, shape[axis_at] // shards_of).reshape([-1 if axis == axis_at else 1 for axis in range(len(shape))])
    return factor_of


def scatter_about(own_key, dims, spread, reach, cuts=(), kind=jnp.bfloat16):
    drawn = jax.random.normal(own_key, dims, jnp.float32) * spread
    if len(cuts) > 0:
        drawn = block_levels(own_key, dims, cuts, -0.22, 0.18) * drawn
    return jnp.clip(drawn, min=-reach, max=reach).astype(kind)


def setup_inputs(seed: int = 0) -> dict:
    seeds = jax.random.split(jax.random.key(seed), 12)
    tokens = scatter_about(seeds[0], (TOKENS, D), 1.0, 6.0, ((0, 256),))
    cotangent = scatter_about(seeds[1], (TOKENS, D), 0.5, 3.0, ((0, 256),))
    timestep = plant(jax.random.randint(seeds[2], (TOKENS,), 0, TSTEPS), jax.random.fold_in(seeds[2], 1), 0, TSTEPS - 1).astype(jnp.int32)
    shift_table = scatter_about(seeds[3], (TSTEPS, D), 0.5, 3.0, (), jnp.float32)
    scale_table = scatter_about(seeds[4], (TSTEPS, D), 0.3, 2.5, (), jnp.float32)
    gate_table = scatter_about(seeds[5], (TSTEPS, D), 1.0, 4.0, (), jnp.float32)
    chosen = draw_chosen(jax.random.fold_in(seeds[11], 71), 0)
    combine = jnp.clip(jnp.exp(math.log(1.0) - 2.3025851 * jax.random.uniform(seeds[7], (GROUPS, EXPERTS, CAP), jnp.float32) ** block_levels(seeds[7], (GROUPS, EXPERTS, CAP), ((0, 16),), -0.2, 0.2)), 0.1, 1.0)
    w_gate = scatter_about(seeds[8], (PEERS, FF_HALF, D), D ** -0.5, 0.125, ((0, 16),))
    w_up = scatter_about(seeds[9], (PEERS, FF_HALF, D), D ** -0.5, 0.125, ((0, 16),))
    w_down = scatter_about(seeds[10], (PEERS, FF_HALF, D), FF ** -0.5, 0.15625, ((0, 16),))
    return dict(tokens=tokens, cotangent=cotangent, timestep=timestep, shift_table=shift_table, scale_table=scale_table, gate_table=gate_table, chosen=chosen, combine=combine, w_gate=w_gate, w_up=w_up, w_down=w_down)


EPSILON = 1e-06

def layer_stats(group_x):
    values = group_x.astype(jnp.float32)
    centred = values - lax.optimization_barrier(jnp.mean(values, axis=1, keepdims=True))
    inverse = lax.rsqrt(lax.optimization_barrier(jnp.mean(centred * centred, axis=1, keepdims=True)) + EPSILON)
    return (centred * inverse, inverse)

def reference(tokens, cotangent, timestep, shift_table, scale_table, gate_table, chosen, combine, w_gate, w_up, w_down):
    groups = chosen.shape[0]
    experts = chosen.shape[1]
    capacity = chosen.shape[2]
    half_units = w_gate.shape[1]
    features = tokens.shape[1]
    group_tokens = tokens.shape[0] // groups
    gate_split = w_gate.reshape(experts, 2, half_units, features)
    up_split = w_up.reshape(experts, 2, half_units, features)
    down_split = w_down.reshape(experts, 2, half_units, features)

    def one_group(grad_sums, group_inputs):
        group_x, group_cot, group_steps, group_lists, group_weights = group_inputs
        normed, inverse = layer_stats(group_x)
        scale_rows = scale_table[group_steps]
        modulated = (normed * (1.0 + scale_rows) + shift_table[group_steps]).astype(jnp.bfloat16)
        scaled = (gate_table[group_steps] * group_cot.astype(jnp.float32)).astype(jnp.bfloat16)

        def one_expert(d_modulated, expert_inputs):
            rows, row_weight, gate_pair, up_pair, down_pair = expert_inputs
            rows_in = jnp.take(modulated, rows, axis=0)
            rows_grad = jnp.take(scaled, rows, axis=0)
            pre_gates = []
            pre_ups = []
            hiddens = []
            expert_out = jnp.zeros((capacity, features), jnp.float32)
            for half_index in range(2):
                pre_gate = jnp.dot(rows_in, gate_pair[half_index].T, preferred_element_type=jnp.float32)
                pre_up = jnp.dot(rows_in, up_pair[half_index].T, preferred_element_type=jnp.float32)
                hidden = (pre_gate * jax.nn.sigmoid(pre_gate) * pre_up).astype(jnp.bfloat16)
                expert_out = expert_out + jnp.dot(hidden, down_pair[half_index], preferred_element_type=jnp.float32)
                pre_gates.append(pre_gate)
                pre_ups.append(pre_up)
                hiddens.append(hidden)
            inner = lax.optimization_barrier(jnp.sum(rows_grad.astype(jnp.float32) * expert_out, axis=1))
            d_out = (row_weight[:, None] * rows_grad.astype(jnp.float32)).astype(jnp.bfloat16)
            grads_gate = []
            grads_up = []
            grads_down = []
            part_sum = jnp.zeros((capacity, features), jnp.float32)
            for half_index in range(2):
                pre_gate = pre_gates[half_index]
                sigmoid_gate = jax.nn.sigmoid(pre_gate)
                d_hidden = jnp.dot(d_out, down_pair[half_index].T, preferred_element_type=jnp.float32)
                grads_down.append(jnp.dot(hiddens[half_index].T, d_out, preferred_element_type=jnp.float32).astype(jnp.bfloat16))
                d_gate = (d_hidden * pre_ups[half_index] * sigmoid_gate * (1.0 + pre_gate * (1.0 - sigmoid_gate))).astype(jnp.bfloat16)
                d_up = (d_hidden * (pre_gate * sigmoid_gate)).astype(jnp.bfloat16)
                grads_gate.append(jnp.dot(d_gate.T, rows_in, preferred_element_type=jnp.float32).astype(jnp.bfloat16))
                grads_up.append(jnp.dot(d_up.T, rows_in, preferred_element_type=jnp.float32).astype(jnp.bfloat16))
                part_sum = part_sum + jnp.dot(d_gate, gate_pair[half_index], preferred_element_type=jnp.float32) + jnp.dot(d_up, up_pair[half_index], preferred_element_type=jnp.float32)
            part_rows = part_sum.astype(jnp.bfloat16)
            d_modulated = d_modulated.at[rows].add(part_rows.astype(jnp.float32))
            return (d_modulated, (inner, jnp.stack(grads_gate), jnp.stack(grads_up), jnp.stack(grads_down)))
        start = jnp.zeros((group_tokens, features), jnp.float32)
        d_modulated, (inners, grad_g, grad_u, grad_d) = lax.scan(one_expert, start, (group_lists, group_weights, gate_split, up_split, down_split))
        d_normed = d_modulated * (1.0 + scale_rows)
        d_x = inverse * (d_normed - lax.optimization_barrier(jnp.mean(d_normed, axis=1, keepdims=True)) - normed * lax.optimization_barrier(jnp.mean(d_normed * normed, axis=1, keepdims=True)))
        new_sums = (grad_sums[0] + grad_g.astype(jnp.float32), grad_sums[1] + grad_u.astype(jnp.float32), grad_sums[2] + grad_d.astype(jnp.float32))
        return (new_sums, (d_x.astype(jnp.bfloat16), inners))
    zero_grad = jnp.zeros((experts, 2, half_units, features), jnp.float32)
    grad_sums, (d_tokens, inners) = lax.scan(one_group, (zero_grad, zero_grad, zero_grad), (tokens.reshape(groups, group_tokens, features), cotangent.reshape(groups, group_tokens, features), timestep.reshape(groups, group_tokens), chosen, combine))
    d_tokens = d_tokens.reshape(groups * group_tokens, features)
    d_combine = inners.reshape(groups, experts * 2, capacity // 2)
    d_w_gate = (grad_sums[0] / groups).astype(jnp.bfloat16).reshape(experts * 2, half_units, features)
    d_w_up = (grad_sums[1] / groups).astype(jnp.bfloat16).reshape(experts * 2, half_units, features)
    d_w_down = (grad_sums[2] / groups).astype(jnp.bfloat16).reshape(experts * 2, half_units, features)
    return (d_tokens, d_combine, d_w_gate, d_w_up, d_w_down)
```

```python
import functools

import jax
import jax.numpy as jnp
from jax import lax
from jax.experimental import pallas as pl
from jax.experimental.pallas import tpu as pltpu
from jax.sharding import PartitionSpec as P

EPSILON = 1e-06
MESH = pl.DeviceIdType.MESH
F32 = jnp.float32
BF16 = jnp.bfloat16
SLOT = 32
SIDE = 4
NN = (((1,), (0,)), ((), ()))
NT = (((1,), (1,)), ((), ()))
TN = (((0,), (0,)), ((), ()))


def mm(a, b, dims):
    return lax.dot_general(a, b, dims, preferred_element_type=F32)


def iota(shape, axis):
    return lax.broadcasted_iota(jnp.int32, shape, axis)


def loop(count, body):
    def step(i, carry):
        body(i)
        return carry

    lax.fori_loop(0, count, step, 0)


def layer_kernel(
    nz,
    tok_ref,
    cot_ref,
    step_ref,
    shift_ref,
    scale_ref,
    gate_ref,
    chosen_ref,
    combine_ref,
    wg_hbm,
    wu_hbm,
    wd_hbm,
    dtok_ref,
    dcomb_ref,
    dwg_ref,
    dwu_ref,
    dwd_ref,
    wg,
    wu,
    wd,
    send_a,
    send_b,
    recv_a,
    recv_b,
    rows_in,
    rows_grad,
    normed,
    scale1,
    table,
    inverse,
    pick,
    pick_t,
    place,
    place_t,
    hidden,
    hidden_c,
    gate_f,
    up_f,
    d_gate,
    d_up,
    d_gate_t,
    d_up_t,
    back,
    sib,
    send_c,
    ret,
    inner_s,
    inner_r,
    grads,
    far1,
    near1,
    far2,
    near2,
    w_sem,
    a_send,
    a_recv,
    b_send,
    b_recv,
    fa_send,
    fb_send,
    c_send,
    c_recv,
    s_send,
    s_recv,
    r_send,
    r_recv,
):
    tok_dev, width = tok_ref.shape
    half = wg.shape[0]
    cap = rows_in.shape[0]
    rows_h = half // 2
    rows_q = half // 4
    g = lax.axis_index("grp")
    me = lax.axis_index("exp")
    z = lax.div(me, 2)
    core = lax.rem(me, 2)
    gx = lax.div(g, SIDE)
    gy = lax.rem(g, SIDE)
    sibling = z * 2 + (1 - core)

    def peer(j):
        return lax.rem(z + j, nz)

    def on_z(zz):
        return {"grp": g, "exp": zz * 2 + core}

    on_sib = {"grp": g, "exp": sibling}

    def on_axis(axis, by):
        if axis == 0:
            return {"grp": lax.rem(gx + by, SIDE) * SIDE + gy, "exp": me}
        return {"grp": gx * SIDE + lax.rem(gy + by, SIDE), "exp": me}

    hops = [4, 3, 5, 2, 6, 1, 7] if nz == 8 else list(range(1, nz))

    loads = [
        pltpu.make_async_copy(src, dst, w_sem.at[i])
        for i, (src, dst) in enumerate(((wg_hbm, wg), (wu_hbm, wu), (wd_hbm, wd)))
    ]
    for load in loads:
        load.start()
    barrier = pltpu.get_barrier_semaphore()
    partners = [on_z(peer(j)) for j in hops] + [on_sib]
    partners += [on_axis(axis, by) for axis in (0, 1) for by in (1, SIDE - 1)]
    for partner in partners:
        pl.semaphore_signal(barrier, inc=1, device_id=partner, device_id_type=MESH)

    first = me * tok_dev
    ids = iota((tok_dev, cap), 0) + first
    lane_e = iota((tok_dev, nz), 1)
    mask = jnp.zeros((tok_dev, nz), F32)
    for e in range(nz):
        hit = jnp.sum(
            jnp.where(ids == chosen_ref[e : e + 1, :], 1.0, 0.0), axis=1, keepdims=True
        )
        mask = jnp.where(lane_e == e, hit, mask)
    earlier = (iota((tok_dev, tok_dev), 1) < iota((tok_dev, tok_dev), 0)).astype(F32)
    rank = mm(earlier.astype(BF16), mask.astype(BF16), NN)
    slots = nz * SLOT
    spread = (lax.div(iota((nz, slots), 1), SLOT) == iota((nz, slots), 0)).astype(F32).astype(BF16)
    rank_p = mm(rank.astype(BF16), spread, NN)
    mask_p = mm(mask.astype(BF16), spread, NN)
    want = lax.rem(iota((tok_dev, slots), 1), SLOT).astype(F32)
    pick_f = jnp.where((rank_p == want) & (mask_p > 0.5), 1.0, 0.0)
    pick_t[...] = pick_f.astype(BF16)
    pick[...] = pick_f.T.astype(BF16)

    steps3 = 3 * scale_ref.shape[0]
    onehot = (lax.rem(iota((steps3, tok_dev), 0), scale_ref.shape[0]) == step_ref[...]).astype(F32)
    onehot = onehot.T.astype(BF16)

    def table_rows(ref):
        whole = ref[...]
        hi = whole.astype(BF16)
        rest = whole - hi.astype(F32)
        mid = rest.astype(BF16)
        low = (rest - mid.astype(F32)).astype(BF16)
        return mm(onehot, jnp.concatenate([hi, mid, low], axis=0), NN)

    scale1[...] = 1.0 + table_rows(scale_ref)
    table[...] = table_rows(shift_ref)

    def normalise(i):
        at = pl.ds(pl.multiple_of(i * 16, 16), 16)
        values = tok_ref[at, :].astype(F32)
        centred = values - jnp.mean(values, axis=1, keepdims=True)
        inv = lax.rsqrt(jnp.mean(centred * centred, axis=1, keepdims=True) + EPSILON)
        inverse[at, :] = inv
        norm = centred * inv
        normed[at, :] = norm
        table[at, :] = norm * scale1[at, :] + table[at, :]

    loop(tok_dev // 16, normalise)

    def fill(dst, i):
        at = pl.ds(pl.multiple_of(i * 512, 512), 512)
        dst[:, at] = mm(pick[...], table[:, at].astype(BF16), NN).astype(BF16)

    def slot_of(zz, cc):
        return pl.ds(pl.multiple_of((cc * nz + zz) * SLOT, SLOT), SLOT)

    def block_of(zz):
        return pl.ds(pl.multiple_of(zz * SLOT, SLOT), SLOT)

    def to_peer(src, dst, s_sem, r_sem, j):
        zz = peer(j)
        return pltpu.make_async_remote_copy(
            src_ref=src.at[block_of(zz)],
            dst_ref=dst.at[slot_of(z, core)],
            send_sem=s_sem.at[j],
            recv_sem=r_sem.at[j],
            device_id=on_z(zz),
            device_id_type=MESH,
        )

    def from_peer(dst, s_sem, r_sem, j):
        zz = peer(nz - j)
        return pltpu.make_async_remote_copy(
            src_ref=dst.at[slot_of(zz, core)],
            dst_ref=dst.at[slot_of(zz, core)],
            send_sem=s_sem.at[j],
            recv_sem=r_sem.at[j],
            device_id=on_z(peer(j)),
            device_id_type=MESH,
        )

    def to_sibling(dst, s_sem, r_sem, j):
        zz = peer(nz - j)
        return pltpu.make_async_remote_copy(
            src_ref=dst.at[slot_of(zz, core)],
            dst_ref=dst.at[slot_of(zz, core)],
            send_sem=s_sem.at[j],
            recv_sem=r_sem.at[nz + j],
            device_id=on_sib,
            device_id_type=MESH,
        )

    def from_sibling(dst, s_sem, r_sem, j):
        zz = peer(nz - j)
        return pltpu.make_async_remote_copy(
            src_ref=dst.at[slot_of(zz, 1 - core)],
            dst_ref=dst.at[slot_of(zz, 1 - core)],
            send_sem=s_sem.at[j],
            recv_sem=r_sem.at[nz + j],
            device_id=on_sib,
            device_id_type=MESH,
        )

    loop(width // 512, functools.partial(fill, send_a))
    pl.semaphore_wait(barrier, len(partners))
    for j in hops:
        to_peer(send_a, recv_a, a_send, a_recv, j).start()
    recv_a[slot_of(z, core), :] = send_a[block_of(z), :]
    to_sibling(recv_a, fa_send, a_recv, 0).start()

    table[...] = table_rows(gate_ref)

    def weigh(i):
        at = pl.ds(pl.multiple_of(i * 16, 16), 16)
        table[at, :] = table[at, :] * cot_ref[at, :].astype(F32)

    loop(tok_dev // 16, weigh)
    loop(width // 512, functools.partial(fill, send_b))
    recv_b[slot_of(z, core), :] = send_b[block_of(z), :]
    to_sibling(recv_b, fb_send, b_recv, 0).start()

    row = chosen_ref[pl.ds(z, 1), :]
    diagonal = iota((cap, cap), 0) == iota((cap, cap), 1)
    column = jnp.sum(jnp.where(diagonal, row.astype(F32), 0.0), axis=1, keepdims=True)
    row_f = row.astype(F32)
    owner_row = jnp.floor(row_f * (1.0 / tok_dev))
    owner_col = jnp.floor(column * (1.0 / tok_dev))
    ahead = jnp.where((owner_row == owner_col) & (row_f < column), 1.0, 0.0)
    place_in = jnp.sum(ahead, axis=1, keepdims=True)
    owner_z = jnp.floor(owner_col * 0.5)
    owner_c = owner_col - 2.0 * owner_z
    at_slot = (owner_c * nz + owner_z) * SLOT + place_in
    place_f = jnp.where(
        iota((cap, 2 * slots), 1).astype(F32) == at_slot, 1.0, 0.0
    )
    place[...] = place_f.astype(BF16)
    place_t[...] = place_f.T.astype(BF16)

    for j in hops:
        from_peer(recv_a, a_send, a_recv, j).wait_recv()
        to_sibling(recv_a, fa_send, a_recv, j).start()
        to_peer(send_a, recv_a, a_send, a_recv, j).wait_send()
        to_peer(send_b, recv_b, b_send, b_recv, j).start()
    for j in [0] + hops:
        from_sibling(recv_a, fa_send, a_recv, j).wait_recv()

    def gather(src, dst, i):
        at = pl.ds(pl.multiple_of(i * 512, 512), 512)
        dst[:, at] = mm(place[...], src[:, at], NN).astype(BF16)

    loop(width // 512, functools.partial(gather, recv_a, rows_in))
    for load in loads:
        load.wait()
    weight = combine_ref[pl.ds(z, 1), :]

    def forward(i):
        at = pl.ds(pl.multiple_of(i * rows_q, rows_q), rows_q)
        pre_gate = mm(wg[at, :], rows_in[...], NT)
        pre_up = mm(wu[at, :], rows_in[...], NT)
        sig = 1.0 / (1.0 + jnp.exp(-pre_gate))
        silu = pre_gate * sig
        hid = silu * pre_up
        hidden[at, :] = hid.astype(BF16)
        hidden_c[at, :] = (hid * weight).astype(BF16)
        up_f[at, :] = silu * weight
        gate_f[at, :] = pre_up * sig * (1.0 + pre_gate * (1.0 - sig)) * weight

    loop(4, forward)

    for j in hops:
        from_peer(recv_b, b_send, b_recv, j).wait_recv()
        to_sibling(recv_b, fb_send, b_recv, j).start()
    for j in [0] + hops:
        from_sibling(recv_b, fb_send, b_recv, j).wait_recv()
    loop(width // 512, functools.partial(gather, recv_b, rows_grad))

    def weight_grad(t, left, right):
        def columns(i):
            at = pl.ds(pl.multiple_of(i * 512, 512), 512)
            product = mm(left[...], right[:, at], NN).astype(BF16)
            for k in range(SIDE):
                piece = product[:, k * 128 : (k + 1) * 128]
                grads[2 * t, i * SIDE + k] = piece[:rows_h]
                grads[2 * t + 1, k * SIDE + i] = piece[rows_h:]

        loop(SIDE, columns)

    def ring(t, h):
        n = 2 * t + h
        ia, ib = (gx, gy) if h == 0 else (gy, gx)
        own, other = h, 1 - h

        def copy(src, dst, k, axis, by):
            return pltpu.make_async_remote_copy(
                src_ref=src,
                dst_ref=dst,
                send_sem=r_send.at[n * 12 + k],
                recv_sem=r_recv.at[n * 12 + k],
                device_id=on_axis(axis, by),
                device_id_type=MESH,
            )

        def pair(dest, q):
            return pl.ds(lax.rem(ia + dest, SIDE) * SIDE + 2 * q, 2)

        def sub(dest):
            return ia * SIDE + lax.rem(ib + dest, SIDE)

        one, two = (1, SIDE - 1), SIDE // 2
        first_copies = [
            copy(grads.at[n, pair(two, 0)], far1.at[n, 0], 0, own, one[0]),
            copy(grads.at[n, pair(two, 1)], far1.at[n, 1], 1, own, one[1]),
            copy(grads.at[n, pair(1, 1)], near1.at[n, 0, pl.ds(2, 2)], 2, own, one[0]),
            copy(grads.at[n, pair(3, 0)], near1.at[n, 1, pl.ds(0, 2)], 3, own, one[1]),
            copy(grads.at[n, pair(1, 0)], near1.at[n, 0, pl.ds(0, 2)], 4, own, one[0]),
            copy(grads.at[n, pair(3, 1)], near1.at[n, 1, pl.ds(2, 2)], 5, own, one[1]),
        ]
        top, low = pl.ds(0, rows_q), pl.ds(rows_q, rows_q)
        next_copies = [
            copy(grads.at[n, sub(two), top], far2.at[n, 0], 6, other, one[0]),
            copy(grads.at[n, sub(two), low], far2.at[n, 1], 7, other, one[1]),
            copy(grads.at[n, sub(1), low], near2.at[n, 0, low], 8, other, one[0]),
            copy(grads.at[n, sub(3), top], near2.at[n, 1, top], 9, other, one[1]),
            copy(grads.at[n, sub(1), top], near2.at[n, 0, top], 10, other, one[0]),
            copy(grads.at[n, sub(3), low], near2.at[n, 1, low], 11, other, one[1]),
        ]

        def start1():
            for c in first_copies[:4]:
                c.start()

        def merge1():
            for side, dest in ((0, 1), (1, 3)):
                first_copies[side].wait_recv()
                base = lax.rem(ia + dest, SIDE) * SIDE + 2 * side

                def add(i):
                    grads[n, base + i] = (
                        grads[n, base + i].astype(F32) + far1[n, side, i].astype(F32)
                    ).astype(BF16)

                loop(2, add)
                first_copies[4 + side].start()

        def finish1():
            for c in first_copies[2:]:
                c.wait_recv()
            base = ia * SIDE

            def add(i):
                grads[n, base + i] = (
                    grads[n, base + i].astype(F32)
                    + near1[n, 0, i].astype(F32)
                    + near1[n, 1, i].astype(F32)
                ).astype(BF16)

            loop(SIDE, add)
            for c in next_copies[:4]:
                c.start()

        def merge2():
            for side, dest, part in ((0, 1, top), (1, 3, low)):
                next_copies[side].wait_recv()
                grads[n, sub(dest), part] = (
                    grads[n, sub(dest), part].astype(F32) + far2[n, side].astype(F32)
                ).astype(BF16)
                next_copies[4 + side].start()

        def finish2(out):
            for c in next_copies[2:]:
                c.wait_recv()
            total = (
                grads[n, sub(0)].astype(F32)
                + near2[n, 0].astype(F32)
                + near2[n, 1].astype(F32)
            )
            out[h * rows_h : (h + 1) * rows_h, :] = (total * (1.0 / (SIDE * SIDE))).astype(BF16)

        def drain():
            for c in first_copies + next_copies:
                c.wait_send()

        return start1, merge1, finish1, merge2, finish2, drain

    rings = {(t, h): ring(t, h) for t in range(3) for h in range(2)}

    def run(t, phase, *args):
        for h in range(2):
            rings[t, h][phase](*args)

    weight_grad(0, hidden_c, rows_grad)
    run(0, 0)

    def backward(i):
        at = pl.ds(pl.multiple_of(i * rows_q, rows_q), rows_q)
        raw = mm(wd[at, :], rows_grad[...], NT)
        inner = jnp.sum(hidden[at, :].astype(F32) * raw, axis=0, keepdims=True)
        d_gate[at, :] = (raw * gate_f[at, :]).astype(BF16)
        d_up[at, :] = (raw * up_f[at, :]).astype(BF16)
        return inner

    inner = backward(0)
    for i in range(1, 4):
        inner = inner + backward(i)
    left, right = inner[:, : cap // 2], inner[:, cap // 2 :]
    mine = jnp.where(core == 0, left, right)
    theirs = jnp.where(core == 0, right, left)
    inner_s[...] = jnp.broadcast_to(theirs, inner_s.shape)
    inner_copy = pltpu.make_async_remote_copy(
        src_ref=inner_s,
        dst_ref=inner_r,
        send_sem=s_send.at[0],
        recv_sem=s_recv.at[0],
        device_id=on_sib,
        device_id_type=MESH,
    )
    inner_copy.start()
    d_gate_t[...] = d_gate[...].astype(F32).T.astype(BF16)
    d_up_t[...] = d_up[...].astype(F32).T.astype(BF16)

    def input_grad(i):
        at = pl.ds(pl.multiple_of(i * 512, 512), 512)
        total = mm(d_gate_t[...], wg[:, at], NN) + mm(d_up_t[...], wu[:, at], NN)
        back[:, at] = mm(place_t[...], total.astype(BF16), NN).astype(BF16)

    loop(width // 512, input_grad)
    their_rows = pl.ds(pl.multiple_of((1 - core) * slots, slots), slots)
    sib_copy = pltpu.make_async_remote_copy(
        src_ref=back.at[their_rows],
        dst_ref=sib,
        send_sem=s_send.at[1],
        recv_sem=s_recv.at[1],
        device_id=on_sib,
        device_id_type=MESH,
    )
    sib_copy.start()
    weight_grad(1, d_gate, rows_in)
    run(1, 0)
    run(0, 1)
    sib_copy.wait_recv()

    def add_halves(i):
        at = pl.ds(pl.multiple_of(i * SLOT, SLOT), SLOT)
        here = slot_of(i, core)
        send_c[at, :] = (back[here, :].astype(F32) + sib[at, :].astype(F32)).astype(BF16)

    loop(nz, add_halves)

    def to_owner(j):
        zz = peer(j)
        return pltpu.make_async_remote_copy(
            src_ref=send_c.at[block_of(zz)],
            dst_ref=ret.at[block_of(z)],
            send_sem=c_send.at[j],
            recv_sem=c_recv.at[j],
            device_id=on_z(zz),
            device_id_type=MESH,
        )

    def from_expert(j):
        zz = peer(nz - j)
        return pltpu.make_async_remote_copy(
            src_ref=ret.at[block_of(zz)],
            dst_ref=ret.at[block_of(zz)],
            send_sem=c_send.at[j],
            recv_sem=c_recv.at[j],
            device_id=on_z(peer(j)),
            device_id_type=MESH,
        )

    for j in hops:
        to_owner(j).start()
    ret[block_of(z), :] = send_c[block_of(z), :]
    weight_grad(2, d_up, rows_in)
    run(2, 0)
    inner_copy.wait_recv()
    dcomb_ref[...] = mine + inner_r[0:1, :]
    run(1, 1)
    run(0, 2)
    run(2, 1)
    run(0, 3)
    run(1, 2)
    run(0, 4, dwd_ref)
    run(1, 3)

    for j in hops:
        from_expert(j).wait_recv()

    def spread_back(i):
        at = pl.ds(pl.multiple_of(i * 512, 512), 512)
        table[:, at] = mm(pick_t[...], ret[:, at], NN)

    loop(width // 512, spread_back)

    def token_grad(i):
        at = pl.ds(pl.multiple_of(i * 16, 16), 16)
        norm = normed[at, :]
        d_norm = table[at, :] * scale1[at, :]
        centre = jnp.mean(d_norm, axis=1, keepdims=True)
        along = jnp.mean(d_norm * norm, axis=1, keepdims=True)
        dtok_ref[at, :] = (inverse[at, :] * (d_norm - centre - norm * along)).astype(BF16)

    loop(tok_dev // 16, token_grad)
    run(2, 2)
    run(1, 4, dwg_ref)
    run(2, 3)
    run(2, 4, dwu_ref)

    for j in hops:
        to_peer(send_b, recv_b, b_send, b_recv, j).wait_send()
        to_owner(j).wait_send()
    for j in [0] + hops:
        to_sibling(recv_a, fa_send, a_recv, j).wait_send()
        to_sibling(recv_b, fb_send, b_recv, j).wait_send()
    inner_copy.wait_send()
    sib_copy.wait_send()
    for t in range(3):
        run(t, 5)


def solution(mesh):
    nz = mesh.shape["exp"] // 2

    def on_device(
        tokens, cotangent, timestep, shift_table, scale_table, gate_table, chosen, combine, w_gate, w_up, w_down
    ):
        tok_dev, width = tokens.shape
        half = w_gate.shape[1]
        cap = chosen.shape[2]
        slots = nz * SLOT
        rows_h, rows_q = half // 2, half // 4
        vmem = pl.BlockSpec(memory_space=pltpu.VMEM)
        hbm = pl.BlockSpec(memory_space=pl.ANY)
        dma = pltpu.SemaphoreType.DMA
        outs = pl.pallas_call(
            functools.partial(layer_kernel, nz),
            out_shape=(
                jax.ShapeDtypeStruct((tok_dev, width), BF16),
                jax.ShapeDtypeStruct((1, cap // 2), F32),
                jax.ShapeDtypeStruct((half, 128), BF16),
                jax.ShapeDtypeStruct((half, 128), BF16),
                jax.ShapeDtypeStruct((half, 128), BF16),
            ),
            in_specs=[vmem] * 8 + [hbm] * 3,
            out_specs=(vmem,) * 5,
            scratch_shapes=[
                pltpu.VMEM((half, width), BF16),
                pltpu.VMEM((half, width), BF16),
                pltpu.VMEM((half, width), BF16),
                pltpu.VMEM((slots, width), BF16),
                pltpu.VMEM((slots, width), BF16),
                pltpu.VMEM((2 * slots, width), BF16),
                pltpu.VMEM((2 * slots, width), BF16),
                pltpu.VMEM((cap, width), BF16),
                pltpu.VMEM((cap, width), BF16),
                pltpu.VMEM((tok_dev, width), F32),
                pltpu.VMEM((tok_dev, width), F32),
                pltpu.VMEM((tok_dev, width), F32),
                pltpu.VMEM((tok_dev, 1), F32),
                pltpu.VMEM((slots, tok_dev), BF16),
                pltpu.VMEM((tok_dev, slots), BF16),
                pltpu.VMEM((cap, 2 * slots), BF16),
                pltpu.VMEM((2 * slots, cap), BF16),
                pltpu.VMEM((half, cap), BF16),
                pltpu.VMEM((half, cap), BF16),
                pltpu.VMEM((half, cap), F32),
                pltpu.VMEM((half, cap), F32),
                pltpu.VMEM((half, cap), BF16),
                pltpu.VMEM((half, cap), BF16),
                pltpu.VMEM((cap, half), BF16),
                pltpu.VMEM((cap, half), BF16),

                pltpu.VMEM((2 * slots, width), BF16),
                pltpu.VMEM((slots, width), BF16),
                pltpu.VMEM((slots, width), BF16),
                pltpu.VMEM((slots, width), BF16),
                pltpu.VMEM((8, cap // 2), F32),
                pltpu.VMEM((8, cap // 2), F32),
                pltpu.VMEM((6, SIDE * SIDE, rows_h, 128), BF16),
                pltpu.VMEM((6, 2, 2, rows_h, 128), BF16),
                pltpu.VMEM((6, 2, SIDE, rows_h, 128), BF16),
                pltpu.VMEM((6, 2, rows_q, 128), BF16),
                pltpu.VMEM((6, 2, rows_h, 128), BF16),
                dma((3,)),
                dma((nz,)),
                dma((2 * nz,)),
                dma((nz,)),
                dma((2 * nz,)),
                dma((nz,)),
                dma((nz,)),
                dma((nz,)),
                dma((nz,)),
                dma((2,)),
                dma((2,)),
                dma((72,)),
                dma((72,)),
            ],
            compiler_params=pltpu.CompilerParams(
                collective_id=0, has_side_effects=True, vmem_limit_bytes=60 * 1024 * 1024
            ),
        )(
            tokens,
            cotangent,
            timestep[None, :],
            shift_table,
            scale_table,
            gate_table,
            chosen[0],
            combine[0],
            w_gate[0],
            w_up[0],
            w_down[0],
        )
        d_tokens, d_combine, d_gate, d_up, d_down = outs
        return d_tokens, d_combine[None], d_gate[None], d_up[None], d_down[None]

    in_specs = (
        P(("grp", "exp"), None),
        P(("grp", "exp"), None),
        P(("grp", "exp")),
        P(),
        P(),
        P(),
        P("grp", None, None),
        P("grp", None, None),
        P("exp", None, None),
        P("exp", None, None),
        P("exp", None, None),
    )
    out_specs = (
        P(("grp", "exp"), None),
        P("grp", "exp", None),
        P("exp", None, "grp"),
        P("exp", None, "grp"),
        P("exp", None, "grp"),
    )
    return jax.shard_map(
        on_device, mesh=mesh, in_specs=in_specs, out_specs=out_specs, check_vma=False
    )
```

```python
import functools

import jax
import jax.numpy as jnp
from jax import lax
from jax.experimental import pallas as pl
from jax.experimental.pallas import tpu as pltpu
from jax.sharding import PartitionSpec as P

EPSILON = 1e-06
MESH = pl.DeviceIdType.MESH
F32 = jnp.float32
BF16 = jnp.bfloat16
SLOT = 32
SIDE = 4
NN = (((1,), (0,)), ((), ()))
NT = (((1,), (1,)), ((), ()))
TN = (((0,), (0,)), ((), ()))


def mm(a, b, dims):
    return lax.dot_general(a, b, dims, preferred_element_type=F32)


def iota(shape, axis):
    return lax.broadcasted_iota(jnp.int32, shape, axis)


def loop(count, body):
    def step(i, carry):
        body(i)
        return carry

    lax.fori_loop(0, count, step, 0)


def layer_kernel(
    nz,
    tok_ref,
    cot_ref,
    step_ref,
    shift_ref,
    scale_ref,
    gate_ref,
    chosen_ref,
    combine_ref,
    wg_hbm,
    wu_hbm,
    wd_hbm,
    dtok_ref,
    dcomb_ref,
    dwg_ref,
    dwu_ref,
    dwd_ref,
    wg,
    wu,
    wd,
    send_a,
    send_b,
    recv_a,
    recv_b,
    rows_in,
    rows_grad,
    normed,
    scale1,
    table,
    inverse,
    pick,
    pick_t,
    place,
    place_t,
    hidden,
    hidden_c,
    gate_f,
    up_f,
    d_gate,
    d_up,
    d_gate_t,
    d_up_t,
    back,
    sib,
    send_c,
    ret,
    inner_s,
    inner_r,
    columns_in,
    line_rows,
    line_gate,
    grads,
    parts,
    far1,
    near1,
    far2,
    near2,
    w_sem,
    a_send,
    a_recv,
    b_send,
    b_recv,
    fa_send,
    fb_send,
    c_send,
    c_recv,
    s_send,
    s_recv,
    r_send,
    r_recv,
    l_send,
    l_recv,
):
    tok_dev, width = tok_ref.shape
    half = wg.shape[0]
    cap = rows_in.shape[0]
    rows_h = half // 2
    rows_q = half // 4
    g = lax.axis_index("grp")
    me = lax.axis_index("exp")
    z = lax.div(me, 2)
    core = lax.rem(me, 2)
    gx = lax.div(g, SIDE)
    gy = lax.rem(g, SIDE)
    sibling = z * 2 + (1 - core)

    def peer(j):
        return lax.rem(z + j, nz)

    def on_z(zz):
        return {"grp": g, "exp": zz * 2 + core}

    on_sib = {"grp": g, "exp": sibling}

    def on_axis(axis, by):
        if axis == 0:
            return {"grp": lax.rem(gx + by, SIDE) * SIDE + gy, "exp": me}
        return {"grp": gx * SIDE + lax.rem(gy + by, SIDE), "exp": me}

    hops = [4, 3, 5, 2, 6, 1, 7] if nz == 8 else list(range(1, nz))

    loads = [
        pltpu.make_async_copy(src, dst, w_sem.at[i])
        for i, (src, dst) in enumerate(((wg_hbm, wg), (wu_hbm, wu), (wd_hbm, wd)))
    ]
    for load in loads:
        load.start()
    barrier = pltpu.get_barrier_semaphore()
    partners = [on_z(peer(j)) for j in hops] + [on_sib]
    partners += [on_axis(axis, by) for axis in (0, 1) for by in (1, 2, 3)]
    for partner in partners:
        pl.semaphore_signal(barrier, inc=1, device_id=partner, device_id_type=MESH)

    first = me * tok_dev
    ids = iota((tok_dev, cap), 0) + first
    lane_e = iota((tok_dev, nz), 1)
    mask = jnp.zeros((tok_dev, nz), F32)
    for e in range(nz):
        hit = jnp.sum(
            jnp.where(ids == chosen_ref[e : e + 1, :], 1.0, 0.0), axis=1, keepdims=True
        )
        mask = jnp.where(lane_e == e, hit, mask)
    earlier = (iota((tok_dev, tok_dev), 1) < iota((tok_dev, tok_dev), 0)).astype(F32)
    rank = mm(earlier.astype(BF16), mask.astype(BF16), NN)
    slots = nz * SLOT
    spread = (lax.div(iota((nz, slots), 1), SLOT) == iota((nz, slots), 0)).astype(F32).astype(BF16)
    rank_p = mm(rank.astype(BF16), spread, NN)
    mask_p = mm(mask.astype(BF16), spread, NN)
    want = lax.rem(iota((tok_dev, slots), 1), SLOT).astype(F32)
    pick_f = jnp.where((rank_p == want) & (mask_p > 0.5), 1.0, 0.0)
    pick_t[...] = pick_f.astype(BF16)
    pick[...] = pick_f.T.astype(BF16)

    steps3 = 3 * scale_ref.shape[0]
    onehot = (lax.rem(iota((steps3, tok_dev), 0), scale_ref.shape[0]) == step_ref[...]).astype(F32)
    onehot = onehot.T.astype(BF16)

    def table_rows(ref):
        whole = ref[...]
        hi = whole.astype(BF16)
        rest = whole - hi.astype(F32)
        mid = rest.astype(BF16)
        low = (rest - mid.astype(F32)).astype(BF16)
        return mm(onehot, jnp.concatenate([hi, mid, low], axis=0), NN)

    scale1[...] = 1.0 + table_rows(scale_ref)
    table[...] = table_rows(shift_ref)

    def normalise(i):
        at = pl.ds(pl.multiple_of(i * 16, 16), 16)
        values = tok_ref[at, :].astype(F32)
        centred = values - jnp.mean(values, axis=1, keepdims=True)
        inv = lax.rsqrt(jnp.mean(centred * centred, axis=1, keepdims=True) + EPSILON)
        inverse[at, :] = inv
        norm = centred * inv
        normed[at, :] = norm
        table[at, :] = norm * scale1[at, :] + table[at, :]

    loop(tok_dev // 16, normalise)

    def fill(dst, i):
        at = pl.ds(pl.multiple_of(i * 512, 512), 512)
        dst[:, at] = mm(pick[...], table[:, at].astype(BF16), NN).astype(BF16)

    def slot_of(zz, cc):
        return pl.ds(pl.multiple_of((cc * nz + zz) * SLOT, SLOT), SLOT)

    def block_of(zz):
        return pl.ds(pl.multiple_of(zz * SLOT, SLOT), SLOT)

    def to_peer(src, dst, s_sem, r_sem, j):
        zz = peer(j)
        return pltpu.make_async_remote_copy(
            src_ref=src.at[block_of(zz)],
            dst_ref=dst.at[slot_of(z, core)],
            send_sem=s_sem.at[j],
            recv_sem=r_sem.at[j],
            device_id=on_z(zz),
            device_id_type=MESH,
        )

    def from_peer(dst, s_sem, r_sem, j):
        zz = peer(nz - j)
        return pltpu.make_async_remote_copy(
            src_ref=dst.at[slot_of(zz, core)],
            dst_ref=dst.at[slot_of(zz, core)],
            send_sem=s_sem.at[j],
            recv_sem=r_sem.at[j],
            device_id=on_z(peer(j)),
            device_id_type=MESH,
        )

    def to_sibling(dst, s_sem, r_sem, j):
        zz = peer(nz - j)
        return pltpu.make_async_remote_copy(
            src_ref=dst.at[slot_of(zz, core)],
            dst_ref=dst.at[slot_of(zz, core)],
            send_sem=s_sem.at[j],
            recv_sem=r_sem.at[nz + j],
            device_id=on_sib,
            device_id_type=MESH,
        )

    def from_sibling(dst, s_sem, r_sem, j):
        zz = peer(nz - j)
        return pltpu.make_async_remote_copy(
            src_ref=dst.at[slot_of(zz, 1 - core)],
            dst_ref=dst.at[slot_of(zz, 1 - core)],
            send_sem=s_sem.at[j],
            recv_sem=r_sem.at[nz + j],
            device_id=on_sib,
            device_id_type=MESH,
        )

    loop(width // 512, functools.partial(fill, send_a))
    pl.semaphore_wait(barrier, len(partners))
    for j in hops:
        to_peer(send_a, recv_a, a_send, a_recv, j).start()
    recv_a[slot_of(z, core), :] = send_a[block_of(z), :]
    to_sibling(recv_a, fa_send, a_recv, 0).start()

    table[...] = table_rows(gate_ref)

    def weigh(i):
        at = pl.ds(pl.multiple_of(i * 16, 16), 16)
        table[at, :] = table[at, :] * cot_ref[at, :].astype(F32)

    loop(tok_dev // 16, weigh)
    loop(width // 512, functools.partial(fill, send_b))
    recv_b[slot_of(z, core), :] = send_b[block_of(z), :]
    to_sibling(recv_b, fb_send, b_recv, 0).start()

    row = chosen_ref[pl.ds(z, 1), :]
    diagonal = iota((cap, cap), 0) == iota((cap, cap), 1)
    column = jnp.sum(jnp.where(diagonal, row.astype(F32), 0.0), axis=1, keepdims=True)
    row_f = row.astype(F32)
    owner_row = jnp.floor(row_f * (1.0 / tok_dev))
    owner_col = jnp.floor(column * (1.0 / tok_dev))
    ahead = jnp.where((owner_row == owner_col) & (row_f < column), 1.0, 0.0)
    place_in = jnp.sum(ahead, axis=1, keepdims=True)
    owner_z = jnp.floor(owner_col * 0.5)
    owner_c = owner_col - 2.0 * owner_z
    at_slot = (owner_c * nz + owner_z) * SLOT + place_in
    place_f = jnp.where(
        iota((cap, 2 * slots), 1).astype(F32) == at_slot, 1.0, 0.0
    )
    place[...] = place_f.astype(BF16)
    place_t[...] = place_f.T.astype(BF16)

    for j in hops:
        from_peer(recv_a, a_send, a_recv, j).wait_recv()
        to_sibling(recv_a, fa_send, a_recv, j).start()
        to_peer(send_a, recv_a, a_send, a_recv, j).wait_send()
        to_peer(send_b, recv_b, b_send, b_recv, j).start()
    for j in [0] + hops:
        from_sibling(recv_a, fa_send, a_recv, j).wait_recv()

    def gather(src, dst, i):
        at = pl.ds(pl.multiple_of(i * 512, 512), 512)
        dst[:, at] = mm(place[...], src[:, at], NN).astype(BF16)

    def gather_in(i):
        at = pl.ds(pl.multiple_of(i * 512, 512), 512)
        product = mm(place[...], recv_a[:, at], NN).astype(BF16)
        rows_in[:, at] = product
        for k in range(SIDE):
            columns_in[i, k] = product[:, k * 128 : (k + 1) * 128]

    loop(SIDE, gather_in)

    def along(axis, by):
        return lax.rem((gx if axis == 0 else gy) + by, SIDE)

    def line_copy(src, dst, k, axis, by):
        return pltpu.make_async_remote_copy(
            src_ref=src,
            dst_ref=dst,
            send_sem=l_send.at[k],
            recv_sem=l_recv.at[k],
            device_id=on_axis(axis, by),
            device_id_type=MESH,
        )

    row_copies = []
    for by in (2, 1, 3):
        row_copies.append(
            line_copy(columns_in.at[along(0, by)], line_rows.at[0, by - 1], by - 1, 0, by)
        )
        row_copies.append(
            line_copy(columns_in.at[:, along(1, by)], line_rows.at[1, by - 1], by + 2, 1, by)
        )
    for c in row_copies:
        c.start()
    for load in loads:
        load.wait()
    weight = combine_ref[pl.ds(z, 1), :]

    def forward(i):
        at = pl.ds(pl.multiple_of(i * rows_q, rows_q), rows_q)
        pre_gate = mm(wg[at, :], rows_in[...], NT)
        pre_up = mm(wu[at, :], rows_in[...], NT)
        sig = 1.0 / (1.0 + jnp.exp(-pre_gate))
        silu = pre_gate * sig
        hid = silu * pre_up
        hidden[at, :] = hid.astype(BF16)
        hidden_c[at, :] = (hid * weight).astype(BF16)
        up_f[at, :] = silu * weight
        gate_f[at, :] = pre_up * sig * (1.0 + pre_gate * (1.0 - sig)) * weight

    loop(4, forward)

    for j in hops:
        from_peer(recv_b, b_send, b_recv, j).wait_recv()
        to_sibling(recv_b, fb_send, b_recv, j).start()
    for j in [0] + hops:
        from_sibling(recv_b, fb_send, b_recv, j).wait_recv()
    loop(width // 512, functools.partial(gather, recv_b, rows_grad))

    def down_grad(i):
        at = pl.ds(pl.multiple_of(i * 512, 512), 512)
        product = mm(hidden_c[...], rows_grad[:, at], NN).astype(BF16)
        for k in range(SIDE):
            piece = product[:, k * 128 : (k + 1) * 128]
            grads[0, i * SIDE + k] = piece[:rows_h]
            grads[1, k * SIDE + i] = piece[rows_h:]

    def line_grad(t, h):
        n = 2 * t + h
        mine = (d_gate, d_up)[t - 1]
        here = [columns_in[gx, k] if h == 0 else columns_in[k, gy] for k in range(SIDE)]
        total = mm(
            mine[h * rows_h : (h + 1) * rows_h, :], jnp.concatenate(here, axis=1), NN
        )
        for r in range(SIDE - 1):
            rows = jnp.concatenate([line_rows[h, r, k] for k in range(SIDE)], axis=1)
            total = total + mm(line_gate[t - 1, h, r], rows, NN)
        total = total.astype(BF16)
        for k in range(SIDE):
            parts[n, k] = total[:, k * 128 : (k + 1) * 128]

    def ring(t, h):
        n = 2 * t + h
        ia, ib = (gx, gy) if h == 0 else (gy, gx)
        own, other = h, 1 - h

        def copy(src, dst, k, axis, by):
            return pltpu.make_async_remote_copy(
                src_ref=src,
                dst_ref=dst,
                send_sem=r_send.at[n * 12 + k],
                recv_sem=r_recv.at[n * 12 + k],
                device_id=on_axis(axis, by),
                device_id_type=MESH,
            )

        def pair(dest, q):
            return pl.ds(lax.rem(ia + dest, SIDE) * SIDE + 2 * q, 2)

        def sub(dest):
            return lax.rem(ib + dest, SIDE)

        one, two = (1, SIDE - 1), SIDE // 2
        first_copies = []
        if t == 0:
            first_copies = [
                copy(grads.at[n, pair(two, 0)], far1.at[n, 0], 0, own, one[0]),
                copy(grads.at[n, pair(two, 1)], far1.at[n, 1], 1, own, one[1]),
                copy(grads.at[n, pair(1, 1)], near1.at[n, 0, pl.ds(2, 2)], 2, own, one[0]),
                copy(grads.at[n, pair(3, 0)], near1.at[n, 1, pl.ds(0, 2)], 3, own, one[1]),
                copy(grads.at[n, pair(1, 0)], near1.at[n, 0, pl.ds(0, 2)], 4, own, one[0]),
                copy(grads.at[n, pair(3, 1)], near1.at[n, 1, pl.ds(2, 2)], 5, own, one[1]),
            ]
        top, low = pl.ds(0, rows_q), pl.ds(rows_q, rows_q)
        next_copies = [
            copy(parts.at[n, sub(two), top], far2.at[n, 0], 6, other, one[0]),
            copy(parts.at[n, sub(two), low], far2.at[n, 1], 7, other, one[1]),
            copy(parts.at[n, sub(1), low], near2.at[n, 0, low], 8, other, one[0]),
            copy(parts.at[n, sub(3), top], near2.at[n, 1, top], 9, other, one[1]),
            copy(parts.at[n, sub(1), top], near2.at[n, 0, top], 10, other, one[0]),
            copy(parts.at[n, sub(3), low], near2.at[n, 1, low], 11, other, one[1]),
        ]

        def start1():
            for c in first_copies[:4]:
                c.start()

        def merge1():
            for side, dest in ((0, 1), (1, 3)):
                first_copies[side].wait_recv()
                base = lax.rem(ia + dest, SIDE) * SIDE + 2 * side

                def add(i):
                    grads[n, base + i] = (
                        grads[n, base + i].astype(F32) + far1[n, side, i].astype(F32)
                    ).astype(BF16)

                loop(2, add)
                first_copies[4 + side].start()

        def start2():
            for c in next_copies[:4]:
                c.start()

        def finish1():
            for c in first_copies[2:]:
                c.wait_recv()
            base = ia * SIDE

            def add(i):
                parts[n, i] = (
                    grads[n, base + i].astype(F32)
                    + near1[n, 0, i].astype(F32)
                    + near1[n, 1, i].astype(F32)
                ).astype(BF16)

            loop(SIDE, add)
            start2()

        def merge2():
            for side, dest, part in ((0, 1, top), (1, 3, low)):
                next_copies[side].wait_recv()
                parts[n, sub(dest), part] = (
                    parts[n, sub(dest), part].astype(F32) + far2[n, side].astype(F32)
                ).astype(BF16)
                next_copies[4 + side].start()

        def finish2(out):
            for c in next_copies[2:]:
                c.wait_recv()
            total = (
                parts[n, sub(0)].astype(F32)
                + near2[n, 0].astype(F32)
                + near2[n, 1].astype(F32)
            )
            out[h * rows_h : (h + 1) * rows_h, :] = (total * (1.0 / (SIDE * SIDE))).astype(BF16)

        def drain():
            for c in first_copies + next_copies:
                c.wait_send()

        return start1, merge1, finish1, merge2, finish2, drain, start2

    rings = {(t, h): ring(t, h) for t in range(3) for h in range(2)}

    def run(t, phase, *args):
        for h in range(2):
            rings[t, h][phase](*args)

    def backward(i):
        at = pl.ds(pl.multiple_of(i * rows_q, rows_q), rows_q)
        raw = mm(wd[at, :], rows_grad[...], NT)
        inner = jnp.sum(hidden[at, :].astype(F32) * raw, axis=0, keepdims=True)
        d_gate[at, :] = (raw * gate_f[at, :]).astype(BF16)
        d_up[at, :] = (raw * up_f[at, :]).astype(BF16)
        return inner

    inner = backward(0)
    for i in range(1, 4):
        inner = inner + backward(i)
    gate_copies = []
    for t, grad in ((1, d_gate), (2, d_up)):
        for by in (2, 1, 3):
            for h in range(2):
                gate_copies.append(
                    line_copy(
                        grad.at[pl.ds(h * rows_h, rows_h)],
                        line_gate.at[t - 1, h, by - 1],
                        6 * t + 3 * h + by - 1,
                        h,
                        by,
                    )
                )
    for c in gate_copies:
        c.start()
    loop(SIDE, down_grad)
    run(0, 0)
    left, right = inner[:, : cap // 2], inner[:, cap // 2 :]
    mine = jnp.where(core == 0, left, right)
    theirs = jnp.where(core == 0, right, left)
    inner_s[...] = jnp.broadcast_to(theirs, inner_s.shape)
    inner_copy = pltpu.make_async_remote_copy(
        src_ref=inner_s,
        dst_ref=inner_r,
        send_sem=s_send.at[0],
        recv_sem=s_recv.at[0],
        device_id=on_sib,
        device_id_type=MESH,
    )
    inner_copy.start()
    d_gate_t[...] = d_gate[...].astype(F32).T.astype(BF16)
    d_up_t[...] = d_up[...].astype(F32).T.astype(BF16)

    def input_grad(i):
        at = pl.ds(pl.multiple_of(i * 512, 512), 512)
        total = mm(d_gate_t[...], wg[:, at], NN) + mm(d_up_t[...], wu[:, at], NN)
        back[:, at] = mm(place_t[...], total.astype(BF16), NN).astype(BF16)

    loop(width // 512, input_grad)
    their_rows = pl.ds(pl.multiple_of((1 - core) * slots, slots), slots)
    sib_copy = pltpu.make_async_remote_copy(
        src_ref=back.at[their_rows],
        dst_ref=sib,
        send_sem=s_send.at[1],
        recv_sem=s_recv.at[1],
        device_id=on_sib,
        device_id_type=MESH,
    )
    sib_copy.start()
    run(0, 1)
    sib_copy.wait_recv()

    def add_halves(i):
        at = pl.ds(pl.multiple_of(i * SLOT, SLOT), SLOT)
        here = slot_of(i, core)
        send_c[at, :] = (back[here, :].astype(F32) + sib[at, :].astype(F32)).astype(BF16)

    loop(nz, add_halves)

    def to_owner(j):
        zz = peer(j)
        return pltpu.make_async_remote_copy(
            src_ref=send_c.at[block_of(zz)],
            dst_ref=ret.at[block_of(z)],
            send_sem=c_send.at[j],
            recv_sem=c_recv.at[j],
            device_id=on_z(zz),
            device_id_type=MESH,
        )

    def from_expert(j):
        zz = peer(nz - j)
        return pltpu.make_async_remote_copy(
            src_ref=ret.at[block_of(zz)],
            dst_ref=ret.at[block_of(zz)],
            send_sem=c_send.at[j],
            recv_sem=c_recv.at[j],
            device_id=on_z(peer(j)),
            device_id_type=MESH,
        )

    for j in hops:
        to_owner(j).start()
    ret[block_of(z), :] = send_c[block_of(z), :]
    inner_copy.wait_recv()
    dcomb_ref[...] = mine + inner_r[0:1, :]
    for c in row_copies:
        c.wait_recv()
    for t in (1, 2):
        for c in gate_copies[6 * (t - 1) : 6 * t]:
            c.wait_recv()
        for h in range(2):
            line_grad(t, h)
            rings[t, h][6]()
    run(0, 2)
    run(1, 3)
    run(2, 3)
    run(0, 3)
    for j in hops:
        from_expert(j).wait_recv()

    def spread_back(i):
        at = pl.ds(pl.multiple_of(i * 512, 512), 512)
        table[:, at] = mm(pick_t[...], ret[:, at], NN)

    loop(width // 512, spread_back)

    def token_grad(i):
        at = pl.ds(pl.multiple_of(i * 16, 16), 16)
        norm = normed[at, :]
        d_norm = table[at, :] * scale1[at, :]
        centre = jnp.mean(d_norm, axis=1, keepdims=True)
        along = jnp.mean(d_norm * norm, axis=1, keepdims=True)
        dtok_ref[at, :] = (inverse[at, :] * (d_norm - centre - norm * along)).astype(BF16)

    loop(tok_dev // 16, token_grad)
    run(1, 4, dwg_ref)
    run(2, 4, dwu_ref)
    run(0, 4, dwd_ref)

    for j in hops:
        to_peer(send_b, recv_b, b_send, b_recv, j).wait_send()
        to_owner(j).wait_send()
    for j in [0] + hops:
        to_sibling(recv_a, fa_send, a_recv, j).wait_send()
        to_sibling(recv_b, fb_send, b_recv, j).wait_send()
    for c in row_copies + gate_copies:
        c.wait_send()
    inner_copy.wait_send()
    sib_copy.wait_send()
    for t in range(3):
        run(t, 5)


def copy_kernel(*refs):
    count = len(refs) // 2
    sems = refs[-1]
    copies = [
        pltpu.make_async_copy(refs[i], refs[count + i], sems.at[i]) for i in range(count)
    ]
    for c in copies:
        c.start()
    for c in copies:
        c.wait()


def solution(mesh):
    nz = mesh.shape["exp"] // 2

    def on_device(
        tokens, cotangent, timestep, shift_table, scale_table, gate_table, chosen, combine, w_gate, w_up, w_down
    ):
        tok_dev, width = tokens.shape
        half = w_gate.shape[1]
        cap = chosen.shape[2]
        slots = nz * SLOT
        rows_h, rows_q = half // 2, half // 4
        vmem = pl.BlockSpec(memory_space=pltpu.VMEM)
        hbm = pl.BlockSpec(memory_space=pl.ANY)
        dma = pltpu.SemaphoreType.DMA
        outs = pl.pallas_call(
            functools.partial(layer_kernel, nz),
            out_shape=(
                jax.ShapeDtypeStruct((tok_dev, width), BF16),
                jax.ShapeDtypeStruct((1, cap // 2), F32),
                jax.ShapeDtypeStruct((half, 128), BF16),
                jax.ShapeDtypeStruct((half, 128), BF16),
                jax.ShapeDtypeStruct((half, 128), BF16),
            ),
            in_specs=[vmem] * 8 + [hbm] * 3,
            out_specs=(vmem,) * 5,
            scratch_shapes=[
                pltpu.VMEM((half, width), BF16),
                pltpu.VMEM((half, width), BF16),
                pltpu.VMEM((half, width), BF16),
                pltpu.VMEM((slots, width), BF16),
                pltpu.VMEM((slots, width), BF16),
                pltpu.VMEM((2 * slots, width), BF16),
                pltpu.VMEM((2 * slots, width), BF16),
                pltpu.VMEM((cap, width), BF16),
                pltpu.VMEM((cap, width), BF16),
                pltpu.VMEM((tok_dev, width), F32),
                pltpu.VMEM((tok_dev, width), F32),
                pltpu.VMEM((tok_dev, width), F32),
                pltpu.VMEM((tok_dev, 1), F32),
                pltpu.VMEM((slots, tok_dev), BF16),
                pltpu.VMEM((tok_dev, slots), BF16),
                pltpu.VMEM((cap, 2 * slots), BF16),
                pltpu.VMEM((2 * slots, cap), BF16),
                pltpu.VMEM((half, cap), BF16),
                pltpu.VMEM((half, cap), BF16),
                pltpu.VMEM((half, cap), F32),
                pltpu.VMEM((half, cap), F32),
                pltpu.VMEM((half, cap), BF16),
                pltpu.VMEM((half, cap), BF16),
                pltpu.VMEM((cap, half), BF16),
                pltpu.VMEM((cap, half), BF16),

                pltpu.VMEM((2 * slots, width), BF16),
                pltpu.VMEM((slots, width), BF16),
                pltpu.VMEM((slots, width), BF16),
                pltpu.VMEM((slots, width), BF16),
                pltpu.VMEM((8, cap // 2), F32),
                pltpu.VMEM((8, cap // 2), F32),
                pltpu.VMEM((SIDE, SIDE, cap, 128), BF16),
                pltpu.VMEM((2, SIDE - 1, SIDE, cap, 128), BF16),
                pltpu.VMEM((2, 2, SIDE - 1, rows_h, cap), BF16),
                pltpu.VMEM((2, SIDE * SIDE, rows_h, 128), BF16),
                pltpu.VMEM((6, SIDE, rows_h, 128), BF16),
                pltpu.VMEM((2, 2, 2, rows_h, 128), BF16),
                pltpu.VMEM((2, 2, SIDE, rows_h, 128), BF16),
                pltpu.VMEM((6, 2, rows_q, 128), BF16),
                pltpu.VMEM((6, 2, rows_h, 128), BF16),
                dma((3,)),
                dma((nz,)),
                dma((2 * nz,)),
                dma((nz,)),
                dma((2 * nz,)),
                dma((nz,)),
                dma((nz,)),
                dma((nz,)),
                dma((nz,)),
                dma((2,)),
                dma((2,)),
                dma((72,)),
                dma((72,)),
                dma((18,)),
                dma((18,)),
            ],
            compiler_params=pltpu.CompilerParams(
                collective_id=0, has_side_effects=True, vmem_limit_bytes=60 * 1024 * 1024
            ),
        )(
            tokens,
            cotangent,
            timestep[None, :],
            shift_table,
            scale_table,
            gate_table,
            chosen[0],
            combine[0],
            w_gate[0],
            w_up[0],
            w_down[0],
        )
        outs = pl.pallas_call(
            copy_kernel,
            out_shape=tuple(jax.ShapeDtypeStruct(o.shape, o.dtype) for o in outs),
            in_specs=[hbm] * 5,
            out_specs=(hbm,) * 5,
            scratch_shapes=[dma((5,))],
        )(*outs)
        d_tokens, d_combine, d_gate, d_up, d_down = outs
        return d_tokens, d_combine[None], d_gate[None], d_up[None], d_down[None]

    in_specs = (
        P(("grp", "exp"), None),
        P(("grp", "exp"), None),
        P(("grp", "exp")),
        P(),
        P(),
        P(),
        P("grp", None, None),
        P("grp", None, None),
        P("exp", None, None),
        P("exp", None, None),
        P("exp", None, None),
    )
    out_specs = (
        P(("grp", "exp"), None),
        P("grp", "exp", None),
        P("exp", None, "grp"),
        P("exp", None, "grp"),
        P("exp", None, "grp"),
    )
    return jax.shard_map(
        on_device, mesh=mesh, in_specs=in_specs, out_specs=out_specs, check_vma=False
    )
```

```python
import functools

import jax
import jax.numpy as jnp
from jax import lax
from jax.experimental import pallas as pl
from jax.experimental.pallas import tpu as pltpu
from jax.sharding import PartitionSpec as P

EPSILON = 1e-06
MESH = pl.DeviceIdType.MESH
F32 = jnp.float32
BF16 = jnp.bfloat16
SLOT = 32
SIDE = 4
CHUNKS = 2
NN = (((1,), (0,)), ((), ()))
NT = (((1,), (1,)), ((), ()))
TN = (((0,), (0,)), ((), ()))


def mm(a, b, dims):
    return lax.dot_general(a, b, dims, preferred_element_type=F32)


def iota(shape, axis):
    return lax.broadcasted_iota(jnp.int32, shape, axis)


def loop(count, body):
    def step(i, carry):
        body(i)
        return carry

    lax.fori_loop(0, count, step, 0)


def layer_kernel(
    nz,
    tok_ref,
    cot_ref,
    step_ref,
    shift_ref,
    scale_ref,
    gate_ref,
    chosen_ref,
    combine_ref,
    wg_hbm,
    wu_hbm,
    wd_hbm,
    dtok_ref,
    dcomb_ref,
    dwg_ref,
    dwu_ref,
    dwd_ref,
    wg,
    wu,
    wd,
    send_a,
    send_b,
    recv_a,
    recv_b,
    rows_in,
    rows_grad,
    normed,
    scale1,
    table,
    inverse,
    pick,
    pick_t,
    place,
    place_t,
    hidden,
    hidden_c,
    gate_f,
    up_f,
    d_gate,
    d_up,
    d_gate_t,
    d_up_t,
    back,
    sib,
    send_c,
    ret,
    inner_s,
    inner_r,
    columns_in,
    line_rows,
    line_gate,
    grads,
    parts,
    far1,
    near1,
    far2,
    near2,
    w_sem,
    a_send,
    a_recv,
    b_send,
    b_recv,
    fa_send,
    fb_send,
    c_send,
    c_recv,
    s_send,
    s_recv,
    r_send,
    r_recv,
    l_send,
    l_recv,
):
    tok_dev, width = tok_ref.shape
    half = wg.shape[0]
    cap = rows_in.shape[0]
    rows_h = half // 2
    rows_q = half // 4
    g = lax.axis_index("grp")
    me = lax.axis_index("exp")
    z = lax.div(me, 2)
    core = lax.rem(me, 2)
    gx = lax.div(g, SIDE)
    gy = lax.rem(g, SIDE)
    sibling = z * 2 + (1 - core)

    def peer(j):
        return lax.rem(z + j, nz)

    def on_z(zz):
        return {"grp": g, "exp": zz * 2 + core}

    on_sib = {"grp": g, "exp": sibling}

    def on_axis(axis, by):
        if axis == 0:
            return {"grp": lax.rem(gx + by, SIDE) * SIDE + gy, "exp": me}
        return {"grp": gx * SIDE + lax.rem(gy + by, SIDE), "exp": me}

    hops = [1, 7, 2, 6, 3, 5, 4] if nz == 8 else list(range(1, nz))

    loads = [
        pltpu.make_async_copy(src, dst, w_sem.at[i])
        for i, (src, dst) in enumerate(((wg_hbm, wg), (wu_hbm, wu), (wd_hbm, wd)))
    ]
    for load in loads:
        load.start()
    barrier = pltpu.get_barrier_semaphore()
    partners = [on_z(peer(j)) for j in hops] + [on_sib]
    partners += [on_axis(axis, by) for axis in (0, 1) for by in (1, 2, 3)]
    for partner in partners:
        pl.semaphore_signal(barrier, inc=1, device_id=partner, device_id_type=MESH)

    first = me * tok_dev
    ids = iota((tok_dev, cap), 0) + first
    lane_e = iota((tok_dev, nz), 1)
    mask = jnp.zeros((tok_dev, nz), F32)
    for e in range(nz):
        hit = jnp.sum(
            jnp.where(ids == chosen_ref[e : e + 1, :], 1.0, 0.0), axis=1, keepdims=True
        )
        mask = jnp.where(lane_e == e, hit, mask)
    earlier = (iota((tok_dev, tok_dev), 1) < iota((tok_dev, tok_dev), 0)).astype(F32)
    rank = mm(earlier.astype(BF16), mask.astype(BF16), NN)
    slots = nz * SLOT
    spread = (lax.div(iota((nz, slots), 1), SLOT) == iota((nz, slots), 0)).astype(F32).astype(BF16)
    rank_p = mm(rank.astype(BF16), spread, NN)
    mask_p = mm(mask.astype(BF16), spread, NN)
    want = lax.rem(iota((tok_dev, slots), 1), SLOT).astype(F32)
    pick_f = jnp.where((rank_p == want) & (mask_p > 0.5), 1.0, 0.0)
    pick_t[...] = pick_f.astype(BF16)
    pick[...] = pick_f.T.astype(BF16)

    steps3 = 3 * scale_ref.shape[0]
    onehot = (lax.rem(iota((steps3, tok_dev), 0), scale_ref.shape[0]) == step_ref[...]).astype(F32)
    onehot = onehot.T.astype(BF16)

    def table_rows(ref):
        whole = ref[...]
        hi = whole.astype(BF16)
        rest = whole - hi.astype(F32)
        mid = rest.astype(BF16)
        low = (rest - mid.astype(F32)).astype(BF16)
        return mm(onehot, jnp.concatenate([hi, mid, low], axis=0), NN)

    scale1[...] = 1.0 + table_rows(scale_ref)
    table[...] = table_rows(shift_ref)

    def normalise(i):
        at = pl.ds(pl.multiple_of(i * 16, 16), 16)
        values = tok_ref[at, :].astype(F32)
        centred = values - jnp.mean(values, axis=1, keepdims=True)
        inv = lax.rsqrt(jnp.mean(centred * centred, axis=1, keepdims=True) + EPSILON)
        inverse[at, :] = inv
        norm = centred * inv
        normed[at, :] = norm
        table[at, :] = norm * scale1[at, :] + table[at, :]

    loop(tok_dev // 16, normalise)

    def fill(dst, i):
        at = pl.ds(pl.multiple_of(i * 512, 512), 512)
        dst[:, at] = mm(pick[...], table[:, at].astype(BF16), NN).astype(BF16)

    def slot_of(zz, cc):
        return pl.ds(pl.multiple_of((cc * nz + zz) * SLOT, SLOT), SLOT)

    def block_of(zz):
        return pl.ds(pl.multiple_of(zz * SLOT, SLOT), SLOT)

    def to_peer(src, dst, s_sem, r_sem, j):
        zz = peer(j)
        return pltpu.make_async_remote_copy(
            src_ref=src.at[block_of(zz)],
            dst_ref=dst.at[slot_of(z, core)],
            send_sem=s_sem.at[j],
            recv_sem=r_sem.at[j],
            device_id=on_z(zz),
            device_id_type=MESH,
        )

    def from_peer(dst, s_sem, r_sem, j):
        zz = peer(nz - j)
        return pltpu.make_async_remote_copy(
            src_ref=dst.at[slot_of(zz, core)],
            dst_ref=dst.at[slot_of(zz, core)],
            send_sem=s_sem.at[j],
            recv_sem=r_sem.at[j],
            device_id=on_z(peer(j)),
            device_id_type=MESH,
        )

    def to_sibling(dst, s_sem, r_sem, j):
        zz = peer(nz - j)
        return pltpu.make_async_remote_copy(
            src_ref=dst.at[slot_of(zz, core)],
            dst_ref=dst.at[slot_of(zz, core)],
            send_sem=s_sem.at[j],
            recv_sem=r_sem.at[nz + j],
            device_id=on_sib,
            device_id_type=MESH,
        )

    def from_sibling(dst, s_sem, r_sem, j):
        zz = peer(nz - j)
        return pltpu.make_async_remote_copy(
            src_ref=dst.at[slot_of(zz, 1 - core)],
            dst_ref=dst.at[slot_of(zz, 1 - core)],
            send_sem=s_sem.at[j],
            recv_sem=r_sem.at[nz + j],
            device_id=on_sib,
            device_id_type=MESH,
        )

    loop(width // 512, functools.partial(fill, send_a))
    pl.semaphore_wait(barrier, len(partners))
    for j in hops:
        to_peer(send_a, recv_a, a_send, a_recv, j).start()
    recv_a[slot_of(z, core), :] = send_a[block_of(z), :]
    to_sibling(recv_a, fa_send, a_recv, 0).start()

    table[...] = table_rows(gate_ref)

    def weigh(i):
        at = pl.ds(pl.multiple_of(i * 16, 16), 16)
        table[at, :] = table[at, :] * cot_ref[at, :].astype(F32)

    loop(tok_dev // 16, weigh)
    loop(width // 512, functools.partial(fill, send_b))
    recv_b[slot_of(z, core), :] = send_b[block_of(z), :]
    to_sibling(recv_b, fb_send, b_recv, 0).start()

    row = chosen_ref[pl.ds(z, 1), :]
    diagonal = iota((cap, cap), 0) == iota((cap, cap), 1)
    column = jnp.sum(jnp.where(diagonal, row.astype(F32), 0.0), axis=1, keepdims=True)
    row_f = row.astype(F32)
    owner_row = jnp.floor(row_f * (1.0 / tok_dev))
    owner_col = jnp.floor(column * (1.0 / tok_dev))
    ahead = jnp.where((owner_row == owner_col) & (row_f < column), 1.0, 0.0)
    place_in = jnp.sum(ahead, axis=1, keepdims=True)
    owner_z = jnp.floor(owner_col * 0.5)
    owner_c = owner_col - 2.0 * owner_z
    at_slot = (owner_c * nz + owner_z) * SLOT + place_in
    place_f = jnp.where(
        iota((cap, 2 * slots), 1).astype(F32) == at_slot, 1.0, 0.0
    )
    place[...] = place_f.astype(BF16)
    place_t[...] = place_f.T.astype(BF16)

    for j in hops:
        from_peer(recv_a, a_send, a_recv, j).wait_recv()
        to_sibling(recv_a, fa_send, a_recv, j).start()
        to_peer(send_a, recv_a, a_send, a_recv, j).wait_send()
        to_peer(send_b, recv_b, b_send, b_recv, j).start()
    for j in [0] + hops:
        from_sibling(recv_a, fa_send, a_recv, j).wait_recv()

    def gather(src, dst, i):
        at = pl.ds(pl.multiple_of(i * 512, 512), 512)
        dst[:, at] = mm(place[...], src[:, at], NN).astype(BF16)

    def gather_in(i):
        at = pl.ds(pl.multiple_of(i * 512, 512), 512)
        product = mm(place[...], recv_a[:, at], NN).astype(BF16)
        rows_in[:, at] = product
        for k in range(SIDE):
            columns_in[i, k] = product[:, k * 128 : (k + 1) * 128]

    loop(SIDE, gather_in)

    def along(axis, by):
        return lax.rem((gx if axis == 0 else gy) + by, SIDE)

    def line_copy(src, dst, k, axis, by):
        return pltpu.make_async_remote_copy(
            src_ref=src,
            dst_ref=dst,
            send_sem=l_send.at[k],
            recv_sem=l_recv.at[k],
            device_id=on_axis(axis, by),
            device_id_type=MESH,
        )

    row_copies = []
    for by in (2, 1, 3):
        row_copies.append(
            line_copy(columns_in.at[along(0, by)], line_rows.at[0, by - 1], by - 1, 0, by)
        )
        row_copies.append(
            line_copy(columns_in.at[:, along(1, by)], line_rows.at[1, by - 1], by + 2, 1, by)
        )
    for c in row_copies:
        c.start()
    for load in loads:
        load.wait()
    weight = combine_ref[pl.ds(z, 1), :]

    def forward(i):
        at = pl.ds(pl.multiple_of(i * rows_q, rows_q), rows_q)
        pre_gate = mm(wg[at, :], rows_in[...], NT)
        pre_up = mm(wu[at, :], rows_in[...], NT)
        sig = 1.0 / (1.0 + jnp.exp(-pre_gate))
        silu = pre_gate * sig
        hid = silu * pre_up
        hidden[at, :] = hid.astype(BF16)
        hidden_c[at, :] = (hid * weight).astype(BF16)
        up_f[at, :] = silu * weight
        gate_f[at, :] = pre_up * sig * (1.0 + pre_gate * (1.0 - sig)) * weight

    loop(4, forward)

    for j in hops:
        from_peer(recv_b, b_send, b_recv, j).wait_recv()
        to_sibling(recv_b, fb_send, b_recv, j).start()
    for j in [0] + hops:
        from_sibling(recv_b, fb_send, b_recv, j).wait_recv()
    loop(width // 512, functools.partial(gather, recv_b, rows_grad))

    def down_grad(i):
        at = pl.ds(pl.multiple_of(i * 512, 512), 512)
        product = mm(hidden_c[...], rows_grad[:, at], NN).astype(BF16)
        for k in range(SIDE):
            piece = product[:, k * 128 : (k + 1) * 128]
            grads[0, i * SIDE + k] = piece[:rows_h]
            grads[1, k * SIDE + i] = piece[rows_h:]

    def line_grad(t, h):
        n = 2 * t + h
        mine = (d_gate, d_up)[t - 1]
        here = [columns_in[gx, k] if h == 0 else columns_in[k, gy] for k in range(SIDE)]
        total = mm(
            mine[h * rows_h : (h + 1) * rows_h, :], jnp.concatenate(here, axis=1), NN
        )
        for r in range(SIDE - 1):
            rows = jnp.concatenate([line_rows[h, r, k] for k in range(SIDE)], axis=1)
            total = total + mm(line_gate[t - 1, h, r], rows, NN)
        total = total.astype(BF16)
        for k in range(SIDE):
            parts[n, k] = total[:, k * 128 : (k + 1) * 128]

    def ring(t, h):
        n = 2 * t + h
        ia, ib = (gx, gy) if h == 0 else (gy, gx)
        own, other = h, 1 - h

        def copy(src, dst, k, axis, by):
            return pltpu.make_async_remote_copy(
                src_ref=src,
                dst_ref=dst,
                send_sem=r_send.at[n * 12 + k],
                recv_sem=r_recv.at[n * 12 + k],
                device_id=on_axis(axis, by),
                device_id_type=MESH,
            )

        def pair(dest, q):
            return pl.ds(lax.rem(ia + dest, SIDE) * SIDE + 2 * q, 2)

        def sub(dest):
            return lax.rem(ib + dest, SIDE)

        one, two = (1, SIDE - 1), SIDE // 2
        first_copies = []
        if t == 0:
            first_copies = [
                copy(grads.at[n, pair(two, 0)], far1.at[n, 0], 0, own, one[0]),
                copy(grads.at[n, pair(two, 1)], far1.at[n, 1], 1, own, one[1]),
                copy(grads.at[n, pair(1, 1)], near1.at[n, 0, pl.ds(2, 2)], 2, own, one[0]),
                copy(grads.at[n, pair(3, 0)], near1.at[n, 1, pl.ds(0, 2)], 3, own, one[1]),
                copy(grads.at[n, pair(1, 0)], near1.at[n, 0, pl.ds(0, 2)], 4, own, one[0]),
                copy(grads.at[n, pair(3, 1)], near1.at[n, 1, pl.ds(2, 2)], 5, own, one[1]),
            ]
        top, low = pl.ds(0, rows_q), pl.ds(rows_q, rows_q)
        next_copies = [
            copy(parts.at[n, sub(two), top], far2.at[n, 0], 6, other, one[0]),
            copy(parts.at[n, sub(two), low], far2.at[n, 1], 7, other, one[1]),
            copy(parts.at[n, sub(1), low], near2.at[n, 0, low], 8, other, one[0]),
            copy(parts.at[n, sub(3), top], near2.at[n, 1, top], 9, other, one[1]),
            copy(parts.at[n, sub(1), top], near2.at[n, 0, top], 10, other, one[0]),
            copy(parts.at[n, sub(3), low], near2.at[n, 1, low], 11, other, one[1]),
        ]

        def start1():
            for c in first_copies[:4]:
                c.start()

        def merge1():
            for side, dest in ((0, 1), (1, 3)):
                first_copies[side].wait_recv()
                base = lax.rem(ia + dest, SIDE) * SIDE + 2 * side

                def add(i):
                    grads[n, base + i] = (
                        grads[n, base + i].astype(F32) + far1[n, side, i].astype(F32)
                    ).astype(BF16)

                loop(2, add)
                first_copies[4 + side].start()

        def start2():
            for c in next_copies[:4]:
                c.start()

        def finish1():
            for c in first_copies[2:]:
                c.wait_recv()
            base = ia * SIDE

            def add(i):
                parts[n, i] = (
                    grads[n, base + i].astype(F32)
                    + near1[n, 0, i].astype(F32)
                    + near1[n, 1, i].astype(F32)
                ).astype(BF16)

            loop(SIDE, add)
            start2()

        def merge2():
            for side, dest, part in ((0, 1, top), (1, 3, low)):
                next_copies[side].wait_recv()
                parts[n, sub(dest), part] = (
                    parts[n, sub(dest), part].astype(F32) + far2[n, side].astype(F32)
                ).astype(BF16)
                next_copies[4 + side].start()

        def finish2(out):
            for c in next_copies[2:]:
                c.wait_recv()
            total = (
                parts[n, sub(0)].astype(F32)
                + near2[n, 0].astype(F32)
                + near2[n, 1].astype(F32)
            )
            out[h * rows_h : (h + 1) * rows_h, :] = (total * (1.0 / (SIDE * SIDE))).astype(BF16)

        def drain():
            for c in first_copies + next_copies:
                c.wait_send()

        return start1, merge1, finish1, merge2, finish2, drain, start2

    rings = {(t, h): ring(t, h) for t in range(3) for h in range(2)}

    def run(t, phase, *args):
        for h in range(2):
            rings[t, h][phase](*args)

    def backward(i):
        at = pl.ds(pl.multiple_of(i * rows_q, rows_q), rows_q)
        raw = mm(wd[at, :], rows_grad[...], NT)
        inner = jnp.sum(hidden[at, :].astype(F32) * raw, axis=0, keepdims=True)
        d_gate[at, :] = (raw * gate_f[at, :]).astype(BF16)
        d_up[at, :] = (raw * up_f[at, :]).astype(BF16)
        return inner

    inner = backward(0)
    for i in range(1, 4):
        inner = inner + backward(i)
    gate_copies = []
    for t, grad in ((1, d_gate), (2, d_up)):
        for by in (2, 1, 3):
            for h in range(2):
                gate_copies.append(
                    line_copy(
                        grad.at[pl.ds(h * rows_h, rows_h)],
                        line_gate.at[t - 1, h, by - 1],
                        6 * t + 3 * h + by - 1,
                        h,
                        by,
                    )
                )
    for c in gate_copies:
        c.start()
    left, right = inner[:, : cap // 2], inner[:, cap // 2 :]
    mine = jnp.where(core == 0, left, right)
    theirs = jnp.where(core == 0, right, left)
    inner_s[...] = jnp.broadcast_to(theirs, inner_s.shape)
    inner_copy = pltpu.make_async_remote_copy(
        src_ref=inner_s,
        dst_ref=inner_r,
        send_sem=s_send.at[0],
        recv_sem=s_recv.at[0],
        device_id=on_sib,
        device_id_type=MESH,
    )
    inner_copy.start()
    d_gate_t[...] = d_gate[...].astype(F32).T.astype(BF16)
    d_up_t[...] = d_up[...].astype(F32).T.astype(BF16)

    chunk = width // CHUNKS
    own_rows = pl.ds(pl.multiple_of(core * slots, slots), slots)
    their_rows = pl.ds(pl.multiple_of((1 - core) * slots, slots), slots)

    def columns(i):
        return pl.ds(i * chunk, chunk)

    sib_copies = [
        pltpu.make_async_remote_copy(
            src_ref=back.at[their_rows, columns(i)],
            dst_ref=sib.at[:, columns(i)],
            send_sem=s_send.at[1 + i],
            recv_sem=s_recv.at[1 + i],
            device_id=on_sib,
            device_id_type=MESH,
        )
        for i in range(CHUNKS)
    ]

    def to_owner(j, i):
        zz = peer(j)
        return pltpu.make_async_remote_copy(
            src_ref=send_c.at[block_of(zz), columns(i)],
            dst_ref=ret.at[block_of(z), columns(i)],
            send_sem=c_send.at[j * CHUNKS + i],
            recv_sem=c_recv.at[j * CHUNKS + i],
            device_id=on_z(zz),
            device_id_type=MESH,
        )

    def from_expert(j, i):
        zz = peer(nz - j)
        return pltpu.make_async_remote_copy(
            src_ref=ret.at[block_of(zz), columns(i)],
            dst_ref=ret.at[block_of(zz), columns(i)],
            send_sem=c_send.at[j * CHUNKS + i],
            recv_sem=c_recv.at[j * CHUNKS + i],
            device_id=on_z(peer(j)),
            device_id_type=MESH,
        )

    def input_grad(i):
        at = columns(i)
        total = mm(d_gate_t[...], wg[:, at], NN) + mm(d_up_t[...], wu[:, at], NN)
        back[:, at] = mm(place_t[...], total.astype(BF16), NN).astype(BF16)
        sib_copies[i].start()

    def send_home(i):
        at = columns(i)
        sib_copies[i].wait_recv()
        send_c[:, at] = (back[own_rows, at].astype(F32) + sib[:, at].astype(F32)).astype(BF16)
        for j in hops:
            to_owner(j, i).start()
        ret[block_of(z), at] = send_c[block_of(z), at]

    for i in range(CHUNKS):
        input_grad(i)
        if i:
            send_home(i - 1)
    loop(SIDE, down_grad)
    run(0, 0)
    send_home(CHUNKS - 1)
    inner_copy.wait_recv()
    dcomb_ref[...] = mine + inner_r[0:1, :]
    for c in row_copies:
        c.wait_recv()
    run(0, 1)
    for t in (1, 2):
        for c in gate_copies[6 * (t - 1) : 6 * t]:
            c.wait_recv()
        for h in range(2):
            line_grad(t, h)
            rings[t, h][6]()
    run(0, 2)
    run(1, 3)
    run(2, 3)
    run(0, 3)
    for j in hops:
        for i in range(CHUNKS):
            from_expert(j, i).wait_recv()

    def spread_back(i):
        at = pl.ds(pl.multiple_of(i * 512, 512), 512)
        table[:, at] = mm(pick_t[...], ret[:, at], NN)

    loop(width // 512, spread_back)

    def token_grad(i):
        at = pl.ds(pl.multiple_of(i * 16, 16), 16)
        norm = normed[at, :]
        d_norm = table[at, :] * scale1[at, :]
        centre = jnp.mean(d_norm, axis=1, keepdims=True)
        along = jnp.mean(d_norm * norm, axis=1, keepdims=True)
        dtok_ref[at, :] = (inverse[at, :] * (d_norm - centre - norm * along)).astype(BF16)

    loop(tok_dev // 16, token_grad)
    run(1, 4, dwg_ref)
    run(2, 4, dwu_ref)
    run(0, 4, dwd_ref)

    for j in hops:
        to_peer(send_b, recv_b, b_send, b_recv, j).wait_send()
        for i in range(CHUNKS):
            to_owner(j, i).wait_send()
    for j in [0] + hops:
        to_sibling(recv_a, fa_send, a_recv, j).wait_send()
        to_sibling(recv_b, fb_send, b_recv, j).wait_send()
    for c in row_copies + gate_copies:
        c.wait_send()
    inner_copy.wait_send()
    for c in sib_copies:
        c.wait_send()
    for t in range(3):
        run(t, 5)


def copy_kernel(*refs):
    count = len(refs) // 2
    for i in range(count):
        refs[count + i][...] = refs[i][...]


def solution(mesh):
    nz = mesh.shape["exp"] // 2

    def on_device(
        tokens, cotangent, timestep, shift_table, scale_table, gate_table, chosen, combine, w_gate, w_up, w_down
    ):
        tok_dev, width = tokens.shape
        half = w_gate.shape[1]
        cap = chosen.shape[2]
        slots = nz * SLOT
        rows_h, rows_q = half // 2, half // 4
        vmem = pl.BlockSpec(memory_space=pltpu.VMEM)
        hbm = pl.BlockSpec(memory_space=pl.ANY)
        dma = pltpu.SemaphoreType.DMA
        outs = pl.pallas_call(
            functools.partial(layer_kernel, nz),
            out_shape=(
                jax.ShapeDtypeStruct((tok_dev, width), BF16),
                jax.ShapeDtypeStruct((1, cap // 2), F32),
                jax.ShapeDtypeStruct((half, 128), BF16),
                jax.ShapeDtypeStruct((half, 128), BF16),
                jax.ShapeDtypeStruct((half, 128), BF16),
            ),
            in_specs=[vmem] * 8 + [hbm] * 3,
            out_specs=(vmem,) * 5,
            scratch_shapes=[
                pltpu.VMEM((half, width), BF16),
                pltpu.VMEM((half, width), BF16),
                pltpu.VMEM((half, width), BF16),
                pltpu.VMEM((slots, width), BF16),
                pltpu.VMEM((slots, width), BF16),
                pltpu.VMEM((2 * slots, width), BF16),
                pltpu.VMEM((2 * slots, width), BF16),
                pltpu.VMEM((cap, width), BF16),
                pltpu.VMEM((cap, width), BF16),
                pltpu.VMEM((tok_dev, width), F32),
                pltpu.VMEM((tok_dev, width), F32),
                pltpu.VMEM((tok_dev, width), F32),
                pltpu.VMEM((tok_dev, 1), F32),
                pltpu.VMEM((slots, tok_dev), BF16),
                pltpu.VMEM((tok_dev, slots), BF16),
                pltpu.VMEM((cap, 2 * slots), BF16),
                pltpu.VMEM((2 * slots, cap), BF16),
                pltpu.VMEM((half, cap), BF16),
                pltpu.VMEM((half, cap), BF16),
                pltpu.VMEM((half, cap), F32),
                pltpu.VMEM((half, cap), F32),
                pltpu.VMEM((half, cap), BF16),
                pltpu.VMEM((half, cap), BF16),
                pltpu.VMEM((cap, half), BF16),
                pltpu.VMEM((cap, half), BF16),

                pltpu.VMEM((2 * slots, width), BF16),
                pltpu.VMEM((slots, width), BF16),
                pltpu.VMEM((slots, width), BF16),
                pltpu.VMEM((slots, width), BF16),
                pltpu.VMEM((8, cap // 2), F32),
                pltpu.VMEM((8, cap // 2), F32),
                pltpu.VMEM((SIDE, SIDE, cap, 128), BF16),
                pltpu.VMEM((2, SIDE - 1, SIDE, cap, 128), BF16),
                pltpu.VMEM((2, 2, SIDE - 1, rows_h, cap), BF16),
                pltpu.VMEM((2, SIDE * SIDE, rows_h, 128), BF16),
                pltpu.VMEM((6, SIDE, rows_h, 128), BF16),
                pltpu.VMEM((2, 2, 2, rows_h, 128), BF16),
                pltpu.VMEM((2, 2, SIDE, rows_h, 128), BF16),
                pltpu.VMEM((6, 2, rows_q, 128), BF16),
                pltpu.VMEM((6, 2, rows_h, 128), BF16),
                dma((3,)),
                dma((nz,)),
                dma((2 * nz,)),
                dma((nz,)),
                dma((2 * nz,)),
                dma((nz,)),
                dma((nz,)),
                dma((nz * CHUNKS,)),
                dma((nz * CHUNKS,)),
                dma((1 + CHUNKS,)),
                dma((1 + CHUNKS,)),
                dma((72,)),
                dma((72,)),
                dma((18,)),
                dma((18,)),
            ],
            compiler_params=pltpu.CompilerParams(
                collective_id=0, has_side_effects=True, vmem_limit_bytes=60 * 1024 * 1024
            ),
        )(
            tokens,
            cotangent,
            timestep[None, :],
            shift_table,
            scale_table,
            gate_table,
            chosen[0],
            combine[0],
            w_gate[0],
            w_up[0],
            w_down[0],
        )
        outs = pl.pallas_call(
            copy_kernel,
            out_shape=tuple(jax.ShapeDtypeStruct(o.shape, o.dtype) for o in outs),
            in_specs=[vmem] * 5,
            out_specs=(vmem,) * 5,
        )(*outs)
        d_tokens, d_combine, d_gate, d_up, d_down = outs
        return d_tokens, d_combine[None], d_gate[None], d_up[None], d_down[None]

    in_specs = (
        P(("grp", "exp"), None),
        P(("grp", "exp"), None),
        P(("grp", "exp")),
        P(),
        P(),
        P(),
        P("grp", None, None),
        P("grp", None, None),
        P("exp", None, None),
        P("exp", None, None),
        P("exp", None, None),
    )
    out_specs = (
        P(("grp", "exp"), None),
        P("grp", "exp", None),
        P("exp", None, "grp"),
        P("exp", None, "grp"),
        P("exp", None, "grp"),
    )
    return jax.shard_map(
        on_device, mesh=mesh, in_specs=in_specs, out_specs=out_specs, check_vma=False
    )
```

```python
import functools

import jax
import jax.numpy as jnp
from jax import lax
from jax.experimental import pallas as pl
from jax.experimental.pallas import tpu as pltpu
from jax.sharding import PartitionSpec as P

EPSILON = 1e-06
MESH = pl.DeviceIdType.MESH
F32 = jnp.float32
BF16 = jnp.bfloat16
SLOT = 32
SIDE = 4
CHUNKS = 2
ORDER = (2, 1, 3, 0)
NN = (((1,), (0,)), ((), ()))
NT = (((1,), (1,)), ((), ()))
TN = (((0,), (0,)), ((), ()))


def mm(a, b, dims):
    return lax.dot_general(a, b, dims, preferred_element_type=F32)


def iota(shape, axis):
    return lax.broadcasted_iota(jnp.int32, shape, axis)


def loop(count, body):
    def step(i, carry):
        body(i)
        return carry

    lax.fori_loop(0, count, step, 0)


def layer_kernel(
    nz,
    tok_ref,
    cot_ref,
    step_ref,
    shift_ref,
    scale_ref,
    gate_ref,
    chosen_ref,
    combine_ref,
    wg_hbm,
    wu_hbm,
    wd_hbm,
    dtok_ref,
    dcomb_ref,
    dwg_ref,
    dwu_ref,
    dwd_ref,
    wg,
    wu,
    wd,
    send_a,
    send_b,
    recv_a,
    recv_b,
    rows_in,
    rows_grad,
    normed,
    scale1,
    table,
    inverse,
    pick,
    pick_t,
    place,
    place_t,
    hidden,
    hidden_c,
    gate_f,
    up_f,
    raw,
    d_gate,
    d_up,
    d_gate_t,
    d_up_t,
    back,
    sib,
    send_c,
    ret,
    inner_s,
    inner_r,
    columns_in,
    line_rows,
    line_gate,
    grads,
    parts,
    far1,
    near1,
    far2,
    near2,
    w_sem,
    a_send,
    a_recv,
    b_send,
    b_recv,
    fa_send,
    fb_send,
    c_send,
    c_recv,
    s_send,
    s_recv,
    r_send,
    r_recv,
    l_send,
    l_recv,
):
    tok_dev, width = tok_ref.shape
    half = wg.shape[0]
    cap = rows_in.shape[0]
    rows_h = half // 2
    rows_q = half // 4
    g = lax.axis_index("grp")
    me = lax.axis_index("exp")
    z = lax.div(me, 2)
    core = lax.rem(me, 2)
    gx = lax.div(g, SIDE)
    gy = lax.rem(g, SIDE)
    sibling = z * 2 + (1 - core)

    def peer(j):
        return lax.rem(z + j, nz)

    def on_z(zz):
        return {"grp": g, "exp": zz * 2 + core}

    on_sib = {"grp": g, "exp": sibling}

    def on_axis(axis, by):
        if axis == 0:
            return {"grp": lax.rem(gx + by, SIDE) * SIDE + gy, "exp": me}
        return {"grp": gx * SIDE + lax.rem(gy + by, SIDE), "exp": me}

    hops = [1, 7, 2, 6, 3, 5, 4] if nz == 8 else list(range(1, nz))

    loads = [
        pltpu.make_async_copy(src, dst, w_sem.at[i])
        for i, (src, dst) in enumerate(((wg_hbm, wg), (wu_hbm, wu), (wd_hbm, wd)))
    ]
    for load in loads:
        load.start()
    barrier = pltpu.get_barrier_semaphore()
    partners = [on_z(peer(j)) for j in hops] + [on_sib]
    partners += [on_axis(axis, by) for axis in (0, 1) for by in (1, 2, 3)]
    for partner in partners:
        pl.semaphore_signal(barrier, inc=1, device_id=partner, device_id_type=MESH)

    first = me * tok_dev
    ids = iota((tok_dev, cap), 0) + first
    lane_e = iota((tok_dev, nz), 1)
    mask = jnp.zeros((tok_dev, nz), F32)
    for e in range(nz):
        hit = jnp.sum(
            jnp.where(ids == chosen_ref[e : e + 1, :], 1.0, 0.0), axis=1, keepdims=True
        )
        mask = jnp.where(lane_e == e, hit, mask)
    earlier = (iota((tok_dev, tok_dev), 1) < iota((tok_dev, tok_dev), 0)).astype(F32)
    rank = mm(earlier.astype(BF16), mask.astype(BF16), NN)
    slots = nz * SLOT
    spread = (lax.div(iota((nz, slots), 1), SLOT) == iota((nz, slots), 0)).astype(F32).astype(BF16)
    rank_p = mm(rank.astype(BF16), spread, NN)
    mask_p = mm(mask.astype(BF16), spread, NN)
    want = lax.rem(iota((tok_dev, slots), 1), SLOT).astype(F32)
    pick_f = jnp.where((rank_p == want) & (mask_p > 0.5), 1.0, 0.0)
    pick_t[...] = pick_f.astype(BF16)
    pick[...] = pick_f.T.astype(BF16)

    steps3 = 3 * scale_ref.shape[0]
    onehot = (lax.rem(iota((steps3, tok_dev), 0), scale_ref.shape[0]) == step_ref[...]).astype(F32)
    onehot = onehot.T.astype(BF16)

    def table_rows(ref):
        whole = ref[...]
        hi = whole.astype(BF16)
        rest = whole - hi.astype(F32)
        mid = rest.astype(BF16)
        low = (rest - mid.astype(F32)).astype(BF16)
        return mm(onehot, jnp.concatenate([hi, mid, low], axis=0), NN)

    scale1[...] = 1.0 + table_rows(scale_ref)
    table[...] = table_rows(shift_ref)

    def normalise(i):
        at = pl.ds(pl.multiple_of(i * 16, 16), 16)
        values = tok_ref[at, :].astype(F32)
        centred = values - jnp.mean(values, axis=1, keepdims=True)
        inv = lax.rsqrt(jnp.mean(centred * centred, axis=1, keepdims=True) + EPSILON)
        inverse[at, :] = inv
        norm = centred * inv
        normed[at, :] = norm
        table[at, :] = norm * scale1[at, :] + table[at, :]

    loop(tok_dev // 16, normalise)

    def fill(dst, i):
        at = pl.ds(pl.multiple_of(i * 512, 512), 512)
        dst[:, at] = mm(pick[...], table[:, at].astype(BF16), NN).astype(BF16)

    def slot_of(zz, cc):
        return pl.ds(pl.multiple_of((cc * nz + zz) * SLOT, SLOT), SLOT)

    def block_of(zz):
        return pl.ds(pl.multiple_of(zz * SLOT, SLOT), SLOT)

    def quarter(s):
        at = lax.rem(gx + ORDER[s], SIDE) * (width // SIDE)
        return pl.ds(pl.multiple_of(at, width // SIDE), width // SIDE)

    def part(ref, rows, s):
        return ref.at[rows] if s is None else ref.at[rows, quarter(s)]

    def sem(j, s):
        return j if s is None else j * SIDE + s

    def to_peer(src, dst, s_sem, r_sem, j, s=None):
        zz = peer(j)
        return pltpu.make_async_remote_copy(
            src_ref=part(src, block_of(zz), s),
            dst_ref=part(dst, slot_of(z, core), s),
            send_sem=s_sem.at[sem(j, s)],
            recv_sem=r_sem.at[sem(j, s)],
            device_id=on_z(zz),
            device_id_type=MESH,
        )

    def from_peer(dst, s_sem, r_sem, j, s=None):
        zz = peer(nz - j)
        return pltpu.make_async_remote_copy(
            src_ref=part(dst, slot_of(zz, core), s),
            dst_ref=part(dst, slot_of(zz, core), s),
            send_sem=s_sem.at[sem(j, s)],
            recv_sem=r_sem.at[sem(j, s)],
            device_id=on_z(peer(j)),
            device_id_type=MESH,
        )

    def to_sibling(dst, s_sem, r_sem, j, s=None):
        zz = peer(nz - j)
        return pltpu.make_async_remote_copy(
            src_ref=part(dst, slot_of(zz, core), s),
            dst_ref=part(dst, slot_of(zz, core), s),
            send_sem=s_sem.at[sem(j, s)],
            recv_sem=r_sem.at[sem(nz + j, s)],
            device_id=on_sib,
            device_id_type=MESH,
        )

    def from_sibling(dst, s_sem, r_sem, j, s=None):
        zz = peer(nz - j)
        return pltpu.make_async_remote_copy(
            src_ref=part(dst, slot_of(zz, 1 - core), s),
            dst_ref=part(dst, slot_of(zz, 1 - core), s),
            send_sem=s_sem.at[sem(j, s)],
            recv_sem=r_sem.at[sem(nz + j, s)],
            device_id=on_sib,
            device_id_type=MESH,
        )

    loop(width // 512, functools.partial(fill, send_a))
    pl.semaphore_wait(barrier, len(partners))
    for j in hops:
        to_peer(send_a, recv_a, a_send, a_recv, j).start()
    recv_a[slot_of(z, core), :] = send_a[block_of(z), :]
    to_sibling(recv_a, fa_send, a_recv, 0).start()

    table[...] = table_rows(gate_ref)

    def weigh(i):
        at = pl.ds(pl.multiple_of(i * 16, 16), 16)
        table[at, :] = table[at, :] * cot_ref[at, :].astype(F32)

    loop(tok_dev // 16, weigh)
    loop(width // 512, functools.partial(fill, send_b))
    recv_b[slot_of(z, core), :] = send_b[block_of(z), :]
    for s in range(SIDE):
        to_sibling(recv_b, fb_send, b_recv, 0, s).start()

    row = chosen_ref[pl.ds(z, 1), :]
    diagonal = iota((cap, cap), 0) == iota((cap, cap), 1)
    column = jnp.sum(jnp.where(diagonal, row.astype(F32), 0.0), axis=1, keepdims=True)
    row_f = row.astype(F32)
    owner_row = jnp.floor(row_f * (1.0 / tok_dev))
    owner_col = jnp.floor(column * (1.0 / tok_dev))
    ahead = jnp.where((owner_row == owner_col) & (row_f < column), 1.0, 0.0)
    place_in = jnp.sum(ahead, axis=1, keepdims=True)
    owner_z = jnp.floor(owner_col * 0.5)
    owner_c = owner_col - 2.0 * owner_z
    at_slot = (owner_c * nz + owner_z) * SLOT + place_in
    place_f = jnp.where(
        iota((cap, 2 * slots), 1).astype(F32) == at_slot, 1.0, 0.0
    )
    place[...] = place_f.astype(BF16)
    place_t[...] = place_f.T.astype(BF16)

    for j in hops:
        from_peer(recv_a, a_send, a_recv, j).wait_recv()
        to_sibling(recv_a, fa_send, a_recv, j).start()
        to_peer(send_a, recv_a, a_send, a_recv, j).wait_send()
        to_peer(send_b, recv_b, b_send, b_recv, j, 0).start()
    for s in range(1, SIDE):
        for j in hops:
            to_peer(send_b, recv_b, b_send, b_recv, j, s).start()
    for j in [0] + hops:
        from_sibling(recv_a, fa_send, a_recv, j).wait_recv()

    def gather_in(i):
        at = pl.ds(pl.multiple_of(i * 512, 512), 512)
        product = mm(place[...], recv_a[:, at], NN).astype(BF16)
        rows_in[:, at] = product
        for k in range(SIDE):
            columns_in[i, k] = product[:, k * 128 : (k + 1) * 128]

    loop(SIDE, gather_in)

    def along(axis, by):
        return lax.rem((gx if axis == 0 else gy) + by, SIDE)

    def line_copy(src, dst, k, axis, by):
        return pltpu.make_async_remote_copy(
            src_ref=src,
            dst_ref=dst,
            send_sem=l_send.at[k],
            recv_sem=l_recv.at[k],
            device_id=on_axis(axis, by),
            device_id_type=MESH,
        )

    row_copies = []
    for by in (2, 1, 3):
        row_copies.append(
            line_copy(columns_in.at[along(0, by)], line_rows.at[0, by - 1], by - 1, 0, by)
        )
        row_copies.append(
            line_copy(columns_in.at[:, along(1, by)], line_rows.at[1, by - 1], by + 2, 1, by)
        )
    for c in row_copies:
        c.start()
    for load in loads:
        load.wait()
    weight = combine_ref[pl.ds(z, 1), :]

    def forward(i):
        at = pl.ds(pl.multiple_of(i * rows_q, rows_q), rows_q)
        pre_gate = mm(wg[at, :], rows_in[...], NT)
        pre_up = mm(wu[at, :], rows_in[...], NT)
        sig = 1.0 / (1.0 + jnp.exp(-pre_gate))
        silu = pre_gate * sig
        hid = silu * pre_up
        hidden[at, :] = hid.astype(BF16)
        hidden_c[at, :] = (hid * weight).astype(BF16)
        up_f[at, :] = silu * weight
        gate_f[at, :] = pre_up * sig * (1.0 + pre_gate * (1.0 - sig)) * weight

    loop(4, forward)

    def down_grad(s):
        product = mm(hidden_c[...], rows_grad[:, quarter(s)], NN).astype(BF16)
        for k in range(SIDE):
            piece = product[:, k * 128 : (k + 1) * 128]
            grads[0, s * SIDE + k] = piece[:rows_h]
            grads[1, k * SIDE + s] = piece[rows_h:]
        ready = {0: ((0, 0), (0, 1)), 1: ((0, 2), (1, 0), (1, 3)), 2: ((0, 3),), 3: ((1, 1), (1, 2))}
        for h, k in ready[s]:
            rings[0, h][0][k].start()

    def line_grad(t, h):
        n = 2 * t + h
        mine = (d_gate, d_up)[t - 1]
        here = [columns_in[gx, k] if h == 0 else columns_in[k, gy] for k in range(SIDE)]
        total = mm(
            mine[h * rows_h : (h + 1) * rows_h, :], jnp.concatenate(here, axis=1), NN
        )
        for r in range(SIDE - 1):
            rows = jnp.concatenate([line_rows[h, r, k] for k in range(SIDE)], axis=1)
            total = total + mm(line_gate[t - 1, h, r], rows, NN)
        total = total.astype(BF16)
        for k in range(SIDE):
            parts[n, k] = total[:, k * 128 : (k + 1) * 128]

    def ring(t, h):
        n = 2 * t + h
        ia, ib = (gx, gy) if h == 0 else (gy, gx)
        own, other = h, 1 - h

        def copy(src, dst, k, axis, by):
            return pltpu.make_async_remote_copy(
                src_ref=src,
                dst_ref=dst,
                send_sem=r_send.at[n * 12 + k],
                recv_sem=r_recv.at[n * 12 + k],
                device_id=on_axis(axis, by),
                device_id_type=MESH,
            )

        def block(dest):
            return (ORDER.index(dest) if h == 0 else lax.rem(ia + dest, SIDE)) * SIDE

        def pair(dest, q):
            return pl.ds(block(dest) + 2 * q, 2)

        def sub(dest):
            return ORDER.index(dest) if t == 0 and h == 1 else lax.rem(ib + dest, SIDE)

        one, two = (1, SIDE - 1), SIDE // 2
        first_copies = []
        if t == 0:
            first_copies = [
                copy(grads.at[n, pair(two, 0)], far1.at[n, 0], 0, own, one[0]),
                copy(grads.at[n, pair(two, 1)], far1.at[n, 1], 1, own, one[1]),
                copy(grads.at[n, pair(1, 1)], near1.at[n, 0, pl.ds(2, 2)], 2, own, one[0]),
                copy(grads.at[n, pair(3, 0)], near1.at[n, 1, pl.ds(0, 2)], 3, own, one[1]),
                copy(grads.at[n, pair(1, 0)], near1.at[n, 0, pl.ds(0, 2)], 4, own, one[0]),
                copy(grads.at[n, pair(3, 1)], near1.at[n, 1, pl.ds(2, 2)], 5, own, one[1]),
            ]
        top, low = pl.ds(0, rows_q), pl.ds(rows_q, rows_q)
        next_copies = [
            copy(parts.at[n, sub(two), top], far2.at[n, 0], 6, other, one[0]),
            copy(parts.at[n, sub(two), low], far2.at[n, 1], 7, other, one[1]),
            copy(parts.at[n, sub(1), low], near2.at[n, 0, low], 8, other, one[0]),
            copy(parts.at[n, sub(3), top], near2.at[n, 1, top], 9, other, one[1]),
            copy(parts.at[n, sub(1), top], near2.at[n, 0, top], 10, other, one[0]),
            copy(parts.at[n, sub(3), low], near2.at[n, 1, low], 11, other, one[1]),
        ]

        def merge1():
            for side, dest in ((0, 1), (1, 3)):
                first_copies[side].wait_recv()
                base = block(dest) + 2 * side

                def add(i):
                    grads[n, base + i] = (
                        grads[n, base + i].astype(F32) + far1[n, side, i].astype(F32)
                    ).astype(BF16)

                loop(2, add)
                first_copies[4 + side].start()

        def start2():
            for c in next_copies[:4]:
                c.start()

        def finish1():
            for c in first_copies[2:]:
                c.wait_recv()
            base = block(0)

            def add(i):
                parts[n, i] = (
                    grads[n, base + i].astype(F32)
                    + near1[n, 0, i].astype(F32)
                    + near1[n, 1, i].astype(F32)
                ).astype(BF16)

            loop(SIDE, add)
            start2()

        def merge2():
            for side, dest, part in ((0, 1, top), (1, 3, low)):
                next_copies[side].wait_recv()
                parts[n, sub(dest), part] = (
                    parts[n, sub(dest), part].astype(F32) + far2[n, side].astype(F32)
                ).astype(BF16)
                next_copies[4 + side].start()

        def finish2(out):
            for c in next_copies[2:]:
                c.wait_recv()
            total = (
                parts[n, sub(0)].astype(F32)
                + near2[n, 0].astype(F32)
                + near2[n, 1].astype(F32)
            )
            out[h * rows_h : (h + 1) * rows_h, :] = (total * (1.0 / (SIDE * SIDE))).astype(BF16)

        def drain():
            for c in first_copies + next_copies:
                c.wait_send()

        return first_copies, merge1, finish1, merge2, finish2, drain, start2

    rings = {(t, h): ring(t, h) for t in range(3) for h in range(2)}

    def run(t, phase, *args):
        for h in range(2):
            rings[t, h][phase](*args)

    def raw_sum(s, i):
        at = pl.ds(pl.multiple_of(i * rows_q, rows_q), rows_q)
        product = mm(wd[at, quarter(s)], rows_grad[:, quarter(s)], NT)
        raw[at, :] = product if s == 0 else raw[at, :] + product

    for s in range(SIDE):
        for j in hops:
            from_peer(recv_b, b_send, b_recv, j, s).wait_recv()
            to_sibling(recv_b, fb_send, b_recv, j, s).start()
        for j in [0] + hops:
            from_sibling(recv_b, fb_send, b_recv, j, s).wait_recv()
        rows_grad[:, quarter(s)] = mm(place[...], recv_b[:, quarter(s)], NN).astype(BF16)
        loop(4, functools.partial(raw_sum, s))
        if s < SIDE - 1:
            down_grad(s)

    def backward(i):
        at = pl.ds(i * rows_q, rows_q)
        value = raw[at, :]
        d_gate[at, :] = (value * gate_f[at, :]).astype(BF16)
        d_up[at, :] = (value * up_f[at, :]).astype(BF16)
        return jnp.sum(hidden[at, :].astype(F32) * value, axis=0, keepdims=True)

    inner = backward(0)
    for i in range(1, 4):
        inner = inner + backward(i)
    gate_copies = []
    for t, grad in ((1, d_gate), (2, d_up)):
        for by in (2, 1, 3):
            for h in range(2):
                gate_copies.append(
                    line_copy(
                        grad.at[pl.ds(h * rows_h, rows_h)],
                        line_gate.at[t - 1, h, by - 1],
                        6 * t + 3 * h + by - 1,
                        h,
                        by,
                    )
                )
    for c in gate_copies:
        c.start()
    left, right = inner[:, : cap // 2], inner[:, cap // 2 :]
    mine = jnp.where(core == 0, left, right)
    theirs = jnp.where(core == 0, right, left)
    inner_s[...] = jnp.broadcast_to(theirs, inner_s.shape)
    inner_copy = pltpu.make_async_remote_copy(
        src_ref=inner_s,
        dst_ref=inner_r,
        send_sem=s_send.at[0],
        recv_sem=s_recv.at[0],
        device_id=on_sib,
        device_id_type=MESH,
    )
    inner_copy.start()
    d_gate_t[...] = d_gate[...].astype(F32).T.astype(BF16)
    d_up_t[...] = d_up[...].astype(F32).T.astype(BF16)

    chunk = width // CHUNKS
    own_rows = pl.ds(pl.multiple_of(core * slots, slots), slots)
    their_rows = pl.ds(pl.multiple_of((1 - core) * slots, slots), slots)

    def columns(i):
        return pl.ds(i * chunk, chunk)

    sib_copies = [
        pltpu.make_async_remote_copy(
            src_ref=back.at[their_rows, columns(i)],
            dst_ref=sib.at[:, columns(i)],
            send_sem=s_send.at[1 + i],
            recv_sem=s_recv.at[1 + i],
            device_id=on_sib,
            device_id_type=MESH,
        )
        for i in range(CHUNKS)
    ]

    def to_owner(j, i):
        zz = peer(j)
        return pltpu.make_async_remote_copy(
            src_ref=send_c.at[block_of(zz), columns(i)],
            dst_ref=ret.at[block_of(z), columns(i)],
            send_sem=c_send.at[j * CHUNKS + i],
            recv_sem=c_recv.at[j * CHUNKS + i],
            device_id=on_z(zz),
            device_id_type=MESH,
        )

    def from_expert(j, i):
        zz = peer(nz - j)
        return pltpu.make_async_remote_copy(
            src_ref=ret.at[block_of(zz), columns(i)],
            dst_ref=ret.at[block_of(zz), columns(i)],
            send_sem=c_send.at[j * CHUNKS + i],
            recv_sem=c_recv.at[j * CHUNKS + i],
            device_id=on_z(peer(j)),
            device_id_type=MESH,
        )

    def input_grad(i):
        at = columns(i)
        total = mm(d_gate_t[...], wg[:, at], NN) + mm(d_up_t[...], wu[:, at], NN)
        back[:, at] = mm(place_t[...], total.astype(BF16), NN).astype(BF16)
        sib_copies[i].start()

    def send_home(i):
        at = columns(i)
        sib_copies[i].wait_recv()
        send_c[:, at] = (back[own_rows, at].astype(F32) + sib[:, at].astype(F32)).astype(BF16)
        for j in hops:
            to_owner(j, i).start()
        ret[block_of(z), at] = send_c[block_of(z), at]

    for i in range(CHUNKS):
        input_grad(i)
        if i:
            send_home(i - 1)
    down_grad(SIDE - 1)
    send_home(CHUNKS - 1)
    inner_copy.wait_recv()
    dcomb_ref[...] = mine + inner_r[0:1, :]
    for c in row_copies:
        c.wait_recv()
    run(0, 1)
    for t in (1, 2):
        for c in gate_copies[6 * (t - 1) : 6 * t]:
            c.wait_recv()
        for h in range(2):
            line_grad(t, h)
            rings[t, h][6]()
    run(0, 2)
    run(1, 3)
    run(2, 3)
    run(0, 3)
    for j in hops:
        for i in range(CHUNKS):
            from_expert(j, i).wait_recv()

    def spread_back(i):
        at = pl.ds(pl.multiple_of(i * 512, 512), 512)
        table[:, at] = mm(pick_t[...], ret[:, at], NN)

    loop(width // 512, spread_back)

    def token_grad(i):
        at = pl.ds(pl.multiple_of(i * 16, 16), 16)
        norm = normed[at, :]
        d_norm = table[at, :] * scale1[at, :]
        centre = jnp.mean(d_norm, axis=1, keepdims=True)
        along = jnp.mean(d_norm * norm, axis=1, keepdims=True)
        dtok_ref[at, :] = (inverse[at, :] * (d_norm - centre - norm * along)).astype(BF16)

    loop(tok_dev // 16, token_grad)
    run(1, 4, dwg_ref)
    run(2, 4, dwu_ref)
    run(0, 4, dwd_ref)

    for j in hops:
        for s in range(SIDE):
            to_peer(send_b, recv_b, b_send, b_recv, j, s).wait_send()
        for i in range(CHUNKS):
            to_owner(j, i).wait_send()
    for j in [0] + hops:
        to_sibling(recv_a, fa_send, a_recv, j).wait_send()
        for s in range(SIDE):
            to_sibling(recv_b, fb_send, b_recv, j, s).wait_send()
    for c in row_copies + gate_copies:
        c.wait_send()
    inner_copy.wait_send()
    for c in sib_copies:
        c.wait_send()
    for t in range(3):
        run(t, 5)


def copy_kernel(*refs):
    count = len(refs) // 2
    for i in range(count):
        refs[count + i][...] = refs[i][...]


def solution(mesh):
    nz = mesh.shape["exp"] // 2

    def on_device(
        tokens, cotangent, timestep, shift_table, scale_table, gate_table, chosen, combine, w_gate, w_up, w_down
    ):
        tok_dev, width = tokens.shape
        half = w_gate.shape[1]
        cap = chosen.shape[2]
        slots = nz * SLOT
        rows_h, rows_q = half // 2, half // 4
        vmem = pl.BlockSpec(memory_space=pltpu.VMEM)
        hbm = pl.BlockSpec(memory_space=pl.ANY)
        dma = pltpu.SemaphoreType.DMA
        outs = pl.pallas_call(
            functools.partial(layer_kernel, nz),
            out_shape=(
                jax.ShapeDtypeStruct((tok_dev, width), BF16),
                jax.ShapeDtypeStruct((1, cap // 2), F32),
                jax.ShapeDtypeStruct((half, 128), BF16),
                jax.ShapeDtypeStruct((half, 128), BF16),
                jax.ShapeDtypeStruct((half, 128), BF16),
            ),
            in_specs=[vmem] * 8 + [hbm] * 3,
            out_specs=(vmem,) * 5,
            scratch_shapes=[
                pltpu.VMEM((half, width), BF16),
                pltpu.VMEM((half, width), BF16),
                pltpu.VMEM((half, width), BF16),
                pltpu.VMEM((slots, width), BF16),
                pltpu.VMEM((slots, width), BF16),
                pltpu.VMEM((2 * slots, width), BF16),
                pltpu.VMEM((2 * slots, width), BF16),
                pltpu.VMEM((cap, width), BF16),
                pltpu.VMEM((cap, width), BF16),
                pltpu.VMEM((tok_dev, width), F32),
                pltpu.VMEM((tok_dev, width), F32),
                pltpu.VMEM((tok_dev, width), F32),
                pltpu.VMEM((tok_dev, 1), F32),
                pltpu.VMEM((slots, tok_dev), BF16),
                pltpu.VMEM((tok_dev, slots), BF16),
                pltpu.VMEM((cap, 2 * slots), BF16),
                pltpu.VMEM((2 * slots, cap), BF16),
                pltpu.VMEM((half, cap), BF16),
                pltpu.VMEM((half, cap), BF16),
                pltpu.VMEM((half, cap), F32),
                pltpu.VMEM((half, cap), F32),
                pltpu.VMEM((half, cap), F32),
                pltpu.VMEM((half, cap), BF16),
                pltpu.VMEM((half, cap), BF16),
                pltpu.VMEM((cap, half), BF16),
                pltpu.VMEM((cap, half), BF16),

                pltpu.VMEM((2 * slots, width), BF16),
                pltpu.VMEM((slots, width), BF16),
                pltpu.VMEM((slots, width), BF16),
                pltpu.VMEM((slots, width), BF16),
                pltpu.VMEM((8, cap // 2), F32),
                pltpu.VMEM((8, cap // 2), F32),
                pltpu.VMEM((SIDE, SIDE, cap, 128), BF16),
                pltpu.VMEM((2, SIDE - 1, SIDE, cap, 128), BF16),
                pltpu.VMEM((2, 2, SIDE - 1, rows_h, cap), BF16),
                pltpu.VMEM((2, SIDE * SIDE, rows_h, 128), BF16),
                pltpu.VMEM((6, SIDE, rows_h, 128), BF16),
                pltpu.VMEM((2, 2, 2, rows_h, 128), BF16),
                pltpu.VMEM((2, 2, SIDE, rows_h, 128), BF16),
                pltpu.VMEM((6, 2, rows_q, 128), BF16),
                pltpu.VMEM((6, 2, rows_h, 128), BF16),
                dma((3,)),
                dma((nz,)),
                dma((2 * nz,)),
                dma((nz * SIDE,)),
                dma((2 * nz * SIDE,)),
                dma((nz,)),
                dma((nz * SIDE,)),
                dma((nz * CHUNKS,)),
                dma((nz * CHUNKS,)),
                dma((1 + CHUNKS,)),
                dma((1 + CHUNKS,)),
                dma((72,)),
                dma((72,)),
                dma((18,)),
                dma((18,)),
            ],
            compiler_params=pltpu.CompilerParams(
                collective_id=0, has_side_effects=True, vmem_limit_bytes=60 * 1024 * 1024
            ),
        )(
            tokens,
            cotangent,
            timestep[None, :],
            shift_table,
            scale_table,
            gate_table,
            chosen[0],
            combine[0],
            w_gate[0],
            w_up[0],
            w_down[0],
        )
        outs = pl.pallas_call(
            copy_kernel,
            out_shape=tuple(jax.ShapeDtypeStruct(o.shape, o.dtype) for o in outs),
            in_specs=[vmem] * 5,
            out_specs=(vmem,) * 5,
        )(*outs)
        d_tokens, d_combine, d_gate, d_up, d_down = outs
        return d_tokens, d_combine[None], d_gate[None], d_up[None], d_down[None]

    in_specs = (
        P(("grp", "exp"), None),
        P(("grp", "exp"), None),
        P(("grp", "exp")),
        P(),
        P(),
        P(),
        P("grp", None, None),
        P("grp", None, None),
        P("exp", None, None),
        P("exp", None, None),
        P("exp", None, None),
    )
    out_specs = (
        P(("grp", "exp"), None),
        P("grp", "exp", None),
        P("exp", None, "grp"),
        P("exp", None, "grp"),
        P("exp", None, "grp"),
    )
    return jax.shard_map(
        on_device, mesh=mesh, in_specs=in_specs, out_specs=out_specs, check_vma=False
    )
```

```python
import functools

import jax
import jax.numpy as jnp
from jax import lax
from jax.experimental import pallas as pl
from jax.experimental.pallas import tpu as pltpu
from jax.sharding import PartitionSpec as P

EPSILON = 1e-06
MESH = pl.DeviceIdType.MESH
F32 = jnp.float32
BF16 = jnp.bfloat16
SLOT = 32
SIDE = 4
CHUNKS = 2
ORDER = (2, 1, 3, 0)
NN = (((1,), (0,)), ((), ()))
NT = (((1,), (1,)), ((), ()))
TN = (((0,), (0,)), ((), ()))


def mm(a, b, dims):
    return lax.dot_general(a, b, dims, preferred_element_type=F32)


def iota(shape, axis):
    return lax.broadcasted_iota(jnp.int32, shape, axis)


def loop(count, body):
    def step(i, carry):
        body(i)
        return carry

    lax.fori_loop(0, count, step, 0)


def layer_kernel(
    nz,
    tok_ref,
    cot_ref,
    step_ref,
    shift_ref,
    scale_ref,
    gate_ref,
    chosen_ref,
    combine_ref,
    wg_hbm,
    wu_hbm,
    wd_hbm,
    dtok_ref,
    dcomb_ref,
    dwg_ref,
    dwu_ref,
    dwd_ref,
    wg,
    wu,
    wd,
    send_a,
    send_b,
    recv_a,
    recv_b,
    rows_in,
    rows_grad,
    normed,
    scale1,
    table,
    inverse,
    pick,
    pick_t,
    place,
    place_t,
    hidden,
    hidden_c,
    gate_f,
    up_f,
    raw,
    d_gate,
    d_up,
    d_gate_t,
    d_up_t,
    back,
    sib,
    send_c,
    ret,
    inner_s,
    inner_r,
    columns_in,
    line_rows,
    line_gate,
    line_sum,
    grads,
    parts,
    far1,
    near1,
    far2,
    near2,
    w_sem,
    a_send,
    a_recv,
    b_send,
    b_recv,
    fa_send,
    fb_send,
    c_send,
    c_recv,
    s_send,
    s_recv,
    r_send,
    r_recv,
    l_send,
    l_recv,
):
    tok_dev, width = tok_ref.shape
    half = wg.shape[0]
    cap = rows_in.shape[0]
    rows_h = half // 2
    rows_q = half // 4
    g = lax.axis_index("grp")
    me = lax.axis_index("exp")
    z = lax.div(me, 2)
    core = lax.rem(me, 2)
    gx = lax.div(g, SIDE)
    gy = lax.rem(g, SIDE)
    sibling = z * 2 + (1 - core)

    def peer(j):
        return lax.rem(z + j, nz)

    def on_z(zz):
        return {"grp": g, "exp": zz * 2 + core}

    on_sib = {"grp": g, "exp": sibling}

    def on_axis(axis, by):
        if axis == 0:
            return {"grp": lax.rem(gx + by, SIDE) * SIDE + gy, "exp": me}
        return {"grp": gx * SIDE + lax.rem(gy + by, SIDE), "exp": me}

    hops = [1, 7, 2, 6, 3, 5, 4] if nz == 8 else list(range(1, nz))

    loads = [
        pltpu.make_async_copy(src, dst, w_sem.at[i])
        for i, (src, dst) in enumerate(((wg_hbm, wg), (wu_hbm, wu), (wd_hbm, wd)))
    ]
    for load in loads:
        load.start()
    barrier = pltpu.get_barrier_semaphore()
    partners = [on_z(peer(j)) for j in hops] + [on_sib]
    partners += [on_axis(axis, by) for axis in (0, 1) for by in (1, 2, 3)]
    for partner in partners:
        pl.semaphore_signal(barrier, inc=1, device_id=partner, device_id_type=MESH)

    first = me * tok_dev
    ids = iota((tok_dev, cap), 0) + first
    lane_e = iota((tok_dev, nz), 1)
    mask = jnp.zeros((tok_dev, nz), F32)
    for e in range(nz):
        hit = jnp.sum(
            jnp.where(ids == chosen_ref[e : e + 1, :], 1.0, 0.0), axis=1, keepdims=True
        )
        mask = jnp.where(lane_e == e, hit, mask)
    earlier = (iota((tok_dev, tok_dev), 1) < iota((tok_dev, tok_dev), 0)).astype(F32)
    rank = mm(earlier.astype(BF16), mask.astype(BF16), NN)
    slots = nz * SLOT
    spread = (lax.div(iota((nz, slots), 1), SLOT) == iota((nz, slots), 0)).astype(F32).astype(BF16)
    rank_p = mm(rank.astype(BF16), spread, NN)
    mask_p = mm(mask.astype(BF16), spread, NN)
    want = lax.rem(iota((tok_dev, slots), 1), SLOT).astype(F32)
    pick_f = jnp.where((rank_p == want) & (mask_p > 0.5), 1.0, 0.0)
    pick_t[...] = pick_f.astype(BF16)
    pick[...] = pick_f.T.astype(BF16)

    steps3 = 3 * scale_ref.shape[0]
    onehot = (lax.rem(iota((steps3, tok_dev), 0), scale_ref.shape[0]) == step_ref[...]).astype(F32)
    onehot = onehot.T.astype(BF16)

    def table_rows(ref):
        whole = ref[...]
        hi = whole.astype(BF16)
        rest = whole - hi.astype(F32)
        mid = rest.astype(BF16)
        low = (rest - mid.astype(F32)).astype(BF16)
        return mm(onehot, jnp.concatenate([hi, mid, low], axis=0), NN)

    scale1[...] = 1.0 + table_rows(scale_ref)
    table[...] = table_rows(shift_ref)

    def normalise(i):
        at = pl.ds(pl.multiple_of(i * 16, 16), 16)
        values = tok_ref[at, :].astype(F32)
        centred = values - jnp.mean(values, axis=1, keepdims=True)
        inv = lax.rsqrt(jnp.mean(centred * centred, axis=1, keepdims=True) + EPSILON)
        inverse[at, :] = inv
        norm = centred * inv
        normed[at, :] = norm
        table[at, :] = norm * scale1[at, :] + table[at, :]

    loop(tok_dev // 16, normalise)

    def fill(dst, i):
        at = pl.ds(pl.multiple_of(i * 512, 512), 512)
        dst[:, at] = mm(pick[...], table[:, at].astype(BF16), NN).astype(BF16)

    def slot_of(zz, cc):
        return pl.ds(pl.multiple_of((cc * nz + zz) * SLOT, SLOT), SLOT)

    def block_of(zz):
        return pl.ds(pl.multiple_of(zz * SLOT, SLOT), SLOT)

    def quarter(s):
        at = lax.rem(gx + ORDER[s], SIDE) * (width // SIDE)
        return pl.ds(pl.multiple_of(at, width // SIDE), width // SIDE)

    def part(ref, rows, s):
        return ref.at[rows] if s is None else ref.at[rows, quarter(s)]

    def sem(j, s):
        return j if s is None else j * SIDE + s

    def to_peer(src, dst, s_sem, r_sem, j, s=None):
        zz = peer(j)
        return pltpu.make_async_remote_copy(
            src_ref=part(src, block_of(zz), s),
            dst_ref=part(dst, slot_of(z, core), s),
            send_sem=s_sem.at[sem(j, s)],
            recv_sem=r_sem.at[sem(j, s)],
            device_id=on_z(zz),
            device_id_type=MESH,
        )

    def from_peer(dst, s_sem, r_sem, j, s=None):
        zz = peer(nz - j)
        return pltpu.make_async_remote_copy(
            src_ref=part(dst, slot_of(zz, core), s),
            dst_ref=part(dst, slot_of(zz, core), s),
            send_sem=s_sem.at[sem(j, s)],
            recv_sem=r_sem.at[sem(j, s)],
            device_id=on_z(peer(j)),
            device_id_type=MESH,
        )

    def to_sibling(dst, s_sem, r_sem, j, s=None):
        zz = peer(nz - j)
        return pltpu.make_async_remote_copy(
            src_ref=part(dst, slot_of(zz, core), s),
            dst_ref=part(dst, slot_of(zz, core), s),
            send_sem=s_sem.at[sem(j, s)],
            recv_sem=r_sem.at[sem(nz + j, s)],
            device_id=on_sib,
            device_id_type=MESH,
        )

    def from_sibling(dst, s_sem, r_sem, j, s=None):
        zz = peer(nz - j)
        return pltpu.make_async_remote_copy(
            src_ref=part(dst, slot_of(zz, 1 - core), s),
            dst_ref=part(dst, slot_of(zz, 1 - core), s),
            send_sem=s_sem.at[sem(j, s)],
            recv_sem=r_sem.at[sem(nz + j, s)],
            device_id=on_sib,
            device_id_type=MESH,
        )

    loop(width // 512, functools.partial(fill, send_a))
    pl.semaphore_wait(barrier, len(partners))
    for j in hops:
        to_peer(send_a, recv_a, a_send, a_recv, j).start()
    recv_a[slot_of(z, core), :] = send_a[block_of(z), :]
    to_sibling(recv_a, fa_send, a_recv, 0).start()

    table[...] = table_rows(gate_ref)

    def weigh(i):
        at = pl.ds(pl.multiple_of(i * 16, 16), 16)
        table[at, :] = table[at, :] * cot_ref[at, :].astype(F32)

    loop(tok_dev // 16, weigh)
    loop(width // 512, functools.partial(fill, send_b))
    recv_b[slot_of(z, core), :] = send_b[block_of(z), :]
    for s in range(SIDE):
        to_sibling(recv_b, fb_send, b_recv, 0, s).start()

    row = chosen_ref[pl.ds(z, 1), :]
    diagonal = iota((cap, cap), 0) == iota((cap, cap), 1)
    column = jnp.sum(jnp.where(diagonal, row.astype(F32), 0.0), axis=1, keepdims=True)
    row_f = row.astype(F32)
    owner_row = jnp.floor(row_f * (1.0 / tok_dev))
    owner_col = jnp.floor(column * (1.0 / tok_dev))
    ahead = jnp.where((owner_row == owner_col) & (row_f < column), 1.0, 0.0)
    place_in = jnp.sum(ahead, axis=1, keepdims=True)
    owner_z = jnp.floor(owner_col * 0.5)
    owner_c = owner_col - 2.0 * owner_z
    at_slot = (owner_c * nz + owner_z) * SLOT + place_in
    place_f = jnp.where(
        iota((cap, 2 * slots), 1).astype(F32) == at_slot, 1.0, 0.0
    )
    place[...] = place_f.astype(BF16)
    place_t[...] = place_f.T.astype(BF16)

    for j in hops:
        from_peer(recv_a, a_send, a_recv, j).wait_recv()
        to_sibling(recv_a, fa_send, a_recv, j).start()
        to_peer(send_a, recv_a, a_send, a_recv, j).wait_send()
        to_peer(send_b, recv_b, b_send, b_recv, j, 0).start()
    for s in range(1, SIDE):
        for j in hops:
            to_peer(send_b, recv_b, b_send, b_recv, j, s).start()
    for j in [0] + hops:
        from_sibling(recv_a, fa_send, a_recv, j).wait_recv()

    def gather_in(i):
        at = pl.ds(pl.multiple_of(i * 512, 512), 512)
        product = mm(place[...], recv_a[:, at], NN).astype(BF16)
        rows_in[:, at] = product
        for k in range(SIDE):
            columns_in[i, k] = product[:, k * 128 : (k + 1) * 128]

    loop(SIDE, gather_in)

    def along(axis, by):
        return lax.rem((gx if axis == 0 else gy) + by, SIDE)

    def line_copy(src, dst, k, axis, by):
        return pltpu.make_async_remote_copy(
            src_ref=src,
            dst_ref=dst,
            send_sem=l_send.at[k],
            recv_sem=l_recv.at[k],
            device_id=on_axis(axis, by),
            device_id_type=MESH,
        )

    row_copies = []
    for by in (2, 1, 3):
        row_copies.append(
            line_copy(columns_in.at[along(0, by)], line_rows.at[0, by - 1], by - 1, 0, by)
        )
        row_copies.append(
            line_copy(columns_in.at[:, along(1, by)], line_rows.at[1, by - 1], by + 2, 1, by)
        )
    for c in row_copies:
        c.start()
    for load in loads:
        load.wait()
    weight = combine_ref[pl.ds(z, 1), :]

    def forward(i):
        at = pl.ds(pl.multiple_of(i * rows_q, rows_q), rows_q)
        pre_gate = mm(wg[at, :], rows_in[...], NT)
        pre_up = mm(wu[at, :], rows_in[...], NT)
        sig = 1.0 / (1.0 + jnp.exp(-pre_gate))
        silu = pre_gate * sig
        hid = silu * pre_up
        hidden[at, :] = hid.astype(BF16)
        hidden_c[at, :] = (hid * weight).astype(BF16)
        up_f[at, :] = silu * weight
        gate_f[at, :] = pre_up * sig * (1.0 + pre_gate * (1.0 - sig)) * weight

    loop(4, forward)

    def down_grad(s):
        product = mm(hidden_c[...], rows_grad[:, quarter(s)], NN).astype(BF16)
        for k in range(SIDE):
            piece = product[:, k * 128 : (k + 1) * 128]
            grads[0, s * SIDE + k] = piece[:rows_h]
            grads[1, k * SIDE + s] = piece[rows_h:]
        ready = {0: ((0, 0), (0, 1)), 1: ((0, 2), (1, 0), (1, 3)), 2: ((0, 3),), 3: ((1, 1), (1, 2))}
        for h, k in ready[s]:
            rings[0, h][0][k].start()

    def line_rows_of(h, r):
        return jnp.concatenate([line_rows[h, r, k] for k in range(SIDE)], axis=1)

    def line_near(t, h):
        grad = (d_gate, d_up)[t - 1]
        here = [columns_in[gx, k] if h == 0 else columns_in[k, gy] for k in range(SIDE)]
        total = mm(
            grad[h * rows_h : (h + 1) * rows_h, :], jnp.concatenate(here, axis=1), NN
        )
        for r in (0, 2):
            total = total + mm(line_gate[t - 1, h, r], line_rows_of(h, r), NN)
        line_sum[t - 1, h] = total

    def line_far(t, h):
        total = line_sum[t - 1, h] + mm(line_gate[t - 1, h, 1], line_rows_of(h, 1), NN)
        total = total.astype(BF16)
        for k in range(SIDE):
            parts[2 * t + h, k] = total[:, k * 128 : (k + 1) * 128]

    def ring(t, h):
        n = 2 * t + h
        ia, ib = (gx, gy) if h == 0 else (gy, gx)
        own, other = h, 1 - h

        def copy(src, dst, k, axis, by):
            return pltpu.make_async_remote_copy(
                src_ref=src,
                dst_ref=dst,
                send_sem=r_send.at[n * 12 + k],
                recv_sem=r_recv.at[n * 12 + k],
                device_id=on_axis(axis, by),
                device_id_type=MESH,
            )

        def block(dest):
            return (ORDER.index(dest) if h == 0 else lax.rem(ia + dest, SIDE)) * SIDE

        def pair(dest, q):
            return pl.ds(block(dest) + 2 * q, 2)

        def sub(dest):
            return ORDER.index(dest) if t == 0 and h == 1 else lax.rem(ib + dest, SIDE)

        one, two = (1, SIDE - 1), SIDE // 2
        first_copies = []
        if t == 0:
            first_copies = [
                copy(grads.at[n, pair(two, 0)], far1.at[n, 0], 0, own, one[0]),
                copy(grads.at[n, pair(two, 1)], far1.at[n, 1], 1, own, one[1]),
                copy(grads.at[n, pair(1, 1)], near1.at[n, 0, pl.ds(2, 2)], 2, own, one[0]),
                copy(grads.at[n, pair(3, 0)], near1.at[n, 1, pl.ds(0, 2)], 3, own, one[1]),
                copy(grads.at[n, pair(1, 0)], near1.at[n, 0, pl.ds(0, 2)], 4, own, one[0]),
                copy(grads.at[n, pair(3, 1)], near1.at[n, 1, pl.ds(2, 2)], 5, own, one[1]),
            ]
        top, low = pl.ds(0, rows_q), pl.ds(rows_q, rows_q)
        next_copies = [
            copy(parts.at[n, sub(two), top], far2.at[n, 0], 6, other, one[0]),
            copy(parts.at[n, sub(two), low], far2.at[n, 1], 7, other, one[1]),
            copy(parts.at[n, sub(1), low], near2.at[n, 0, low], 8, other, one[0]),
            copy(parts.at[n, sub(3), top], near2.at[n, 1, top], 9, other, one[1]),
            copy(parts.at[n, sub(1), top], near2.at[n, 0, top], 10, other, one[0]),
            copy(parts.at[n, sub(3), low], near2.at[n, 1, low], 11, other, one[1]),
        ]

        def merge1():
            for side, dest in ((0, 1), (1, 3)):
                first_copies[side].wait_recv()
                base = block(dest) + 2 * side

                def add(i):
                    grads[n, base + i] = (
                        grads[n, base + i].astype(F32) + far1[n, side, i].astype(F32)
                    ).astype(BF16)

                loop(2, add)
                first_copies[4 + side].start()

        def start2():
            for c in next_copies[:4]:
                c.start()

        def finish1():
            for c in first_copies[2:]:
                c.wait_recv()
            base = block(0)

            def add(i):
                parts[n, i] = (
                    grads[n, base + i].astype(F32)
                    + near1[n, 0, i].astype(F32)
                    + near1[n, 1, i].astype(F32)
                ).astype(BF16)

            loop(SIDE, add)
            start2()

        def merge2():
            for side, dest, part in ((0, 1, top), (1, 3, low)):
                next_copies[side].wait_recv()
                parts[n, sub(dest), part] = (
                    parts[n, sub(dest), part].astype(F32) + far2[n, side].astype(F32)
                ).astype(BF16)
                next_copies[4 + side].start()

        def finish2(out):
            for c in next_copies[2:]:
                c.wait_recv()
            total = (
                parts[n, sub(0)].astype(F32)
                + near2[n, 0].astype(F32)
                + near2[n, 1].astype(F32)
            )
            out[h * rows_h : (h + 1) * rows_h, :] = (total * (1.0 / (SIDE * SIDE))).astype(BF16)

        def drain():
            for c in first_copies + next_copies:
                c.wait_send()

        return first_copies, merge1, finish1, merge2, finish2, drain, start2

    rings = {(t, h): ring(t, h) for t in range(3) for h in range(2)}

    def run(t, phase, *args):
        for h in range(2):
            rings[t, h][phase](*args)

    def raw_sum(s, i):
        at = pl.ds(pl.multiple_of(i * rows_q, rows_q), rows_q)
        product = mm(wd[at, quarter(s)], rows_grad[:, quarter(s)], NT)
        raw[at, :] = product if s == 0 else raw[at, :] + product

    for s in range(SIDE):
        for j in hops:
            from_peer(recv_b, b_send, b_recv, j, s).wait_recv()
            to_sibling(recv_b, fb_send, b_recv, j, s).start()
        for j in [0] + hops:
            from_sibling(recv_b, fb_send, b_recv, j, s).wait_recv()
        rows_grad[:, quarter(s)] = mm(place[...], recv_b[:, quarter(s)], NN).astype(BF16)
        loop(4, functools.partial(raw_sum, s))
        if s < SIDE - 1:
            down_grad(s)

    def backward(i):
        at = pl.ds(i * rows_q, rows_q)
        value = raw[at, :]
        d_gate[at, :] = (value * gate_f[at, :]).astype(BF16)
        d_up[at, :] = (value * up_f[at, :]).astype(BF16)
        return jnp.sum(hidden[at, :].astype(F32) * value, axis=0, keepdims=True)

    inner = backward(0)
    for i in range(1, 4):
        inner = inner + backward(i)
    gate_copies, forwards = {}, {}
    for t, grad in ((1, d_gate), (2, d_up)):
        for h in range(2):
            for side, by in ((0, 1), (1, 3)):
                gate_copies[t, h, side] = line_copy(
                    grad.at[pl.ds(h * rows_h, rows_h)],
                    line_gate.at[t - 1, h, by - 1],
                    8 * t + 4 * h + side,
                    h,
                    by,
                )
                piece = pl.ds(side * rows_q, rows_q)
                forwards[t, h, side] = line_copy(
                    line_gate.at[t - 1, h, by - 1, piece],
                    line_gate.at[t - 1, h, 1, piece],
                    8 * t + 4 * h + 2 + side,
                    h,
                    by,
                )
    for c in gate_copies.values():
        c.start()
    left, right = inner[:, : cap // 2], inner[:, cap // 2 :]
    mine = jnp.where(core == 0, left, right)
    theirs = jnp.where(core == 0, right, left)
    inner_s[...] = jnp.broadcast_to(theirs, inner_s.shape)
    inner_copy = pltpu.make_async_remote_copy(
        src_ref=inner_s,
        dst_ref=inner_r,
        send_sem=s_send.at[0],
        recv_sem=s_recv.at[0],
        device_id=on_sib,
        device_id_type=MESH,
    )
    inner_copy.start()
    d_gate_t[...] = d_gate[...].astype(F32).T.astype(BF16)
    d_up_t[...] = d_up[...].astype(F32).T.astype(BF16)

    chunk = width // CHUNKS
    own_rows = pl.ds(pl.multiple_of(core * slots, slots), slots)
    their_rows = pl.ds(pl.multiple_of((1 - core) * slots, slots), slots)

    def columns(i):
        return pl.ds(i * chunk, chunk)

    sib_copies = [
        pltpu.make_async_remote_copy(
            src_ref=back.at[their_rows, columns(i)],
            dst_ref=sib.at[:, columns(i)],
            send_sem=s_send.at[1 + i],
            recv_sem=s_recv.at[1 + i],
            device_id=on_sib,
            device_id_type=MESH,
        )
        for i in range(CHUNKS)
    ]

    def to_owner(j, i):
        zz = peer(j)
        return pltpu.make_async_remote_copy(
            src_ref=send_c.at[block_of(zz), columns(i)],
            dst_ref=ret.at[block_of(z), columns(i)],
            send_sem=c_send.at[j * CHUNKS + i],
            recv_sem=c_recv.at[j * CHUNKS + i],
            device_id=on_z(zz),
            device_id_type=MESH,
        )

    def from_expert(j, i):
        zz = peer(nz - j)
        return pltpu.make_async_remote_copy(
            src_ref=ret.at[block_of(zz), columns(i)],
            dst_ref=ret.at[block_of(zz), columns(i)],
            send_sem=c_send.at[j * CHUNKS + i],
            recv_sem=c_recv.at[j * CHUNKS + i],
            device_id=on_z(peer(j)),
            device_id_type=MESH,
        )

    def input_grad(i):
        at = columns(i)
        total = mm(d_gate_t[...], wg[:, at], NN) + mm(d_up_t[...], wu[:, at], NN)
        back[:, at] = mm(place_t[...], total.astype(BF16), NN).astype(BF16)
        sib_copies[i].start()

    def send_home(i):
        at = columns(i)
        sib_copies[i].wait_recv()
        send_c[:, at] = (back[own_rows, at].astype(F32) + sib[:, at].astype(F32)).astype(BF16)
        for j in hops:
            to_owner(j, i).start()
        ret[block_of(z), at] = send_c[block_of(z), at]

    for i in range(CHUNKS):
        input_grad(i)
        if i:
            send_home(i - 1)
    down_grad(SIDE - 1)
    send_home(CHUNKS - 1)
    for key, c in gate_copies.items():
        c.wait_recv()
        forwards[key].start()
    run(0, 1)
    for c in row_copies:
        c.wait_recv()
    for t in (1, 2):
        for h in range(2):
            line_near(t, h)
    inner_copy.wait_recv()
    dcomb_ref[...] = mine + inner_r[0:1, :]
    for t in (1, 2):
        for h in range(2):
            for side in range(2):
                forwards[t, h, side].wait_recv()
            line_far(t, h)
            rings[t, h][6]()
    run(0, 2)
    run(1, 3)
    run(2, 3)
    run(0, 3)
    for j in hops:
        for i in range(CHUNKS):
            from_expert(j, i).wait_recv()

    def spread_back(i):
        at = pl.ds(pl.multiple_of(i * 512, 512), 512)
        table[:, at] = mm(pick_t[...], ret[:, at], NN)

    loop(width // 512, spread_back)

    def token_grad(i):
        at = pl.ds(pl.multiple_of(i * 16, 16), 16)
        norm = normed[at, :]
        d_norm = table[at, :] * scale1[at, :]
        centre = jnp.mean(d_norm, axis=1, keepdims=True)
        along = jnp.mean(d_norm * norm, axis=1, keepdims=True)
        dtok_ref[at, :] = (inverse[at, :] * (d_norm - centre - norm * along)).astype(BF16)

    loop(tok_dev // 16, token_grad)
    run(1, 4, dwg_ref)
    run(2, 4, dwu_ref)
    run(0, 4, dwd_ref)

    for j in hops:
        for s in range(SIDE):
            to_peer(send_b, recv_b, b_send, b_recv, j, s).wait_send()
        for i in range(CHUNKS):
            to_owner(j, i).wait_send()
    for j in [0] + hops:
        to_sibling(recv_a, fa_send, a_recv, j).wait_send()
        for s in range(SIDE):
            to_sibling(recv_b, fb_send, b_recv, j, s).wait_send()
    for c in [*row_copies, *gate_copies.values(), *forwards.values()]:
        c.wait_send()
    inner_copy.wait_send()
    for c in sib_copies:
        c.wait_send()
    for t in range(3):
        run(t, 5)


def copy_kernel(*refs):
    count = len(refs) // 2
    for i in range(count):
        refs[count + i][...] = refs[i][...]


def solution(mesh):
    nz = mesh.shape["exp"] // 2

    def on_device(
        tokens, cotangent, timestep, shift_table, scale_table, gate_table, chosen, combine, w_gate, w_up, w_down
    ):
        tok_dev, width = tokens.shape
        half = w_gate.shape[1]
        cap = chosen.shape[2]
        slots = nz * SLOT
        rows_h, rows_q = half // 2, half // 4
        vmem = pl.BlockSpec(memory_space=pltpu.VMEM)
        hbm = pl.BlockSpec(memory_space=pl.ANY)
        dma = pltpu.SemaphoreType.DMA
        outs = pl.pallas_call(
            functools.partial(layer_kernel, nz),
            out_shape=(
                jax.ShapeDtypeStruct((tok_dev, width), BF16),
                jax.ShapeDtypeStruct((1, cap // 2), F32),
                jax.ShapeDtypeStruct((half, 128), BF16),
                jax.ShapeDtypeStruct((half, 128), BF16),
                jax.ShapeDtypeStruct((half, 128), BF16),
            ),
            in_specs=[vmem] * 8 + [hbm] * 3,
            out_specs=(vmem,) * 5,
            scratch_shapes=[
                pltpu.VMEM((half, width), BF16),
                pltpu.VMEM((half, width), BF16),
                pltpu.VMEM((half, width), BF16),
                pltpu.VMEM((slots, width), BF16),
                pltpu.VMEM((slots, width), BF16),
                pltpu.VMEM((2 * slots, width), BF16),
                pltpu.VMEM((2 * slots, width), BF16),
                pltpu.VMEM((cap, width), BF16),
                pltpu.VMEM((cap, width), BF16),
                pltpu.VMEM((tok_dev, width), F32),
                pltpu.VMEM((tok_dev, width), F32),
                pltpu.VMEM((tok_dev, width), F32),
                pltpu.VMEM((tok_dev, 1), F32),
                pltpu.VMEM((slots, tok_dev), BF16),
                pltpu.VMEM((tok_dev, slots), BF16),
                pltpu.VMEM((cap, 2 * slots), BF16),
                pltpu.VMEM((2 * slots, cap), BF16),
                pltpu.VMEM((half, cap), BF16),
                pltpu.VMEM((half, cap), BF16),
                pltpu.VMEM((half, cap), F32),
                pltpu.VMEM((half, cap), F32),
                pltpu.VMEM((half, cap), F32),
                pltpu.VMEM((half, cap), BF16),
                pltpu.VMEM((half, cap), BF16),
                pltpu.VMEM((cap, half), BF16),
                pltpu.VMEM((cap, half), BF16),

                pltpu.VMEM((2 * slots, width), BF16),
                pltpu.VMEM((slots, width), BF16),
                pltpu.VMEM((slots, width), BF16),
                pltpu.VMEM((slots, width), BF16),
                pltpu.VMEM((8, cap // 2), F32),
                pltpu.VMEM((8, cap // 2), F32),
                pltpu.VMEM((SIDE, SIDE, cap, 128), BF16),
                pltpu.VMEM((2, SIDE - 1, SIDE, cap, 128), BF16),
                pltpu.VMEM((2, 2, SIDE - 1, rows_h, cap), BF16),
                pltpu.VMEM((2, 2, rows_h, width // SIDE), F32),
                pltpu.VMEM((2, SIDE * SIDE, rows_h, 128), BF16),
                pltpu.VMEM((6, SIDE, rows_h, 128), BF16),
                pltpu.VMEM((2, 2, 2, rows_h, 128), BF16),
                pltpu.VMEM((2, 2, SIDE, rows_h, 128), BF16),
                pltpu.VMEM((6, 2, rows_q, 128), BF16),
                pltpu.VMEM((6, 2, rows_h, 128), BF16),
                dma((3,)),
                dma((nz,)),
                dma((2 * nz,)),
                dma((nz * SIDE,)),
                dma((2 * nz * SIDE,)),
                dma((nz,)),
                dma((nz * SIDE,)),
                dma((nz * CHUNKS,)),
                dma((nz * CHUNKS,)),
                dma((1 + CHUNKS,)),
                dma((1 + CHUNKS,)),
                dma((72,)),
                dma((72,)),
                dma((24,)),
                dma((24,)),
            ],
            compiler_params=pltpu.CompilerParams(
                collective_id=0, has_side_effects=True, vmem_limit_bytes=60 * 1024 * 1024
            ),
        )(
            tokens,
            cotangent,
            timestep[None, :],
            shift_table,
            scale_table,
            gate_table,
            chosen[0],
            combine[0],
            w_gate[0],
            w_up[0],
            w_down[0],
        )
        outs = pl.pallas_call(
            copy_kernel,
            out_shape=tuple(jax.ShapeDtypeStruct(o.shape, o.dtype) for o in outs),
            in_specs=[vmem] * 5,
            out_specs=(vmem,) * 5,
        )(*outs)
        d_tokens, d_combine, d_gate, d_up, d_down = outs
        return d_tokens, d_combine[None], d_gate[None], d_up[None], d_down[None]

    in_specs = (
        P(("grp", "exp"), None),
        P(("grp", "exp"), None),
        P(("grp", "exp")),
        P(),
        P(),
        P(),
        P("grp", None, None),
        P("grp", None, None),
        P("exp", None, None),
        P("exp", None, None),
        P("exp", None, None),
    )
    out_specs = (
        P(("grp", "exp"), None),
        P("grp", "exp", None),
        P("exp", None, "grp"),
        P("exp", None, "grp"),
        P("exp", None, "grp"),
    )
    return jax.shard_map(
        on_device, mesh=mesh, in_specs=in_specs, out_specs=out_specs, check_vma=False
    )
```

```python
import functools

import jax
import jax.numpy as jnp
from jax import lax
from jax.experimental import pallas as pl
from jax.experimental.pallas import tpu as pltpu
from jax.sharding import PartitionSpec as P

EPSILON = 1e-06
MESH = pl.DeviceIdType.MESH
F32 = jnp.float32
BF16 = jnp.bfloat16
SLOT = 32
SIDE = 4
CHUNKS = 2
ORDER = (2, 1, 3, 0)
NN = (((1,), (0,)), ((), ()))
NT = (((1,), (1,)), ((), ()))
TN = (((0,), (0,)), ((), ()))


def mm(a, b, dims):
    return lax.dot_general(a, b, dims, preferred_element_type=F32)


def iota(shape, axis):
    return lax.broadcasted_iota(jnp.int32, shape, axis)


def loop(count, body):
    def step(i, carry):
        body(i)
        return carry

    lax.fori_loop(0, count, step, 0)


def layer_kernel(
    nz,
    tok_ref,
    cot_ref,
    step_ref,
    shift_ref,
    scale_ref,
    gate_ref,
    chosen_ref,
    combine_ref,
    wg_hbm,
    wu_hbm,
    wd_hbm,
    dtok_ref,
    dcomb_ref,
    dwg_ref,
    dwu_ref,
    dwd_ref,
    wg,
    wu,
    wd,
    send_a,
    send_b,
    recv_a,
    recv_b,
    rows_in,
    rows_grad,
    normed,
    scale1,
    table,
    inverse,
    pick,
    pick_t,
    place,
    place_t,
    hidden,
    hidden_c,
    gate_f,
    up_f,
    raw,
    d_gate,
    d_up,
    d_gate_t,
    d_up_t,
    back,
    sib,
    send_c,
    ret,
    inner_s,
    inner_r,
    columns_in,
    line_rows,
    line_gate,
    line_sum,
    grads,
    parts,
    far1,
    near1,
    far2,
    near2,
    w_sem,
    a_send,
    a_recv,
    b_send,
    b_recv,
    fa_send,
    fb_send,
    c_send,
    c_recv,
    s_send,
    s_recv,
    r_send,
    r_recv,
    l_send,
    l_recv,
):
    tok_dev, width = tok_ref.shape
    half = wg.shape[0]
    cap = rows_in.shape[0]
    rows_h = half // 2
    rows_q = half // 4
    g = lax.axis_index("grp")
    me = lax.axis_index("exp")
    z = lax.div(me, 2)
    core = lax.rem(me, 2)
    gx = lax.div(g, SIDE)
    gy = lax.rem(g, SIDE)
    sibling = z * 2 + (1 - core)

    def peer(j):
        return lax.rem(z + j, nz)

    def on_z(zz):
        return {"grp": g, "exp": zz * 2 + core}

    on_sib = {"grp": g, "exp": sibling}

    def on_axis(axis, by):
        if axis == 0:
            return {"grp": lax.rem(gx + by, SIDE) * SIDE + gy, "exp": me}
        return {"grp": gx * SIDE + lax.rem(gy + by, SIDE), "exp": me}

    hops = [4, 3, 5, 2, 6, 1, 7] if nz == 8 else list(range(1, nz))

    loads = [
        pltpu.make_async_copy(src, dst, w_sem.at[i])
        for i, (src, dst) in enumerate(((wg_hbm, wg), (wu_hbm, wu), (wd_hbm, wd)))
    ]
    for load in loads:
        load.start()
    barrier = pltpu.get_barrier_semaphore()
    partners = [on_z(peer(j)) for j in hops] + [on_sib]
    partners += [on_axis(axis, by) for axis in (0, 1) for by in (1, 2, 3)]
    for partner in partners:
        pl.semaphore_signal(barrier, inc=1, device_id=partner, device_id_type=MESH)

    first = me * tok_dev
    ids = iota((tok_dev, cap), 0) + first
    lane_e = iota((tok_dev, nz), 1)
    mask = jnp.zeros((tok_dev, nz), F32)
    for e in range(nz):
        hit = jnp.sum(
            jnp.where(ids == chosen_ref[e : e + 1, :], 1.0, 0.0), axis=1, keepdims=True
        )
        mask = jnp.where(lane_e == e, hit, mask)
    earlier = (iota((tok_dev, tok_dev), 1) < iota((tok_dev, tok_dev), 0)).astype(F32)
    rank = mm(earlier.astype(BF16), mask.astype(BF16), NN)
    slots = nz * SLOT
    spread = (lax.div(iota((nz, slots), 1), SLOT) == iota((nz, slots), 0)).astype(F32).astype(BF16)
    rank_p = mm(rank.astype(BF16), spread, NN)
    mask_p = mm(mask.astype(BF16), spread, NN)
    want = lax.rem(iota((tok_dev, slots), 1), SLOT).astype(F32)
    pick_f = jnp.where((rank_p == want) & (mask_p > 0.5), 1.0, 0.0)
    pick_t[...] = pick_f.astype(BF16)
    pick[...] = pick_f.T.astype(BF16)

    steps3 = 3 * scale_ref.shape[0]
    onehot = (lax.rem(iota((steps3, tok_dev), 0), scale_ref.shape[0]) == step_ref[...]).astype(F32)
    onehot = onehot.T.astype(BF16)

    def table_rows(ref):
        whole = ref[...]
        hi = whole.astype(BF16)
        rest = whole - hi.astype(F32)
        mid = rest.astype(BF16)
        low = (rest - mid.astype(F32)).astype(BF16)
        return mm(onehot, jnp.concatenate([hi, mid, low], axis=0), NN)

    scale1[...] = 1.0 + table_rows(scale_ref)
    table[...] = table_rows(shift_ref)

    def normalise(i):
        at = pl.ds(pl.multiple_of(i * 16, 16), 16)
        values = tok_ref[at, :].astype(F32)
        centred = values - jnp.mean(values, axis=1, keepdims=True)
        inv = lax.rsqrt(jnp.mean(centred * centred, axis=1, keepdims=True) + EPSILON)
        inverse[at, :] = inv
        norm = centred * inv
        normed[at, :] = norm
        table[at, :] = norm * scale1[at, :] + table[at, :]

    loop(tok_dev // 16, normalise)

    def fill(dst, i):
        at = pl.ds(pl.multiple_of(i * 512, 512), 512)
        dst[:, at] = mm(pick[...], table[:, at].astype(BF16), NN).astype(BF16)

    def slot_of(zz, cc):
        return pl.ds(pl.multiple_of((cc * nz + zz) * SLOT, SLOT), SLOT)

    def block_of(zz):
        return pl.ds(pl.multiple_of(zz * SLOT, SLOT), SLOT)

    def quarter(s):
        at = lax.rem(gx + ORDER[s], SIDE) * (width // SIDE)
        return pl.ds(pl.multiple_of(at, width // SIDE), width // SIDE)

    def part(ref, rows, s):
        return ref.at[rows] if s is None else ref.at[rows, quarter(s)]

    def sem(j, s):
        return j if s is None else j * SIDE + s

    def to_peer(src, dst, s_sem, r_sem, j, s=None):
        zz = peer(j)
        return pltpu.make_async_remote_copy(
            src_ref=part(src, block_of(zz), s),
            dst_ref=part(dst, slot_of(z, core), s),
            send_sem=s_sem.at[sem(j, s)],
            recv_sem=r_sem.at[sem(j, s)],
            device_id=on_z(zz),
            device_id_type=MESH,
        )

    def from_peer(dst, s_sem, r_sem, j, s=None):
        zz = peer(nz - j)
        return pltpu.make_async_remote_copy(
            src_ref=part(dst, slot_of(zz, core), s),
            dst_ref=part(dst, slot_of(zz, core), s),
            send_sem=s_sem.at[sem(j, s)],
            recv_sem=r_sem.at[sem(j, s)],
            device_id=on_z(peer(j)),
            device_id_type=MESH,
        )

    def to_sibling(dst, s_sem, r_sem, j, s=None):
        zz = peer(nz - j)
        return pltpu.make_async_remote_copy(
            src_ref=part(dst, slot_of(zz, core), s),
            dst_ref=part(dst, slot_of(zz, core), s),
            send_sem=s_sem.at[sem(j, s)],
            recv_sem=r_sem.at[sem(nz + j, s)],
            device_id=on_sib,
            device_id_type=MESH,
        )

    def from_sibling(dst, s_sem, r_sem, j, s=None):
        zz = peer(nz - j)
        return pltpu.make_async_remote_copy(
            src_ref=part(dst, slot_of(zz, 1 - core), s),
            dst_ref=part(dst, slot_of(zz, 1 - core), s),
            send_sem=s_sem.at[sem(j, s)],
            recv_sem=r_sem.at[sem(nz + j, s)],
            device_id=on_sib,
            device_id_type=MESH,
        )

    loop(width // 512, functools.partial(fill, send_a))
    pl.semaphore_wait(barrier, len(partners))
    for j in hops:
        to_peer(send_a, recv_a, a_send, a_recv, j).start()
    recv_a[slot_of(z, core), :] = send_a[block_of(z), :]
    to_sibling(recv_a, fa_send, a_recv, 0).start()

    table[...] = table_rows(gate_ref)

    def weigh(i):
        at = pl.ds(pl.multiple_of(i * 16, 16), 16)
        table[at, :] = table[at, :] * cot_ref[at, :].astype(F32)

    loop(tok_dev // 16, weigh)
    loop(width // 512, functools.partial(fill, send_b))
    recv_b[slot_of(z, core), :] = send_b[block_of(z), :]
    for s in range(SIDE):
        to_sibling(recv_b, fb_send, b_recv, 0, s).start()

    row = chosen_ref[pl.ds(z, 1), :]
    diagonal = iota((cap, cap), 0) == iota((cap, cap), 1)
    column = jnp.sum(jnp.where(diagonal, row.astype(F32), 0.0), axis=1, keepdims=True)
    row_f = row.astype(F32)
    owner_row = jnp.floor(row_f * (1.0 / tok_dev))
    owner_col = jnp.floor(column * (1.0 / tok_dev))
    ahead = jnp.where((owner_row == owner_col) & (row_f < column), 1.0, 0.0)
    place_in = jnp.sum(ahead, axis=1, keepdims=True)
    owner_z = jnp.floor(owner_col * 0.5)
    owner_c = owner_col - 2.0 * owner_z
    at_slot = (owner_c * nz + owner_z) * SLOT + place_in
    place_f = jnp.where(
        iota((cap, 2 * slots), 1).astype(F32) == at_slot, 1.0, 0.0
    )
    place[...] = place_f.astype(BF16)
    place_t[...] = place_f.T.astype(BF16)

    for j in hops:
        from_peer(recv_a, a_send, a_recv, j).wait_recv()
        to_sibling(recv_a, fa_send, a_recv, j).start()
        to_peer(send_a, recv_a, a_send, a_recv, j).wait_send()
        to_peer(send_b, recv_b, b_send, b_recv, j, 0).start()
    for s in range(1, SIDE):
        for j in hops:
            to_peer(send_b, recv_b, b_send, b_recv, j, s).start()
    for j in [0] + hops:
        from_sibling(recv_a, fa_send, a_recv, j).wait_recv()

    def gather_in(i):
        at = pl.ds(pl.multiple_of(i * 512, 512), 512)
        product = mm(place[...], recv_a[:, at], NN).astype(BF16)
        rows_in[:, at] = product
        for k in range(SIDE):
            columns_in[i, k] = product[:, k * 128 : (k + 1) * 128]

    loop(SIDE, gather_in)

    def along(axis, by):
        return lax.rem((gx if axis == 0 else gy) + by, SIDE)

    def line_copy(src, dst, k, axis, by):
        return pltpu.make_async_remote_copy(
            src_ref=src,
            dst_ref=dst,
            send_sem=l_send.at[k],
            recv_sem=l_recv.at[k],
            device_id=on_axis(axis, by),
            device_id_type=MESH,
        )

    row_copies = []
    for by in (2, 1, 3):
        row_copies.append(
            line_copy(columns_in.at[along(0, by)], line_rows.at[0, by - 1], by - 1, 0, by)
        )
        row_copies.append(
            line_copy(columns_in.at[:, along(1, by)], line_rows.at[1, by - 1], by + 2, 1, by)
        )
    for c in row_copies:
        c.start()
    for load in loads:
        load.wait()
    weight = combine_ref[pl.ds(z, 1), :]

    def forward(i):
        at = pl.ds(pl.multiple_of(i * rows_q, rows_q), rows_q)
        pre_gate = mm(wg[at, :], rows_in[...], NT)
        pre_up = mm(wu[at, :], rows_in[...], NT)
        sig = 1.0 / (1.0 + jnp.exp(-pre_gate))
        silu = pre_gate * sig
        hid = silu * pre_up
        hidden[at, :] = hid.astype(BF16)
        hidden_c[at, :] = (hid * weight).astype(BF16)
        up_f[at, :] = silu * weight
        gate_f[at, :] = pre_up * sig * (1.0 + pre_gate * (1.0 - sig)) * weight

    loop(4, forward)

    def down_grad(s):
        product = mm(hidden_c[...], rows_grad[:, quarter(s)], NN).astype(BF16)
        for k in range(SIDE):
            piece = product[:, k * 128 : (k + 1) * 128]
            grads[0, s * SIDE + k] = piece[:rows_h]
            grads[1, k * SIDE + s] = piece[rows_h:]
        ready = {0: ((0, 0), (0, 1)), 1: ((0, 2), (1, 0), (1, 3)), 2: ((0, 3),), 3: ((1, 1), (1, 2))}
        for h, k in ready[s]:
            rings[0, h][0][k].start()

    def line_rows_of(h, r):
        return jnp.concatenate([line_rows[h, r, k] for k in range(SIDE)], axis=1)

    def line_near(t, h):
        grad = (d_gate, d_up)[t - 1]
        here = [columns_in[gx, k] if h == 0 else columns_in[k, gy] for k in range(SIDE)]
        total = mm(
            grad[h * rows_h : (h + 1) * rows_h, :], jnp.concatenate(here, axis=1), NN
        )
        for r in (0, 2):
            total = total + mm(line_gate[t - 1, h, r], line_rows_of(h, r), NN)
        line_sum[t - 1, h] = total

    def line_far(t, h):
        total = line_sum[t - 1, h] + mm(line_gate[t - 1, h, 1], line_rows_of(h, 1), NN)
        total = total.astype(BF16)
        for k in range(SIDE):
            parts[2 * t + h, k] = total[:, k * 128 : (k + 1) * 128]

    def ring(t, h):
        n = 2 * t + h
        ia, ib = (gx, gy) if h == 0 else (gy, gx)
        own, other = h, 1 - h

        def copy(src, dst, k, axis, by):
            return pltpu.make_async_remote_copy(
                src_ref=src,
                dst_ref=dst,
                send_sem=r_send.at[n * 12 + k],
                recv_sem=r_recv.at[n * 12 + k],
                device_id=on_axis(axis, by),
                device_id_type=MESH,
            )

        def block(dest):
            return (ORDER.index(dest) if h == 0 else lax.rem(ia + dest, SIDE)) * SIDE

        def pair(dest, q):
            return pl.ds(block(dest) + 2 * q, 2)

        def sub(dest):
            return ORDER.index(dest) if t == 0 and h == 1 else lax.rem(ib + dest, SIDE)

        one, two = (1, SIDE - 1), SIDE // 2
        first_copies = []
        if t == 0:
            first_copies = [
                copy(grads.at[n, pair(two, 0)], far1.at[n, 0], 0, own, one[0]),
                copy(grads.at[n, pair(two, 1)], far1.at[n, 1], 1, own, one[1]),
                copy(grads.at[n, pair(1, 1)], near1.at[n, 0, pl.ds(2, 2)], 2, own, one[0]),
                copy(grads.at[n, pair(3, 0)], near1.at[n, 1, pl.ds(0, 2)], 3, own, one[1]),
                copy(grads.at[n, pair(1, 0)], near1.at[n, 0, pl.ds(0, 2)], 4, own, one[0]),
                copy(grads.at[n, pair(3, 1)], near1.at[n, 1, pl.ds(2, 2)], 5, own, one[1]),
            ]
        top, low = pl.ds(0, rows_q), pl.ds(rows_q, rows_q)
        next_copies = [
            copy(parts.at[n, sub(two), top], far2.at[n, 0], 6, other, one[0]),
            copy(parts.at[n, sub(two), low], far2.at[n, 1], 7, other, one[1]),
            copy(parts.at[n, sub(1), low], near2.at[n, 0, low], 8, other, one[0]),
            copy(parts.at[n, sub(3), top], near2.at[n, 1, top], 9, other, one[1]),
            copy(parts.at[n, sub(1), top], near2.at[n, 0, top], 10, other, one[0]),
            copy(parts.at[n, sub(3), low], near2.at[n, 1, low], 11, other, one[1]),
        ]

        def merge1():
            for side, dest in ((0, 1), (1, 3)):
                first_copies[side].wait_recv()
                base = block(dest) + 2 * side

                def add(i):
                    grads[n, base + i] = (
                        grads[n, base + i].astype(F32) + far1[n, side, i].astype(F32)
                    ).astype(BF16)

                loop(2, add)
                first_copies[4 + side].start()

        def start2():
            for c in next_copies[:4]:
                c.start()

        def finish1():
            for c in first_copies[2:]:
                c.wait_recv()
            base = block(0)

            def add(i):
                parts[n, i] = (
                    grads[n, base + i].astype(F32)
                    + near1[n, 0, i].astype(F32)
                    + near1[n, 1, i].astype(F32)
                ).astype(BF16)

            loop(SIDE, add)
            start2()

        def merge2():
            for side, dest, part in ((0, 1, top), (1, 3, low)):
                next_copies[side].wait_recv()
                parts[n, sub(dest), part] = (
                    parts[n, sub(dest), part].astype(F32) + far2[n, side].astype(F32)
                ).astype(BF16)
                next_copies[4 + side].start()

        def finish2(out):
            for c in next_copies[2:]:
                c.wait_recv()
            total = (
                parts[n, sub(0)].astype(F32)
                + near2[n, 0].astype(F32)
                + near2[n, 1].astype(F32)
            )
            out[h * rows_h : (h + 1) * rows_h, :] = (total * (1.0 / (SIDE * SIDE))).astype(BF16)

        def drain():
            for c in first_copies + next_copies:
                c.wait_send()

        return first_copies, merge1, finish1, merge2, finish2, drain, start2

    rings = {(t, h): ring(t, h) for t in range(3) for h in range(2)}

    def run(t, phase, *args):
        for h in range(2):
            rings[t, h][phase](*args)

    def raw_sum(s, i):
        at = pl.ds(pl.multiple_of(i * rows_q, rows_q), rows_q)
        product = mm(wd[at, quarter(s)], rows_grad[:, quarter(s)], NT)
        raw[at, :] = product if s == 0 else raw[at, :] + product

    for s in range(SIDE):
        for j in hops:
            from_peer(recv_b, b_send, b_recv, j, s).wait_recv()
            to_sibling(recv_b, fb_send, b_recv, j, s).start()
        for j in [0] + hops:
            from_sibling(recv_b, fb_send, b_recv, j, s).wait_recv()
        rows_grad[:, quarter(s)] = mm(place[...], recv_b[:, quarter(s)], NN).astype(BF16)
        loop(4, functools.partial(raw_sum, s))
        if s < SIDE - 1:
            down_grad(s)
        if s == 2:
            rings[0, 0][1]()

    def backward(i):
        at = pl.ds(i * rows_q, rows_q)
        value = raw[at, :]
        d_gate[at, :] = (value * gate_f[at, :]).astype(BF16)
        d_up[at, :] = (value * up_f[at, :]).astype(BF16)
        return jnp.sum(hidden[at, :].astype(F32) * value, axis=0, keepdims=True)

    inner = backward(0)
    for i in range(1, 4):
        inner = inner + backward(i)
    gate_copies, forwards = {}, {}
    for t, grad in ((1, d_gate), (2, d_up)):
        for h in range(2):
            for side, by in ((0, 1), (1, 3)):
                gate_copies[t, h, side] = line_copy(
                    grad.at[pl.ds(h * rows_h, rows_h)],
                    line_gate.at[t - 1, h, by - 1],
                    8 * t + 4 * h + side,
                    h,
                    by,
                )
                piece = pl.ds(side * rows_q, rows_q)
                forwards[t, h, side] = line_copy(
                    line_gate.at[t - 1, h, by - 1, piece],
                    line_gate.at[t - 1, h, 1, piece],
                    8 * t + 4 * h + 2 + side,
                    h,
                    by,
                )
    for c in gate_copies.values():
        c.start()
    left, right = inner[:, : cap // 2], inner[:, cap // 2 :]
    mine = jnp.where(core == 0, left, right)
    theirs = jnp.where(core == 0, right, left)
    inner_s[...] = jnp.broadcast_to(theirs, inner_s.shape)
    inner_copy = pltpu.make_async_remote_copy(
        src_ref=inner_s,
        dst_ref=inner_r,
        send_sem=s_send.at[0],
        recv_sem=s_recv.at[0],
        device_id=on_sib,
        device_id_type=MESH,
    )
    inner_copy.start()
    d_gate_t[...] = d_gate[...].astype(F32).T.astype(BF16)
    d_up_t[...] = d_up[...].astype(F32).T.astype(BF16)

    chunk = width // CHUNKS
    own_rows = pl.ds(pl.multiple_of(core * slots, slots), slots)
    their_rows = pl.ds(pl.multiple_of((1 - core) * slots, slots), slots)

    def columns(i):
        return pl.ds(i * chunk, chunk)

    sib_copies = [
        pltpu.make_async_remote_copy(
            src_ref=back.at[their_rows, columns(i)],
            dst_ref=sib.at[:, columns(i)],
            send_sem=s_send.at[1 + i],
            recv_sem=s_recv.at[1 + i],
            device_id=on_sib,
            device_id_type=MESH,
        )
        for i in range(CHUNKS)
    ]

    def to_owner(j, i):
        zz = peer(j)
        return pltpu.make_async_remote_copy(
            src_ref=send_c.at[block_of(zz), columns(i)],
            dst_ref=ret.at[block_of(z), columns(i)],
            send_sem=c_send.at[j * CHUNKS + i],
            recv_sem=c_recv.at[j * CHUNKS + i],
            device_id=on_z(zz),
            device_id_type=MESH,
        )

    def from_expert(j, i):
        zz = peer(nz - j)
        return pltpu.make_async_remote_copy(
            src_ref=ret.at[block_of(zz), columns(i)],
            dst_ref=ret.at[block_of(zz), columns(i)],
            send_sem=c_send.at[j * CHUNKS + i],
            recv_sem=c_recv.at[j * CHUNKS + i],
            device_id=on_z(peer(j)),
            device_id_type=MESH,
        )

    def input_grad(i):
        at = columns(i)
        total = mm(d_gate_t[...], wg[:, at], NN) + mm(d_up_t[...], wu[:, at], NN)
        back[:, at] = mm(place_t[...], total.astype(BF16), NN).astype(BF16)
        sib_copies[i].start()

    def send_home(i):
        at = columns(i)
        sib_copies[i].wait_recv()
        send_c[:, at] = (back[own_rows, at].astype(F32) + sib[:, at].astype(F32)).astype(BF16)
        for j in hops:
            to_owner(j, i).start()
        ret[block_of(z), at] = send_c[block_of(z), at]

    for i in range(CHUNKS):
        input_grad(i)
        if i:
            send_home(i - 1)
    down_grad(SIDE - 1)
    send_home(CHUNKS - 1)
    for key, c in gate_copies.items():
        c.wait_recv()
        forwards[key].start()
    rings[0, 1][1]()
    for c in row_copies:
        c.wait_recv()
    for t in (1, 2):
        for h in range(2):
            line_near(t, h)
    inner_copy.wait_recv()
    dcomb_ref[...] = mine + inner_r[0:1, :]
    for t in (1, 2):
        for h in range(2):
            for side in range(2):
                forwards[t, h, side].wait_recv()
            line_far(t, h)
            rings[t, h][6]()
    run(0, 2)
    run(1, 3)
    run(2, 3)
    run(0, 3)
    for j in hops:
        for i in range(CHUNKS):
            from_expert(j, i).wait_recv()

    def spread_back(i):
        at = pl.ds(pl.multiple_of(i * 512, 512), 512)
        table[:, at] = mm(pick_t[...], ret[:, at], NN)

    loop(width // 512, spread_back)

    def token_grad(i):
        at = pl.ds(pl.multiple_of(i * 16, 16), 16)
        norm = normed[at, :]
        d_norm = table[at, :] * scale1[at, :]
        centre = jnp.mean(d_norm, axis=1, keepdims=True)
        along = jnp.mean(d_norm * norm, axis=1, keepdims=True)
        dtok_ref[at, :] = (inverse[at, :] * (d_norm - centre - norm * along)).astype(BF16)

    loop(tok_dev // 16, token_grad)
    run(1, 4, dwg_ref)
    run(2, 4, dwu_ref)
    run(0, 4, dwd_ref)

    for j in hops:
        for s in range(SIDE):
            to_peer(send_b, recv_b, b_send, b_recv, j, s).wait_send()
        for i in range(CHUNKS):
            to_owner(j, i).wait_send()
    for j in [0] + hops:
        to_sibling(recv_a, fa_send, a_recv, j).wait_send()
        for s in range(SIDE):
            to_sibling(recv_b, fb_send, b_recv, j, s).wait_send()
    for c in [*row_copies, *gate_copies.values(), *forwards.values()]:
        c.wait_send()
    inner_copy.wait_send()
    for c in sib_copies:
        c.wait_send()
    for t in range(3):
        run(t, 5)


def copy_kernel(*refs):
    count = len(refs) // 2
    for i in range(count):
        refs[count + i][...] = refs[i][...]


def solution(mesh):
    nz = mesh.shape["exp"] // 2

    def on_device(
        tokens, cotangent, timestep, shift_table, scale_table, gate_table, chosen, combine, w_gate, w_up, w_down
    ):
        tok_dev, width = tokens.shape
        half = w_gate.shape[1]
        cap = chosen.shape[2]
        slots = nz * SLOT
        rows_h, rows_q = half // 2, half // 4
        vmem = pl.BlockSpec(memory_space=pltpu.VMEM)
        hbm = pl.BlockSpec(memory_space=pl.ANY)
        dma = pltpu.SemaphoreType.DMA
        outs = pl.pallas_call(
            functools.partial(layer_kernel, nz),
            out_shape=(
                jax.ShapeDtypeStruct((tok_dev, width), BF16),
                jax.ShapeDtypeStruct((1, cap // 2), F32),
                jax.ShapeDtypeStruct((half, 128), BF16),
                jax.ShapeDtypeStruct((half, 128), BF16),
                jax.ShapeDtypeStruct((half, 128), BF16),
            ),
            in_specs=[vmem] * 8 + [hbm] * 3,
            out_specs=(vmem,) * 5,
            scratch_shapes=[
                pltpu.VMEM((half, width), BF16),
                pltpu.VMEM((half, width), BF16),
                pltpu.VMEM((half, width), BF16),
                pltpu.VMEM((slots, width), BF16),
                pltpu.VMEM((slots, width), BF16),
                pltpu.VMEM((2 * slots, width), BF16),
                pltpu.VMEM((2 * slots, width), BF16),
                pltpu.VMEM((cap, width), BF16),
                pltpu.VMEM((cap, width), BF16),
                pltpu.VMEM((tok_dev, width), F32),
                pltpu.VMEM((tok_dev, width), F32),
                pltpu.VMEM((tok_dev, width), F32),
                pltpu.VMEM((tok_dev, 1), F32),
                pltpu.VMEM((slots, tok_dev), BF16),
                pltpu.VMEM((tok_dev, slots), BF16),
                pltpu.VMEM((cap, 2 * slots), BF16),
                pltpu.VMEM((2 * slots, cap), BF16),
                pltpu.VMEM((half, cap), BF16),
                pltpu.VMEM((half, cap), BF16),
                pltpu.VMEM((half, cap), F32),
                pltpu.VMEM((half, cap), F32),
                pltpu.VMEM((half, cap), F32),
                pltpu.VMEM((half, cap), BF16),
                pltpu.VMEM((half, cap), BF16),
                pltpu.VMEM((cap, half), BF16),
                pltpu.VMEM((cap, half), BF16),

                pltpu.VMEM((2 * slots, width), BF16),
                pltpu.VMEM((slots, width), BF16),
                pltpu.VMEM((slots, width), BF16),
                pltpu.VMEM((slots, width), BF16),
                pltpu.VMEM((8, cap // 2), F32),
                pltpu.VMEM((8, cap // 2), F32),
                pltpu.VMEM((SIDE, SIDE, cap, 128), BF16),
                pltpu.VMEM((2, SIDE - 1, SIDE, cap, 128), BF16),
                pltpu.VMEM((2, 2, SIDE - 1, rows_h, cap), BF16),
                pltpu.VMEM((2, 2, rows_h, width // SIDE), F32),
                pltpu.VMEM((2, SIDE * SIDE, rows_h, 128), BF16),
                pltpu.VMEM((6, SIDE, rows_h, 128), BF16),
                pltpu.VMEM((2, 2, 2, rows_h, 128), BF16),
                pltpu.VMEM((2, 2, SIDE, rows_h, 128), BF16),
                pltpu.VMEM((6, 2, rows_q, 128), BF16),
                pltpu.VMEM((6, 2, rows_h, 128), BF16),
                dma((3,)),
                dma((nz,)),
                dma((2 * nz,)),
                dma((nz * SIDE,)),
                dma((2 * nz * SIDE,)),
                dma((nz,)),
                dma((nz * SIDE,)),
                dma((nz * CHUNKS,)),
                dma((nz * CHUNKS,)),
                dma((1 + CHUNKS,)),
                dma((1 + CHUNKS,)),
                dma((72,)),
                dma((72,)),
                dma((24,)),
                dma((24,)),
            ],
            compiler_params=pltpu.CompilerParams(
                collective_id=0, has_side_effects=True, vmem_limit_bytes=60 * 1024 * 1024
            ),
        )(
            tokens,
            cotangent,
            timestep[None, :],
            shift_table,
            scale_table,
            gate_table,
            chosen[0],
            combine[0],
            w_gate[0],
            w_up[0],
            w_down[0],
        )
        outs = pl.pallas_call(
            copy_kernel,
            out_shape=tuple(jax.ShapeDtypeStruct(o.shape, o.dtype) for o in outs),
            in_specs=[vmem] * 5,
            out_specs=(vmem,) * 5,
        )(*outs)
        d_tokens, d_combine, d_gate, d_up, d_down = outs
        return d_tokens, d_combine[None], d_gate[None], d_up[None], d_down[None]

    in_specs = (
        P(("grp", "exp"), None),
        P(("grp", "exp"), None),
        P(("grp", "exp")),
        P(),
        P(),
        P(),
        P("grp", None, None),
        P("grp", None, None),
        P("exp", None, None),
        P("exp", None, None),
        P("exp", None, None),
    )
    out_specs = (
        P(("grp", "exp"), None),
        P("grp", "exp", None),
        P("exp", None, "grp"),
        P("exp", None, "grp"),
        P("exp", None, "grp"),
    )
    return jax.shard_map(
        on_device, mesh=mesh, in_specs=in_specs, out_specs=out_specs, check_vma=False
    )
```

```python
import functools

import jax
import jax.numpy as jnp
from jax import lax
from jax.experimental import pallas as pl
from jax.experimental.pallas import tpu as pltpu
from jax.sharding import PartitionSpec as P

EPSILON = 1e-06
MESH = pl.DeviceIdType.MESH
F32 = jnp.float32
BF16 = jnp.bfloat16
SLOT = 32
SIDE = 4
CHUNKS = 2
ORDER = (2, 1, 3, 0)
NN = (((1,), (0,)), ((), ()))
NT = (((1,), (1,)), ((), ()))
TN = (((0,), (0,)), ((), ()))


def mm(a, b, dims):
    return lax.dot_general(a, b, dims, preferred_element_type=F32)


def iota(shape, axis):
    return lax.broadcasted_iota(jnp.int32, shape, axis)


def loop(count, body):
    def step(i, carry):
        body(i)
        return carry

    lax.fori_loop(0, count, step, 0)


def layer_kernel(
    nz,
    tok_ref,
    cot_ref,
    step_ref,
    shift_ref,
    scale_ref,
    gate_ref,
    chosen_ref,
    combine_ref,
    wg_hbm,
    wu_hbm,
    wd_hbm,
    dtok_ref,
    dcomb_ref,
    dwg_ref,
    dwu_ref,
    dwd_ref,
    wg,
    wu,
    wd,
    send_a,
    send_b,
    recv_a,
    recv_b,
    rows_in,
    rows_grad,
    normed,
    scale1,
    table,
    inverse,
    pick,
    pick_t,
    place,
    place_t,
    hidden,
    hidden_c,
    gate_f,
    up_f,
    raw,
    d_gate,
    d_up,
    d_gate_t,
    d_up_t,
    back,
    sib,
    send_c,
    ret,
    inner_s,
    inner_r,
    columns_in,
    line_rows,
    line_gate,
    line_sum,
    grads,
    parts,
    far1,
    near1,
    far2,
    near2,
    w_sem,
    a_send,
    a_recv,
    b_send,
    b_recv,
    fa_send,
    fb_send,
    c_send,
    c_recv,
    s_send,
    s_recv,
    r_send,
    r_recv,
    l_send,
    l_recv,
):
    tok_dev, width = tok_ref.shape
    half = wg.shape[0]
    cap = rows_in.shape[0]
    rows_h = half // 2
    rows_q = half // 4
    g = lax.axis_index("grp")
    me = lax.axis_index("exp")
    z = lax.div(me, 2)
    core = lax.rem(me, 2)
    gx = lax.div(g, SIDE)
    gy = lax.rem(g, SIDE)
    sibling = z * 2 + (1 - core)

    def peer(j):
        return lax.rem(z + j, nz)

    def on_z(zz):
        return {"grp": g, "exp": zz * 2 + core}

    on_sib = {"grp": g, "exp": sibling}

    def on_axis(axis, by):
        if axis == 0:
            return {"grp": lax.rem(gx + by, SIDE) * SIDE + gy, "exp": me}
        return {"grp": gx * SIDE + lax.rem(gy + by, SIDE), "exp": me}

    hops = [4, 3, 5, 2, 6, 1, 7] if nz == 8 else list(range(1, nz))

    loads = [
        pltpu.make_async_copy(src, dst, w_sem.at[i])
        for i, (src, dst) in enumerate(((wg_hbm, wg), (wu_hbm, wu), (wd_hbm, wd)))
    ]
    for load in loads:
        load.start()
    barrier = pltpu.get_barrier_semaphore()
    partners = [on_z(peer(j)) for j in hops] + [on_sib]
    partners += [on_axis(axis, by) for axis in (0, 1) for by in (1, 2, 3)]
    for partner in partners:
        pl.semaphore_signal(barrier, inc=1, device_id=partner, device_id_type=MESH)

    first = me * tok_dev
    ids = iota((tok_dev, cap), 0) + first
    lane_e = iota((tok_dev, nz), 1)
    mask = jnp.zeros((tok_dev, nz), F32)
    for e in range(nz):
        hit = jnp.sum(
            jnp.where(ids == chosen_ref[e : e + 1, :], 1.0, 0.0), axis=1, keepdims=True
        )
        mask = jnp.where(lane_e == e, hit, mask)
    earlier = (iota((tok_dev, tok_dev), 1) < iota((tok_dev, tok_dev), 0)).astype(F32)
    rank = mm(earlier.astype(BF16), mask.astype(BF16), NN)
    slots = nz * SLOT
    spread = (lax.div(iota((nz, slots), 1), SLOT) == iota((nz, slots), 0)).astype(F32).astype(BF16)
    rank_p = mm(rank.astype(BF16), spread, NN)
    mask_p = mm(mask.astype(BF16), spread, NN)
    want = lax.rem(iota((tok_dev, slots), 1), SLOT).astype(F32)
    pick_f = jnp.where((rank_p == want) & (mask_p > 0.5), 1.0, 0.0)
    pick_t[...] = pick_f.astype(BF16)
    pick[...] = pick_f.T.astype(BF16)

    steps3 = 3 * scale_ref.shape[0]
    onehot = (lax.rem(iota((steps3, tok_dev), 0), scale_ref.shape[0]) == step_ref[...]).astype(F32)
    onehot = onehot.T.astype(BF16)

    def table_rows(ref):
        whole = ref[...]
        hi = whole.astype(BF16)
        rest = whole - hi.astype(F32)
        mid = rest.astype(BF16)
        low = (rest - mid.astype(F32)).astype(BF16)
        return mm(onehot, jnp.concatenate([hi, mid, low], axis=0), NN)

    scale1[...] = 1.0 + table_rows(scale_ref)
    table[...] = table_rows(shift_ref)

    def normalise(i):
        at = pl.ds(pl.multiple_of(i * 16, 16), 16)
        values = tok_ref[at, :].astype(F32)
        centred = values - jnp.mean(values, axis=1, keepdims=True)
        inv = lax.rsqrt(jnp.mean(centred * centred, axis=1, keepdims=True) + EPSILON)
        inverse[at, :] = inv
        norm = centred * inv
        normed[at, :] = norm
        table[at, :] = norm * scale1[at, :] + table[at, :]

    loop(tok_dev // 16, normalise)

    def fill(dst, i):
        at = pl.ds(pl.multiple_of(i * 512, 512), 512)
        dst[:, at] = mm(pick[...], table[:, at].astype(BF16), NN).astype(BF16)

    def slot_of(zz, cc):
        return pl.ds(pl.multiple_of((cc * nz + zz) * SLOT, SLOT), SLOT)

    def block_of(zz):
        return pl.ds(pl.multiple_of(zz * SLOT, SLOT), SLOT)

    def quarter(s):
        at = lax.rem(gx + ORDER[s], SIDE) * (width // SIDE)
        return pl.ds(pl.multiple_of(at, width // SIDE), width // SIDE)

    def part(ref, rows, s):
        return ref.at[rows] if s is None else ref.at[rows, quarter(s)]

    def sem(j, s):
        return j if s is None else j * SIDE + s

    def to_peer(src, dst, s_sem, r_sem, j, s=None):
        zz = peer(j)
        return pltpu.make_async_remote_copy(
            src_ref=part(src, block_of(zz), s),
            dst_ref=part(dst, slot_of(z, core), s),
            send_sem=s_sem.at[sem(j, s)],
            recv_sem=r_sem.at[sem(j, s)],
            device_id=on_z(zz),
            device_id_type=MESH,
        )

    def from_peer(dst, s_sem, r_sem, j, s=None):
        zz = peer(nz - j)
        return pltpu.make_async_remote_copy(
            src_ref=part(dst, slot_of(zz, core), s),
            dst_ref=part(dst, slot_of(zz, core), s),
            send_sem=s_sem.at[sem(j, s)],
            recv_sem=r_sem.at[sem(j, s)],
            device_id=on_z(peer(j)),
            device_id_type=MESH,
        )

    def to_sibling(dst, s_sem, r_sem, j, s=None):
        zz = peer(nz - j)
        return pltpu.make_async_remote_copy(
            src_ref=part(dst, slot_of(zz, core), s),
            dst_ref=part(dst, slot_of(zz, core), s),
            send_sem=s_sem.at[sem(j, s)],
            recv_sem=r_sem.at[sem(nz + j, s)],
            device_id=on_sib,
            device_id_type=MESH,
        )

    def from_sibling(dst, s_sem, r_sem, j, s=None):
        zz = peer(nz - j)
        return pltpu.make_async_remote_copy(
            src_ref=part(dst, slot_of(zz, 1 - core), s),
            dst_ref=part(dst, slot_of(zz, 1 - core), s),
            send_sem=s_sem.at[sem(j, s)],
            recv_sem=r_sem.at[sem(nz + j, s)],
            device_id=on_sib,
            device_id_type=MESH,
        )

    loop(width // 512, functools.partial(fill, send_a))
    pl.semaphore_wait(barrier, len(partners))
    for j in hops:
        to_peer(send_a, recv_a, a_send, a_recv, j).start()
    recv_a[slot_of(z, core), :] = send_a[block_of(z), :]
    to_sibling(recv_a, fa_send, a_recv, 0).start()

    table[...] = table_rows(gate_ref)

    def weigh(i):
        at = pl.ds(pl.multiple_of(i * 16, 16), 16)
        table[at, :] = table[at, :] * cot_ref[at, :].astype(F32)

    loop(tok_dev // 16, weigh)
    loop(width // 512, functools.partial(fill, send_b))
    recv_b[slot_of(z, core), :] = send_b[block_of(z), :]
    for s in range(SIDE):
        to_sibling(recv_b, fb_send, b_recv, 0, s).start()

    row = chosen_ref[pl.ds(z, 1), :]
    diagonal = iota((cap, cap), 0) == iota((cap, cap), 1)
    column = jnp.sum(jnp.where(diagonal, row.astype(F32), 0.0), axis=1, keepdims=True)
    row_f = row.astype(F32)
    owner_row = jnp.floor(row_f * (1.0 / tok_dev))
    owner_col = jnp.floor(column * (1.0 / tok_dev))
    ahead = jnp.where((owner_row == owner_col) & (row_f < column), 1.0, 0.0)
    place_in = jnp.sum(ahead, axis=1, keepdims=True)
    owner_z = jnp.floor(owner_col * 0.5)
    owner_c = owner_col - 2.0 * owner_z
    at_slot = (owner_c * nz + owner_z) * SLOT + place_in
    place_f = jnp.where(
        iota((cap, 2 * slots), 1).astype(F32) == at_slot, 1.0, 0.0
    )
    place[...] = place_f.astype(BF16)
    place_t[...] = place_f.T.astype(BF16)

    for j in hops:
        to_peer(send_a, recv_a, a_send, a_recv, j).wait_send()
        to_peer(send_b, recv_b, b_send, b_recv, j, 0).start()
    for s in range(1, SIDE):
        for j in hops:
            to_peer(send_b, recv_b, b_send, b_recv, j, s).start()
    for j in hops:
        from_peer(recv_a, a_send, a_recv, j).wait_recv()
        to_sibling(recv_a, fa_send, a_recv, j).start()
    for j in [0] + hops:
        from_sibling(recv_a, fa_send, a_recv, j).wait_recv()

    def gather_in(i):
        at = pl.ds(pl.multiple_of(i * 512, 512), 512)
        product = mm(place[...], recv_a[:, at], NN).astype(BF16)
        rows_in[:, at] = product
        for k in range(SIDE):
            columns_in[i, k] = product[:, k * 128 : (k + 1) * 128]

    loop(SIDE, gather_in)

    def along(axis, by):
        return lax.rem((gx if axis == 0 else gy) + by, SIDE)

    def line_copy(src, dst, k, axis, by):
        return pltpu.make_async_remote_copy(
            src_ref=src,
            dst_ref=dst,
            send_sem=l_send.at[k],
            recv_sem=l_recv.at[k],
            device_id=on_axis(axis, by),
            device_id_type=MESH,
        )

    row_copies = []
    for by in (2, 1, 3):
        row_copies.append(
            line_copy(columns_in.at[along(0, by)], line_rows.at[0, by - 1], by - 1, 0, by)
        )
        row_copies.append(
            line_copy(columns_in.at[:, along(1, by)], line_rows.at[1, by - 1], by + 2, 1, by)
        )
    for c in row_copies:
        c.start()
    for load in loads:
        load.wait()
    weight = combine_ref[pl.ds(z, 1), :]

    def forward(i):
        at = pl.ds(pl.multiple_of(i * rows_q, rows_q), rows_q)
        pre_gate = mm(wg[at, :], rows_in[...], NT)
        pre_up = mm(wu[at, :], rows_in[...], NT)
        sig = 1.0 / (1.0 + jnp.exp(-pre_gate))
        silu = pre_gate * sig
        hid = silu * pre_up
        hidden[at, :] = hid.astype(BF16)
        hidden_c[at, :] = (hid * weight).astype(BF16)
        up_f[at, :] = silu * weight
        gate_f[at, :] = pre_up * sig * (1.0 + pre_gate * (1.0 - sig)) * weight

    loop(4, forward)

    def down_grad(s):
        product = mm(hidden_c[...], rows_grad[:, quarter(s)], NN).astype(BF16)
        for k in range(SIDE):
            piece = product[:, k * 128 : (k + 1) * 128]
            grads[0, s * SIDE + k] = piece[:rows_h]
            grads[1, k * SIDE + s] = piece[rows_h:]
        ready = {0: ((0, 0), (0, 1)), 1: ((0, 2), (1, 0), (1, 3)), 2: ((0, 3),), 3: ((1, 1), (1, 2))}
        for h, k in ready[s]:
            rings[0, h][0][k].start()

    def line_rows_of(h, r):
        return jnp.concatenate([line_rows[h, r, k] for k in range(SIDE)], axis=1)

    def line_near(t, h):
        grad = (d_gate, d_up)[t - 1]
        here = [columns_in[gx, k] if h == 0 else columns_in[k, gy] for k in range(SIDE)]
        total = mm(
            grad[h * rows_h : (h + 1) * rows_h, :], jnp.concatenate(here, axis=1), NN
        )
        for r in (0, 2):
            total = total + mm(line_gate[t - 1, h, r], line_rows_of(h, r), NN)
        line_sum[t - 1, h] = total

    def line_far(t, h):
        total = line_sum[t - 1, h] + mm(line_gate[t - 1, h, 1], line_rows_of(h, 1), NN)
        total = total.astype(BF16)
        for k in range(SIDE):
            parts[2 * t + h, k] = total[:, k * 128 : (k + 1) * 128]

    def ring(t, h):
        n = 2 * t + h
        ia, ib = (gx, gy) if h == 0 else (gy, gx)
        own, other = h, 1 - h

        def copy(src, dst, k, axis, by):
            return pltpu.make_async_remote_copy(
                src_ref=src,
                dst_ref=dst,
                send_sem=r_send.at[n * 12 + k],
                recv_sem=r_recv.at[n * 12 + k],
                device_id=on_axis(axis, by),
                device_id_type=MESH,
            )

        def block(dest):
            return (ORDER.index(dest) if h == 0 else lax.rem(ia + dest, SIDE)) * SIDE

        def pair(dest, q):
            return pl.ds(block(dest) + 2 * q, 2)

        def sub(dest):
            return ORDER.index(dest) if t == 0 and h == 1 else lax.rem(ib + dest, SIDE)

        one, two = (1, SIDE - 1), SIDE // 2
        first_copies = []
        if t == 0:
            first_copies = [
                copy(grads.at[n, pair(two, 0)], far1.at[n, 0], 0, own, one[0]),
                copy(grads.at[n, pair(two, 1)], far1.at[n, 1], 1, own, one[1]),
                copy(grads.at[n, pair(1, 1)], near1.at[n, 0, pl.ds(2, 2)], 2, own, one[0]),
                copy(grads.at[n, pair(3, 0)], near1.at[n, 1, pl.ds(0, 2)], 3, own, one[1]),
                copy(grads.at[n, pair(1, 0)], near1.at[n, 0, pl.ds(0, 2)], 4, own, one[0]),
                copy(grads.at[n, pair(3, 1)], near1.at[n, 1, pl.ds(2, 2)], 5, own, one[1]),
            ]
        top, low = pl.ds(0, rows_q), pl.ds(rows_q, rows_q)
        next_copies = [
            copy(parts.at[n, sub(two), top], far2.at[n, 0], 6, other, one[0]),
            copy(parts.at[n, sub(two), low], far2.at[n, 1], 7, other, one[1]),
            copy(parts.at[n, sub(1), low], near2.at[n, 0, low], 8, other, one[0]),
            copy(parts.at[n, sub(3), top], near2.at[n, 1, top], 9, other, one[1]),
            copy(parts.at[n, sub(1), top], near2.at[n, 0, top], 10, other, one[0]),
            copy(parts.at[n, sub(3), low], near2.at[n, 1, low], 11, other, one[1]),
        ]

        def merge1():
            for side, dest in ((0, 1), (1, 3)):
                first_copies[side].wait_recv()
                base = block(dest) + 2 * side

                def add(i):
                    grads[n, base + i] = (
                        grads[n, base + i].astype(F32) + far1[n, side, i].astype(F32)
                    ).astype(BF16)

                loop(2, add)
                first_copies[4 + side].start()

        def start2():
            for c in next_copies[:4]:
                c.start()

        def finish1():
            for c in first_copies[2:]:
                c.wait_recv()
            base = block(0)

            def add(i):
                parts[n, i] = (
                    grads[n, base + i].astype(F32)
                    + near1[n, 0, i].astype(F32)
                    + near1[n, 1, i].astype(F32)
                ).astype(BF16)

            loop(SIDE, add)
            start2()

        def merge2():
            for side, dest, part in ((0, 1, top), (1, 3, low)):
                next_copies[side].wait_recv()
                parts[n, sub(dest), part] = (
                    parts[n, sub(dest), part].astype(F32) + far2[n, side].astype(F32)
                ).astype(BF16)
                next_copies[4 + side].start()

        def finish2(out):
            for c in next_copies[2:]:
                c.wait_recv()
            total = (
                parts[n, sub(0)].astype(F32)
                + near2[n, 0].astype(F32)
                + near2[n, 1].astype(F32)
            )
            out[h * rows_h : (h + 1) * rows_h, :] = (total * (1.0 / (SIDE * SIDE))).astype(BF16)

        def drain():
            for c in first_copies + next_copies:
                c.wait_send()

        return first_copies, merge1, finish1, merge2, finish2, drain, start2

    rings = {(t, h): ring(t, h) for t in range(3) for h in range(2)}

    def run(t, phase, *args):
        for h in range(2):
            rings[t, h][phase](*args)

    def raw_sum(s, i):
        at = pl.ds(pl.multiple_of(i * rows_q, rows_q), rows_q)
        product = mm(wd[at, quarter(s)], rows_grad[:, quarter(s)], NT)
        raw[at, :] = product if s == 0 else raw[at, :] + product

    for s in range(SIDE):
        for j in hops:
            from_peer(recv_b, b_send, b_recv, j, s).wait_recv()
            to_sibling(recv_b, fb_send, b_recv, j, s).start()
        for j in [0] + hops:
            from_sibling(recv_b, fb_send, b_recv, j, s).wait_recv()
        rows_grad[:, quarter(s)] = mm(place[...], recv_b[:, quarter(s)], NN).astype(BF16)
        loop(4, functools.partial(raw_sum, s))
        if s < SIDE - 1:
            down_grad(s)
        if s == 2:
            rings[0, 0][1]()

    def backward(i):
        at = pl.ds(i * rows_q, rows_q)
        value = raw[at, :]
        d_gate[at, :] = (value * gate_f[at, :]).astype(BF16)
        d_up[at, :] = (value * up_f[at, :]).astype(BF16)
        return jnp.sum(hidden[at, :].astype(F32) * value, axis=0, keepdims=True)

    inner = backward(0)
    for i in range(1, 4):
        inner = inner + backward(i)
    gate_copies, forwards = {}, {}
    for t, grad in ((1, d_gate), (2, d_up)):
        for h in range(2):
            for side, by in ((0, 1), (1, 3)):
                gate_copies[t, h, side] = line_copy(
                    grad.at[pl.ds(h * rows_h, rows_h)],
                    line_gate.at[t - 1, h, by - 1],
                    8 * t + 4 * h + side,
                    h,
                    by,
                )
                piece = pl.ds(side * rows_q, rows_q)
                forwards[t, h, side] = line_copy(
                    line_gate.at[t - 1, h, by - 1, piece],
                    line_gate.at[t - 1, h, 1, piece],
                    8 * t + 4 * h + 2 + side,
                    h,
                    by,
                )
    for c in gate_copies.values():
        c.start()
    left, right = inner[:, : cap // 2], inner[:, cap // 2 :]
    mine = jnp.where(core == 0, left, right)
    theirs = jnp.where(core == 0, right, left)
    inner_s[...] = jnp.broadcast_to(theirs, inner_s.shape)
    inner_copy = pltpu.make_async_remote_copy(
        src_ref=inner_s,
        dst_ref=inner_r,
        send_sem=s_send.at[0],
        recv_sem=s_recv.at[0],
        device_id=on_sib,
        device_id_type=MESH,
    )
    inner_copy.start()
    d_gate_t[...] = d_gate[...].astype(F32).T.astype(BF16)
    d_up_t[...] = d_up[...].astype(F32).T.astype(BF16)

    chunk = width // CHUNKS
    own_rows = pl.ds(pl.multiple_of(core * slots, slots), slots)
    their_rows = pl.ds(pl.multiple_of((1 - core) * slots, slots), slots)

    def columns(i):
        return pl.ds(i * chunk, chunk)

    sib_copies = [
        pltpu.make_async_remote_copy(
            src_ref=back.at[their_rows, columns(i)],
            dst_ref=sib.at[:, columns(i)],
            send_sem=s_send.at[1 + i],
            recv_sem=s_recv.at[1 + i],
            device_id=on_sib,
            device_id_type=MESH,
        )
        for i in range(CHUNKS)
    ]

    def to_owner(j, i):
        zz = peer(j)
        return pltpu.make_async_remote_copy(
            src_ref=send_c.at[block_of(zz), columns(i)],
            dst_ref=ret.at[block_of(z), columns(i)],
            send_sem=c_send.at[j * CHUNKS + i],
            recv_sem=c_recv.at[j * CHUNKS + i],
            device_id=on_z(zz),
            device_id_type=MESH,
        )

    def from_expert(j, i):
        zz = peer(nz - j)
        return pltpu.make_async_remote_copy(
            src_ref=ret.at[block_of(zz), columns(i)],
            dst_ref=ret.at[block_of(zz), columns(i)],
            send_sem=c_send.at[j * CHUNKS + i],
            recv_sem=c_recv.at[j * CHUNKS + i],
            device_id=on_z(peer(j)),
            device_id_type=MESH,
        )

    def input_grad(i):
        at = columns(i)
        total = mm(d_gate_t[...], wg[:, at], NN) + mm(d_up_t[...], wu[:, at], NN)
        back[:, at] = mm(place_t[...], total.astype(BF16), NN).astype(BF16)
        sib_copies[i].start()

    def send_home(i):
        at = columns(i)
        sib_copies[i].wait_recv()
        send_c[:, at] = (back[own_rows, at].astype(F32) + sib[:, at].astype(F32)).astype(BF16)
        for j in hops:
            to_owner(j, i).start()
        ret[block_of(z), at] = send_c[block_of(z), at]

    for i in range(CHUNKS):
        input_grad(i)
        if i:
            send_home(i - 1)
    down_grad(SIDE - 1)
    send_home(CHUNKS - 1)
    for key, c in gate_copies.items():
        c.wait_recv()
        forwards[key].start()
    rings[0, 1][1]()
    for c in row_copies:
        c.wait_recv()
    for t in (1, 2):
        for h in range(2):
            line_near(t, h)
    inner_copy.wait_recv()
    dcomb_ref[...] = mine + inner_r[0:1, :]
    for t in (1, 2):
        for h in range(2):
            for side in range(2):
                forwards[t, h, side].wait_recv()
            line_far(t, h)
            rings[t, h][6]()
    run(0, 2)
    run(1, 3)
    run(2, 3)
    run(0, 3)
    for j in hops:
        for i in range(CHUNKS):
            from_expert(j, i).wait_recv()

    def spread_back(i):
        at = pl.ds(pl.multiple_of(i * 512, 512), 512)
        table[:, at] = mm(pick_t[...], ret[:, at], NN)

    loop(width // 512, spread_back)

    def token_grad(i):
        at = pl.ds(pl.multiple_of(i * 16, 16), 16)
        norm = normed[at, :]
        d_norm = table[at, :] * scale1[at, :]
        centre = jnp.mean(d_norm, axis=1, keepdims=True)
        along = jnp.mean(d_norm * norm, axis=1, keepdims=True)
        dtok_ref[at, :] = (inverse[at, :] * (d_norm - centre - norm * along)).astype(BF16)

    loop(tok_dev // 16, token_grad)
    run(1, 4, dwg_ref)
    run(2, 4, dwu_ref)
    run(0, 4, dwd_ref)

    for j in hops:
        for s in range(SIDE):
            to_peer(send_b, recv_b, b_send, b_recv, j, s).wait_send()
        for i in range(CHUNKS):
            to_owner(j, i).wait_send()
    for j in [0] + hops:
        to_sibling(recv_a, fa_send, a_recv, j).wait_send()
        for s in range(SIDE):
            to_sibling(recv_b, fb_send, b_recv, j, s).wait_send()
    for c in [*row_copies, *gate_copies.values(), *forwards.values()]:
        c.wait_send()
    inner_copy.wait_send()
    for c in sib_copies:
        c.wait_send()
    for t in range(3):
        run(t, 5)


def copy_kernel(*refs):
    count = len(refs) // 2
    for i in range(count):
        refs[count + i][...] = refs[i][...]


def solution(mesh):
    nz = mesh.shape["exp"] // 2

    def on_device(
        tokens, cotangent, timestep, shift_table, scale_table, gate_table, chosen, combine, w_gate, w_up, w_down
    ):
        tok_dev, width = tokens.shape
        half = w_gate.shape[1]
        cap = chosen.shape[2]
        slots = nz * SLOT
        rows_h, rows_q = half // 2, half // 4
        vmem = pl.BlockSpec(memory_space=pltpu.VMEM)
        hbm = pl.BlockSpec(memory_space=pl.ANY)
        dma = pltpu.SemaphoreType.DMA
        outs = pl.pallas_call(
            functools.partial(layer_kernel, nz),
            out_shape=(
                jax.ShapeDtypeStruct((tok_dev, width), BF16),
                jax.ShapeDtypeStruct((1, cap // 2), F32),
                jax.ShapeDtypeStruct((half, 128), BF16),
                jax.ShapeDtypeStruct((half, 128), BF16),
                jax.ShapeDtypeStruct((half, 128), BF16),
            ),
            in_specs=[vmem] * 8 + [hbm] * 3,
            out_specs=(vmem,) * 5,
            scratch_shapes=[
                pltpu.VMEM((half, width), BF16),
                pltpu.VMEM((half, width), BF16),
                pltpu.VMEM((half, width), BF16),
                pltpu.VMEM((slots, width), BF16),
                pltpu.VMEM((slots, width), BF16),
                pltpu.VMEM((2 * slots, width), BF16),
                pltpu.VMEM((2 * slots, width), BF16),
                pltpu.VMEM((cap, width), BF16),
                pltpu.VMEM((cap, width), BF16),
                pltpu.VMEM((tok_dev, width), F32),
                pltpu.VMEM((tok_dev, width), F32),
                pltpu.VMEM((tok_dev, width), F32),
                pltpu.VMEM((tok_dev, 1), F32),
                pltpu.VMEM((slots, tok_dev), BF16),
                pltpu.VMEM((tok_dev, slots), BF16),
                pltpu.VMEM((cap, 2 * slots), BF16),
                pltpu.VMEM((2 * slots, cap), BF16),
                pltpu.VMEM((half, cap), BF16),
                pltpu.VMEM((half, cap), BF16),
                pltpu.VMEM((half, cap), F32),
                pltpu.VMEM((half, cap), F32),
                pltpu.VMEM((half, cap), F32),
                pltpu.VMEM((half, cap), BF16),
                pltpu.VMEM((half, cap), BF16),
                pltpu.VMEM((cap, half), BF16),
                pltpu.VMEM((cap, half), BF16),

                pltpu.VMEM((2 * slots, width), BF16),
                pltpu.VMEM((slots, width), BF16),
                pltpu.VMEM((slots, width), BF16),
                pltpu.VMEM((slots, width), BF16),
                pltpu.VMEM((8, cap // 2), F32),
                pltpu.VMEM((8, cap // 2), F32),
                pltpu.VMEM((SIDE, SIDE, cap, 128), BF16),
                pltpu.VMEM((2, SIDE - 1, SIDE, cap, 128), BF16),
                pltpu.VMEM((2, 2, SIDE - 1, rows_h, cap), BF16),
                pltpu.VMEM((2, 2, rows_h, width // SIDE), F32),
                pltpu.VMEM((2, SIDE * SIDE, rows_h, 128), BF16),
                pltpu.VMEM((6, SIDE, rows_h, 128), BF16),
                pltpu.VMEM((2, 2, 2, rows_h, 128), BF16),
                pltpu.VMEM((2, 2, SIDE, rows_h, 128), BF16),
                pltpu.VMEM((6, 2, rows_q, 128), BF16),
                pltpu.VMEM((6, 2, rows_h, 128), BF16),
                dma((3,)),
                dma((nz,)),
                dma((2 * nz,)),
                dma((nz * SIDE,)),
                dma((2 * nz * SIDE,)),
                dma((nz,)),
                dma((nz * SIDE,)),
                dma((nz * CHUNKS,)),
                dma((nz * CHUNKS,)),
                dma((1 + CHUNKS,)),
                dma((1 + CHUNKS,)),
                dma((72,)),
                dma((72,)),
                dma((24,)),
                dma((24,)),
            ],
            compiler_params=pltpu.CompilerParams(
                collective_id=0, has_side_effects=True, vmem_limit_bytes=60 * 1024 * 1024
            ),
        )(
            tokens,
            cotangent,
            timestep[None, :],
            shift_table,
            scale_table,
            gate_table,
            chosen[0],
            combine[0],
            w_gate[0],
            w_up[0],
            w_down[0],
        )
        outs = pl.pallas_call(
            copy_kernel,
            out_shape=tuple(jax.ShapeDtypeStruct(o.shape, o.dtype) for o in outs),
            in_specs=[vmem] * 5,
            out_specs=(vmem,) * 5,
        )(*outs)
        d_tokens, d_combine, d_gate, d_up, d_down = outs
        return d_tokens, d_combine[None], d_gate[None], d_up[None], d_down[None]

    in_specs = (
        P(("grp", "exp"), None),
        P(("grp", "exp"), None),
        P(("grp", "exp")),
        P(),
        P(),
        P(),
        P("grp", None, None),
        P("grp", None, None),
        P("exp", None, None),
        P("exp", None, None),
        P("exp", None, None),
    )
    out_specs = (
        P(("grp", "exp"), None),
        P("grp", "exp", None),
        P("exp", None, "grp"),
        P("exp", None, "grp"),
        P("exp", None, "grp"),
    )
    return jax.shard_map(
        on_device, mesh=mesh, in_specs=in_specs, out_specs=out_specs, check_vma=False
    )
```
